512 devices in a mesh: dp: 8 (over x, core), seq: 64 (over y, z).
Axes of the slice: x: 4, y: 4, z: 16, core: 2. Of those that a mesh axis runs over, the one named last changes fastest.
Arguments:
- inputs: bfloat16 [8, 128, 128, 1152], P('dp', 'seq'), may hold values from -6 to 6
- mid_inputs: bfloat16 [8, 128, 128, 1152], P('dp', 'seq'), may hold values from -6 to 6
- cotangent: bfloat16 [8, 128, 128, 1152], P('dp', 'seq'), may hold values from -6 to 6
- modulation: float32 [8, 6, 1152], P('dp'), may hold values from -4 to 4
- valid_frames: int32 [8], P('dp'), may hold values from 64 to 128, as said below
- qkv_spatial: bfloat16 [1152, 1728], P('dp', 'seq'), may hold values from -1 to 1
- out_spatial: bfloat16 [576, 1152], P('dp', 'seq'), may hold values from -0.25 to 0.25
- qkv_temporal: bfloat16 [1152, 1728], P('dp', 'seq'), may hold values from -1 to 1
- out_temporal: bfloat16 [576, 1152], P('dp', 'seq'), may hold values from -0.25 to 0.25
Outputs:
- input_grad: bfloat16 [8, 128, 128, 1152], P('dp', 'seq')
The draws below stay inside these ranges and needn't reach their ends.
Inputs may be any that keep to these rules, and one draw needn't show every extreme that they name: `valid_frames`: frames from a clip's count on are padding; one clip has all 128 frames valid and another exactly 64.
All inputs are finite; a program needn't handle non-finite values.
Results may differ from the reference program's by a relative error of at most 0.024.
The reference program's roundings to bfloat16 on the way (of `normin`, `qkv`, `gated`, `dout`, `probs_b`, `dscore`, `dqkv` and `dnorm`) count: a program that leaves them out, or rounds other values in their place, can miss the bound.
Values may be sent and summed in bfloat16 or wider, within the bound.
A program may use at most 64 MiB of HBM per device.

```python
import jax
import jax.numpy as jnp
from jax import lax

D = 1152
HDIM = 72
PATCH = 128
H = 576
FRAMES = 128
CLIPS = 8


def draw_valid_frames(key, part):
    key = jax.random.fold_in(key, 11)
    first, second = jax.random.split(key)
    counts = jax.random.randint(first, (CLIPS,), FRAMES // 2, FRAMES + 1)
    order = jax.random.permutation(second, CLIPS)
    counts = counts.at[order[0]].set(FRAMES)
    counts = counts.at[order[1]].set(FRAMES // 2)
    return counts.astype(jnp.int32)


def projection_draw(key):
    entries = jax.random.truncated_normal(key, -4.0, 4.0, (D, 3 * H), jnp.float32) * D ** (-0.5)
    queries = entries[:, :H]
    key_cols = entries[:, H:2 * H]
    values = entries[:, 2 * H:]
    leading = jnp.arange(H) < 2 * HDIM
    key_cols = jnp.where(leading[None, :], key_cols, key_cols)
    return jnp.clip(jnp.concatenate([queries, key_cols, values], 1), -1.0, 1.0)


def draw_qkv_spatial(key, part):
    key = jax.random.fold_in(key, 21)
    return projection_draw(key).astype(jnp.bfloat16)


def draw_qkv_temporal(key, part):
    key = jax.random.fold_in(key, 31)
    return projection_draw(key).astype(jnp.bfloat16)


def steps_of(stream_key, shape, cuts, low, high):
    gain = 1.0
    for axis_at, blocks in cuts:
        heights = jax.random.uniform(jax.random.fold_in(jax.random.fold_in(stream_key, 6), axis_at), (blocks,), jnp.float32, low / len(cuts), high / len(cuts))
        gain = gain * jnp.repeat(jnp.exp(heights), shape[axis_at] // blocks).reshape((-1,) + (1,) * (len(shape) - 1 - axis_at))
    return gain


def normal_values(stream_key, extent, deviation, limit, pieces=(), kind=jnp.bfloat16):
    values = deviation * jax.random.normal(stream_key, extent, jnp.float32)
    if pieces:
        values = values * steps_of(stream_key, extent, pieces, -0.22, 0.18)
    return jnp.clip(values, -limit, limit).astype(kind)


def setup_inputs(seed: int = 0) -> dict:
    splits = jax.random.split(jax.random.key(seed), 10)
    return {
        "inputs": normal_values(splits[0], (CLIPS, FRAMES, PATCH, D), 1.0, 6.0, ((0, 8), (1, 64))),
        "mid_inputs": normal_values(splits[1], (CLIPS, FRAMES, PATCH, D), 1.0, 6.0, ((0, 8), (1, 64))),
        "cotangent": normal_values(splits[2], (CLIPS, FRAMES, PATCH, D), 1.0, 6.0, ((0, 8), (1, 64))),
        "modulation": normal_values(splits[3], (CLIPS, 6, D), 1.0, 4.0, ((0, 8),), jnp.float32),
        "valid_frames": draw_valid_frames(jax.random.fold_in(splits[9], 71), 0),
        "qkv_spatial": draw_qkv_spatial(jax.random.fold_in(splits[9], 71), 0),
        "out_spatial": normal_values(splits[6], (H, D), H ** -0.5, 0.25, ((0, 8), (1, 64))),
        "qkv_temporal": draw_qkv_temporal(jax.random.fold_in(splits[9], 71), 0),
        "out_temporal": normal_values(splits[8], (H, D), H ** -0.5, 0.25, ((0, 8), (1, 64))),
    }


eps = 1e-06

def layer_norm(tokens):
    values = tokens.astype(jnp.float32)
    center = lax.optimization_barrier(jnp.mean(values, -1, keepdims=True))
    spread = lax.optimization_barrier(jnp.mean((values - center) ** 2, -1, keepdims=True))
    rstd = lax.rsqrt(spread + eps)
    return ((values - center) * rstd, rstd)

def attention_grad(qkv, dout, key_live):
    width = dout.shape[-1]
    heads = width // HDIM
    scale = HDIM ** (-0.5)
    lead = qkv.shape[:-1]
    query = qkv[..., :width].reshape(lead + (heads, HDIM)).astype(jnp.float32)
    key_part = qkv[..., width:2 * width].reshape(lead + (heads, HDIM)).astype(jnp.float32)
    value = qkv[..., 2 * width:].reshape(lead + (heads, HDIM)).astype(jnp.float32)
    upstream = dout.reshape(lead + (heads, HDIM)).astype(jnp.float32)
    scores = jnp.einsum('bqhd,bkhd->bhqk', query, key_part) * scale
    if key_live is not None:
        scores = jnp.where(key_live, scores, -1e+30)
    peak = lax.optimization_barrier(jnp.max(scores, -1, keepdims=True))
    probs = jnp.exp(scores - peak)
    probs = probs / lax.optimization_barrier(jnp.sum(probs, -1, keepdims=True))
    probs_b = probs.astype(jnp.bfloat16).astype(jnp.float32)
    dvalue = jnp.einsum('bhqk,bqhd->bkhd', probs_b, upstream)
    dprobs = jnp.einsum('bqhd,bkhd->bhqk', upstream, value)
    delta = lax.optimization_barrier(jnp.sum(probs * dprobs, -1, keepdims=True))
    dscore = (probs * (dprobs - delta)).astype(jnp.bfloat16).astype(jnp.float32)
    dquery = jnp.einsum('bhqk,bkhd->bqhd', dscore, key_part) * scale
    dkey = jnp.einsum('bhqk,bqhd->bkhd', dscore, query) * scale
    parts = [part.reshape(lead + (width,)) for part in (dquery, dkey, dvalue)]
    return jnp.concatenate(parts, -1).astype(jnp.bfloat16)

def block_grad(tokens, upstream, shift, scale, gate, qkv_weight, out_weight, key_live):
    normed, rstd = layer_norm(tokens)
    normin = (normed * (1.0 + scale) + shift).astype(jnp.bfloat16)
    qkv = jnp.dot(normin, qkv_weight, preferred_element_type=jnp.float32).astype(jnp.bfloat16)
    gated = (upstream * gate).astype(jnp.bfloat16)
    dout = jnp.dot(gated, out_weight.T, preferred_element_type=jnp.float32).astype(jnp.bfloat16)
    dqkv = attention_grad(qkv, dout, key_live)
    dnorm = jnp.dot(dqkv, qkv_weight.T, preferred_element_type=jnp.float32).astype(jnp.bfloat16)
    grad_n = dnorm.astype(jnp.float32) * (1.0 + scale)
    inner = grad_n - lax.optimization_barrier(jnp.mean(grad_n, -1, keepdims=True)) - normed * lax.optimization_barrier(jnp.mean(grad_n * normed, -1, keepdims=True))
    return upstream + rstd * inner

def reference(inputs, mid_inputs, cotangent, modulation, valid_frames, qkv_spatial, out_spatial, qkv_temporal, out_temporal):

    def per_clip(items):
        tokens, middle, upstream, shifts, frame_count = items
        live_frames = jnp.arange(FRAMES, dtype=jnp.int32) < frame_count
        masked = jnp.where(live_frames[:, None, None], upstream.astype(jnp.float32), 0.0)
        middle_t = jnp.swapaxes(middle, 0, 1)
        masked_t = jnp.swapaxes(masked, 0, 1)
        dmid_t = block_grad(middle_t, masked_t, shifts[3], shifts[4], shifts[5], qkv_temporal, out_temporal, live_frames)
        dmid = jnp.swapaxes(dmid_t, 0, 1)
        result = block_grad(tokens, dmid, shifts[0], shifts[1], shifts[2], qkv_spatial, out_spatial, None)
        return result.astype(jnp.bfloat16)
    return lax.map(per_clip, (inputs, mid_inputs, cotangent, modulation, valid_frames))
```

```python
import jax
import jax.numpy as jnp
from jax import lax
from jax.experimental import pallas as pl
from jax.experimental.pallas import tpu as pltpu
from jax.sharding import PartitionSpec as P

HDIM = 72
HEADS = 8
D = 1152
EPS = 1e-06
TOK = 256
NY, NX, NZ = 4, 4, 16
NSEQ = NY * NZ
QW = 512
OW = 384
HP = 80
f32, bf16 = jnp.float32, jnp.bfloat16

NN = (((1,), (0,)), ((), ()))
NT = (((1,), (1,)), ((), ()))
TN = (((0,), (0,)), ((), ()))


def dot(a, b, dims=NN):
    return lax.dot_general(a, b, dims, preferred_element_type=f32)


def iota(shape, axis):
    return lax.broadcasted_iota(jnp.int32, shape, axis)


def head_at(n):
    return (n // 6) * QW + (n % 6) * HDIM


def norm_stats(x):
    center = jnp.mean(x, -1, keepdims=True)
    diff = x - center
    spread = jnp.mean(diff * diff, -1, keepdims=True)
    rstd = lax.rsqrt(spread + EPS)
    return diff * rstd, rstd


def norm_back(dnorm, normed, rstd, gain):
    g = dnorm * gain
    return rstd * (
        g
        - jnp.mean(g, -1, keepdims=True)
        - normed * jnp.mean(g * normed, -1, keepdims=True)
    )


def kernel(
    inp, mid, cot, mod, frames, qkv_s, out_s, qkv_t, out_t, result,
    zbuf, eq, eo, q_t, o_t, q_s, o_s,
    msend, mrecv, dsend, drecv, rsend, rrecv,
    pm, pr, normin, qkv, dqkv, dout, probs, acc, nm_t, rs_t, nm_s, rs_s, dmid,
    zsend_sem, zrecv_sem, jsend_sem, jrecv_sem, asend_sem, arecv_sem,
):
    dp = lax.axis_index("dp")
    s = lax.axis_index("seq")
    x, c = dp // 2, dp % 2
    y, z = s // NZ, s % NZ
    other = 1 - c
    pending = []

    def seq_dev(yy, zz):
        return {"seq": yy * NZ + zz}

    def x_dev(xx):
        return {"dp": xx * 2 + c}

    def peer(j):
        t = j // 4
        dz = jnp.where(t % 2 == 1, (t + 1) // 2, NZ - t // 2)
        return ((y + j % 4) % NY) * NZ + (z + dz) % NZ

    barrier = pltpu.get_barrier_semaphore()

    def greet(j, carry):
        pl.semaphore_signal(barrier, inc=1, device_id={"seq": peer(j)})
        return carry

    for xx in ((x + 1) % NX, (x + 3) % NX):
        pl.semaphore_signal(barrier, inc=1, device_id=x_dev(xx))
    pl.semaphore_signal(barrier, inc=1, device_id={"dp": x * 2 + other})
    lax.fori_loop(1, NSEQ, greet, 0)

    def pack(qkv_ref, out_ref):
        q, o = qkv_ref[...], out_ref[...]

        def place(rows, g):
            hit = iota((rows, 128), 1) == iota((rows, 128), 0) + 32 * g
            return jnp.where(hit, 1.0, 0.0).astype(bf16)

        q0 = dot(q, place(27, 0), TN)[0:64]
        q1 = dot(q, place(27, 1), TN)[64:128]
        q2 = dot(q, place(27, 2), TN)[128:144]
        o2 = dot(o, place(18, 2))[0:48]
        o3 = dot(o, place(18, 3))[48:72]
        full = q0 + q1 + jnp.concatenate([q2, o2], 0)
        full = full + jnp.concatenate([o3, jnp.zeros((40, 128), f32)], 0)
        return full.astype(bf16)

    zbuf[z, 0:64] = pack(qkv_t, out_t)
    zbuf[z, 64:128] = pack(qkv_s, out_s)

    ri, ci = iota((TOK, TOK), 0), iota((TOK, TOK), 1)
    pm[...] = jnp.where(ci == (ri & 1) * 128 + (ri >> 2) * 2 + ((ri >> 1) & 1), 1.0, 0.0).astype(bf16)
    pr[...] = jnp.where(
        ci == ((ri & 127) >> 1) * 4 + (ri >> 7) * 2 + (ri & 1), 1.0, 0.0
    ).astype(bf16)

    msend[...] = dot(pm[...], mid[...].reshape(TOK, D)).astype(bf16).reshape(NSEQ, 4, D)

    pl.semaphore_wait(barrier, NSEQ - 1 + 3)

    def zcopy(block, way, step):
        to = (z + 1) % NZ if way == 0 else (z + NZ - 1) % NZ
        return pltpu.make_async_remote_copy(
            src_ref=zbuf.at[block], dst_ref=zbuf.at[block],
            send_sem=zsend_sem.at[way, step], recv_sem=zrecv_sem.at[way, step],
            device_id=seq_dev(y, to),
        )

    def scatter(src, dst, k, lo, hi):
        def one(j, carry):
            to = peer(j)
            pltpu.make_async_remote_copy(
                src_ref=src.at[to], dst_ref=dst.at[s],
                send_sem=asend_sem.at[k], recv_sem=arecv_sem.at[k],
                device_id={"seq": to},
            ).start()
            return carry
        lax.fori_loop(lo, hi, one, 0)

    def wait_scatter(ref, sem, k):
        part = ref.at[pl.ds(0, NSEQ - 1)]
        pltpu.make_async_copy(part, part, sem.at[k]).wait()

    for step in range(8):
        if step > 0:
            zcopy((z + NZ - step) % NZ, 0, step - 1).wait_recv()
        cp = zcopy((z + NZ - step) % NZ, 0, step)
        cp.start()
        pending.append(cp)
        if step > 0:
            zcopy((z + step) % NZ, 1, step - 1).wait_recv()
        if step < 7:
            cp = zcopy((z + step) % NZ, 1, step)
            cp.start()
            pending.append(cp)
            scatter(msend, mrecv, 0, 1 + 9 * step, 10 + 9 * step)
        if step == 0:
            def fill(zz, carry):
                lane = iota((224, QW), 0) - 96
                live = (lane >= 0) & (lane < 27)
                hit = live & (iota((224, QW), 1) == lane + 27 * zz)
                eq[zz] = jnp.where(hit, 1.0, 0.0).astype(bf16)
                lane = iota((224, OW), 0) - 96
                live = (lane >= 0) & (lane < 18)
                hit = live & (iota((224, OW), 1) == lane + 18 * zz + 32 * y)
                eo[zz] = jnp.where(hit, 1.0, 0.0).astype(bf16)
                return carry
            lax.fori_loop(0, NZ, fill, 0)
    zcopy((z + NZ - 8) % NZ, 0, 7).wait_recv()

    def unpack(at, q_ref, o_ref):
        whole = jnp.concatenate([zbuf[i, at:at + 64] for i in range(NZ)], 1)

        def pick(table, g):
            lo = 96 - 32 * g
            return dot(whole, table[:, lo:lo + 128, :].reshape(NZ * 128, -1)).astype(bf16)

        o_ref[y, c, x] = jnp.concatenate([pick(eo, 2)[16:64], pick(eo, 3)[0:32]], 0)
        q_ref[y, c, x] = jnp.concatenate([pick(eq, 0), pick(eq, 1), pick(eq, 2)[0:16]], 0)

    jobs_t = [
        (0, o_t, "y", 0, 48, 32), (1, o_t, "x", 48, 32, 16),
        (2, q_t, "y", 0, 80, 48), (3, q_t, "x", 80, 64, 32),
    ]
    jobs_s = [
        (4, o_s, "y", 0, 48, 32), (5, o_s, "x", 48, 32, 16),
        (6, q_s, "y", 0, 80, 48), (7, q_s, "x", 80, 64, 32),
    ]

    def view(job, phase, rel, half, core):
        _, ref, first, r, n, m = job
        lo, size = {"all": (r, n), "a": (r, m), "b": (r + m, n - m)}[half]
        rows = pl.ds(lo, size)
        axis = first if phase == 0 else ("x" if first == "y" else "y")
        if axis == "x":
            return ref.at[y if phase == 0 else slice(None), core, (x + rel) % NX, rows]
        return ref.at[(y + rel) % NY, core, x if phase == 0 else slice(None), rows]

    def hop(job, phase, rel, half, way, slot):
        first = job[2]
        axis = first if phase == 0 else ("x" if first == "y" else "y")
        step = 1 if way == 0 else 3
        dev = x_dev((x + step) % NX) if axis == "x" else seq_dev((y + step) % NY, z)
        ref = view(job, phase, rel, half, c)
        return pltpu.make_async_remote_copy(
            src_ref=ref, dst_ref=ref,
            send_sem=jsend_sem.at[job[0], phase * 4 + slot],
            recv_sem=jrecv_sem.at[job[0], phase * 4 + slot],
            device_id=dev,
        )

    def go(cp):
        cp.start()
        pending.append(cp)

    def first_step(job, phase):
        go(hop(job, phase, 0, "all", 0, 0))
        go(hop(job, phase, 0, "all", 1, 1))

    def pass_on(job, phase):
        hop(job, phase, 3, "all", 0, 0).wait_recv()
        go(hop(job, phase, 3, "a", 0, 2))
        hop(job, phase, 1, "all", 1, 1).wait_recv()
        go(hop(job, phase, 1, "b", 1, 3))

    def last_step(job, phase):
        hop(job, phase, 2, "a", 0, 2).wait_recv()
        hop(job, phase, 2, "b", 1, 3).wait_recv()

    def share(job, rel, core):
        ref = view(job, 1, rel, "all", core)
        return pltpu.make_async_remote_copy(
            src_ref=ref, dst_ref=ref,
            send_sem=jsend_sem.at[job[0], 8 + rel], recv_sem=jrecv_sem.at[job[0], 8 + rel],
            device_id={"dp": x * 2 + other},
        )

    def share_wait(job):
        for rel in range(4):
            share(job, rel, other).wait_recv()

    unpack(0, q_t, o_t)
    for job in jobs_t:
        first_step(job, 0)
    unpack(64, q_s, o_s)
    for job in jobs_t:
        pass_on(job, 0)
    for job in jobs_t:
        last_step(job, 0)
        first_step(job, 1)
        go(share(job, 0, c))
    for job in jobs_s:
        first_step(job, 0)
    for job in jobs_t:
        pass_on(job, 1)
        go(share(job, 3, c))
        go(share(job, 1, c))
    for job in jobs_s:
        pass_on(job, 0)
    for job in jobs_t:
        last_step(job, 1)
        go(share(job, 2, c))
    for job in jobs_s:
        last_step(job, 0)
        first_step(job, 1)
        go(share(job, 0, c))

    def live_cot(f):
        cell = iota((128, 1), 0) * 0 + (2 * s + f)
        return jnp.where(cell < frames[0], cot[f].astype(f32), 0.0)

    def out_rows(o_ref, yy):
        return jnp.concatenate([o_ref[yy, d % 2, d // 2] for d in range(HEADS)], 0)

    def qkv_rows(q_ref, yy):
        return jnp.concatenate([q_ref[yy, d % 2, d // 2] for d in range(8)], 0)

    def out_back(gated, o_ref):
        total = None
        for yy in range(NY):
            term = dot(gated[:, 256 * yy:256 * yy + OW], out_rows(o_ref, yy), NT)
            total = term if total is None else total + term
        return total.astype(bf16)

    for job in jobs_t[:2]:
        share_wait(job)
    for f in range(2):
        normin[f * 128:(f + 1) * 128, :] = (live_cot(f) * mod[5:6, :]).astype(bf16)
    dout[...] = out_back(normin, o_t)
    dsend[...] = dot(pm[...], dout[...]).astype(bf16).reshape(NSEQ, 4, HEADS * HP)
    scatter(dsend, drecv, 1, 1, NSEQ)
    mrecv[s] = msend[s]
    drecv[s] = dsend[s]

    def project(q_ref):
        def body(yy, carry):
            lanes = pl.ds(pl.multiple_of(yy * QW, QW), QW)
            qkv[:, lanes] = dot(normin[...], qkv_rows(q_ref, yy)).astype(bf16)
            return carry
        lax.fori_loop(0, NY, body, 0)

    def project_back(q_ref):
        acc[...] = jnp.zeros((TOK, D), f32)

        def body(yy, carry):
            lanes = pl.ds(pl.multiple_of(yy * QW, QW), QW)
            acc[...] += dot(dqkv[:, lanes], qkv_rows(q_ref, yy), NT)
            return carry
        lax.fori_loop(0, NY, body, 0)

    def attend(masked):
        def body(b, carry):
            rows = pl.ds(pl.multiple_of(b * 128, 128), 128)
            for h in range(HEADS):
                q = qkv[rows, head_at(h):head_at(h) + HDIM]
                k = qkv[rows, head_at(8 + h):head_at(8 + h) + HDIM]
                scores = dot(q, k, NT) * HDIM ** -0.5
                if masked:
                    scores = jnp.where(iota((128, 128), 1) < frames[0], scores, -1e30)
                e = jnp.exp(scores - jnp.max(scores, -1, keepdims=True))
                probs[b * HEADS + h] = e / jnp.sum(e, -1, keepdims=True)
            return carry
        lax.fori_loop(0, 2, body, 0)

    def attend_back():
        def body(b, carry):
            rows = pl.ds(pl.multiple_of(b * 128, 128), 128)
            for h in range(HEADS):
                q = qkv[rows, head_at(h):head_at(h) + HDIM]
                k = qkv[rows, head_at(8 + h):head_at(8 + h) + HDIM]
                v = qkv[rows, head_at(16 + h):head_at(16 + h) + HDIM]
                up = dout[rows, HP * h:HP * h + HDIM]
                p = probs[b * HEADS + h]
                dv = dot(p.astype(bf16), up, TN)
                dp_ = dot(up, v, NT)
                delta = jnp.sum(p * dp_, -1, keepdims=True)
                ds = (p * (dp_ - delta)).astype(bf16)
                dq = dot(ds, k) * HDIM ** -0.5
                dk = dot(ds, q, TN) * HDIM ** -0.5
                dqkv[rows, head_at(h):head_at(h) + HDIM] = dq.astype(bf16)
                dqkv[rows, head_at(8 + h):head_at(8 + h) + HDIM] = dk.astype(bf16)
                dqkv[rows, head_at(16 + h):head_at(16 + h) + HDIM] = dv.astype(bf16)
            return carry
        lax.fori_loop(0, 2, body, 0)

    dqkv[...] = jnp.zeros((TOK, NY * QW), bf16)

    def own_norms(i, carry):
        rows = pl.ds(pl.multiple_of(i * 64, 64), 64)
        f, r = i // 2, pl.ds(pl.multiple_of((i % 2) * 64, 64), 64)
        nm_t[rows, :], rs_t[rows, :] = norm_stats(mid[f, r, :].astype(f32))
        nm_s[rows, :], rs_s[rows, :] = norm_stats(inp[f, r, :].astype(f32))
        return carry
    lax.fori_loop(0, 4, own_norms, 0)

    wait_scatter(mrecv, arecv_sem, 0)
    acc[...] = dot(pr[...], mrecv[...].reshape(TOK, D))

    def patch_norm(i, carry):
        rows = pl.ds(pl.multiple_of(i * 64, 64), 64)
        normed, _ = norm_stats(acc[rows, :])
        normin[rows, :] = (normed * (1.0 + mod[4:5, :]) + mod[3:4, :]).astype(bf16)
        return carry
    lax.fori_loop(0, 4, patch_norm, 0)
    for job in jobs_t[2:]:
        share_wait(job)
    project(q_t)
    attend(True)
    for job in jobs_s:
        pass_on(job, 1)
        go(share(job, 3, c))
        go(share(job, 1, c))
    wait_scatter(drecv, arecv_sem, 1)
    dout[...] = dot(pr[...], drecv[...].reshape(TOK, HEADS * HP)).astype(bf16)
    attend_back()
    project_back(q_t)
    rsend[...] = dot(pr[...], acc[...].astype(bf16), TN).astype(bf16).reshape(NSEQ, 4, D)
    scatter(rsend, rrecv, 2, 1, NSEQ)
    rrecv[s] = rsend[s]

    for job in jobs_s:
        last_step(job, 1)
        go(share(job, 2, c))

    def frame_norm(i, carry):
        rows = pl.ds(pl.multiple_of(i * 64, 64), 64)
        normin[rows, :] = (nm_s[rows, :] * (1.0 + mod[1:2, :]) + mod[0:1, :]).astype(bf16)
        return carry
    lax.fori_loop(0, 4, frame_norm, 0)
    for job in jobs_s:
        share_wait(job)
    project(q_s)
    attend(False)

    wait_scatter(rrecv, arecv_sem, 2)
    acc[...] = dot(pm[...], rrecv[...].reshape(TOK, D), TN)

    def mid_grad(i, carry):
        rows = pl.ds(pl.multiple_of(i * 64, 64), 64)
        f, r = i // 2, pl.ds(pl.multiple_of((i % 2) * 64, 64), 64)
        cell = iota((64, 1), 0) * 0 + (2 * s + f)
        masked = jnp.where(cell < frames[0], cot[f, r, :].astype(f32), 0.0)
        grad = masked + norm_back(acc[rows, :], nm_t[rows, :], rs_t[rows, :], 1.0 + mod[4:5, :])
        dmid[rows, :] = grad
        normin[rows, :] = (grad * mod[2:3, :]).astype(bf16)
        return carry
    lax.fori_loop(0, 4, mid_grad, 0)
    dout[...] = out_back(normin, o_s)
    attend_back()
    project_back(q_s)

    def last_grad(i, carry):
        rows = pl.ds(pl.multiple_of(i * 64, 64), 64)
        f, r = i // 2, pl.ds(pl.multiple_of((i % 2) * 64, 64), 64)
        dnorm = acc[rows, :].astype(bf16).astype(f32)
        grad = norm_back(dnorm, nm_s[rows, :], rs_s[rows, :], 1.0 + mod[1:2, :])
        result[f, r, :] = (dmid[rows, :] + grad).astype(bf16)
        return carry
    lax.fori_loop(0, 4, last_grad, 0)

    for cp in pending:
        cp.wait_send()
    wait_scatter(msend, asend_sem, 0)
    wait_scatter(dsend, asend_sem, 1)
    wait_scatter(rsend, asend_sem, 2)


def per_device(inputs, mid_inputs, cotangent, modulation, frames, qkv_s, out_s, qkv_t, out_t):
    vmem = pl.BlockSpec(memory_space=pltpu.VMEM)
    dma = pltpu.SemaphoreType.DMA
    out = pl.pallas_call(
        kernel,
        out_shape=jax.ShapeDtypeStruct((2, 128, D), bf16),
        in_specs=[vmem] * 4 + [pl.BlockSpec(memory_space=pltpu.SMEM)] + [vmem] * 4,
        out_specs=vmem,
        scratch_shapes=[
            pltpu.VMEM((NZ, 128, 128), bf16),
            pltpu.VMEM((NZ, 224, QW), bf16),
            pltpu.VMEM((NZ, 224, OW), bf16),
            pltpu.VMEM((NY, 2, NX, 144, QW), bf16),
            pltpu.VMEM((NY, 2, NX, HP, OW), bf16),
            pltpu.VMEM((NY, 2, NX, 144, QW), bf16),
            pltpu.VMEM((NY, 2, NX, HP, OW), bf16),
            pltpu.VMEM((NSEQ, 4, D), bf16),
            pltpu.VMEM((NSEQ, 4, D), bf16),
            pltpu.VMEM((NSEQ, 4, HEADS * HP), bf16),
            pltpu.VMEM((NSEQ, 4, HEADS * HP), bf16),
            pltpu.VMEM((NSEQ, 4, D), bf16),
            pltpu.VMEM((NSEQ, 4, D), bf16),
            pltpu.VMEM((TOK, TOK), bf16),
            pltpu.VMEM((TOK, TOK), bf16),
            pltpu.VMEM((TOK, D), bf16),
            pltpu.VMEM((TOK, NY * QW), bf16),
            pltpu.VMEM((TOK, NY * QW), bf16),
            pltpu.VMEM((TOK, HEADS * HP), bf16),
            pltpu.VMEM((2 * HEADS, 128, 128), f32),
            pltpu.VMEM((TOK, D), f32),
            pltpu.VMEM((TOK, D), f32),
            pltpu.VMEM((TOK, 1), f32),
            pltpu.VMEM((TOK, D), f32),
            pltpu.VMEM((TOK, 1), f32),
            pltpu.VMEM((TOK, D), f32),
            dma((2, 8)), dma((2, 8)), dma((8, 12)), dma((8, 12)), dma((3,)), dma((3,)),
        ],
        compiler_params=pltpu.CompilerParams(
            collective_id=0, has_side_effects=True, vmem_limit_bytes=56 * 1024 * 1024
        ),
        name="blocks_grad",
    )(
        inputs[0], mid_inputs[0], cotangent[0], modulation[0], frames,
        qkv_s.T, out_s, qkv_t.T, out_t,
    )
    return out[None]


def solution(mesh):
    big = P("dp", "seq", None, None)
    weight = P("dp", "seq")
    return jax.shard_map(
        per_device,
        mesh=mesh,
        in_specs=(big, big, big, P("dp", None, None), P("dp")) + (weight,) * 4,
        out_specs=big,
        check_vma=False,
    )
```

```python
import jax
import jax.numpy as jnp
from jax import lax
from jax.experimental import pallas as pl
from jax.experimental.pallas import tpu as pltpu
from jax.sharding import PartitionSpec as P

HDIM = 72
HEADS = 8
D = 1152
EPS = 1e-06
TOK = 256
NY, NX, NZ = 4, 4, 16
NSEQ = NY * NZ
QW = 512
OW = 384
HP = 80
f32, bf16 = jnp.float32, jnp.bfloat16

NN = (((1,), (0,)), ((), ()))
NT = (((1,), (1,)), ((), ()))
TN = (((0,), (0,)), ((), ()))


def dot(a, b, dims=NN):
    return lax.dot_general(a, b, dims, preferred_element_type=f32)


def iota(shape, axis):
    return lax.broadcasted_iota(jnp.int32, shape, axis)


def head_at(n):
    return (n // 6) * QW + (n % 6) * HDIM


def norm_stats(x):
    center = jnp.mean(x, -1, keepdims=True)
    diff = x - center
    spread = jnp.mean(diff * diff, -1, keepdims=True)
    rstd = lax.rsqrt(spread + EPS)
    return diff * rstd, rstd


def norm_back(dnorm, normed, rstd, gain):
    g = dnorm * gain
    return rstd * (
        g
        - jnp.mean(g, -1, keepdims=True)
        - normed * jnp.mean(g * normed, -1, keepdims=True)
    )


def kernel(
    inp, mid, cot, mod, frames, qkv_s, out_s, qkv_t, out_t, result,
    zbuf, eq, eo, q_t, o_t, q_s, o_s,
    msend, mrecv, dsend, drecv, rsend, rrecv,
    pm, pr, back, normin, qkv, dqkv, dout, probs, acc, nm_t, rs_t, nm_s, rs_s, dmid,
    zsend_sem, zrecv_sem, jsend_sem, jrecv_sem, asend_sem, arecv_sem,
):
    dp = lax.axis_index("dp")
    s = lax.axis_index("seq")
    x, c = dp // 2, dp % 2
    y, z = s // NZ, s % NZ
    other = 1 - c
    pending = []

    def seq_dev(yy, zz):
        return {"seq": yy * NZ + zz}

    def x_dev(xx):
        return {"dp": xx * 2 + c}

    def peer(j):
        near = 7 - (j - 4) // 8
        dz = jnp.where(j < 4, 8, jnp.where(j >= 60, 0, jnp.where(j % 2 == 0, near, NZ - near)))
        dy = jnp.where((j < 4) | (j >= 60), j % 4, ((j - 4) % 8) // 2)
        return ((y + dy) % NY) * NZ + (z + dz) % NZ

    barrier = pltpu.get_barrier_semaphore()

    def greet(j, carry):
        pl.semaphore_signal(barrier, inc=1, device_id={"seq": peer(j)})
        return carry

    for xx in ((x + 1) % NX, (x + 3) % NX):
        pl.semaphore_signal(barrier, inc=1, device_id=x_dev(xx))
    pl.semaphore_signal(barrier, inc=1, device_id={"dp": x * 2 + other})
    lax.fori_loop(0, NSEQ - 4, greet, 0)
    lax.fori_loop(NSEQ - 3, NSEQ, greet, 0)

    def pack(qkv_ref, out_ref):
        q, o = qkv_ref[...], out_ref[...]

        def place(rows, g):
            hit = iota((rows, 128), 1) == iota((rows, 128), 0) + 32 * g
            return jnp.where(hit, 1.0, 0.0).astype(bf16)

        q0 = dot(q, place(27, 0), TN)[0:64]
        q1 = dot(q, place(27, 1), TN)[64:128]
        q2 = dot(q, place(27, 2), TN)[128:144]
        o2 = dot(o, place(18, 2), TN)[0:48]
        o3 = dot(o, place(18, 3), TN)[48:72]
        full = q0 + q1 + jnp.concatenate([q2, o2], 0)
        full = full + jnp.concatenate([o3, jnp.zeros((40, 128), f32)], 0)
        return full.astype(bf16)

    zbuf[z, 0:64] = pack(qkv_t, out_t)
    zbuf[z, 64:128] = pack(qkv_s, out_s)

    ri, ci = iota((TOK, TOK), 0), iota((TOK, TOK), 1)
    pm[...] = jnp.where(ci == (ri & 1) * 128 + (ri >> 2) * 2 + ((ri >> 1) & 1), 1.0, 0.0).astype(bf16)
    pr[...] = jnp.where(
        ci == ((ri & 127) >> 1) * 4 + (ri >> 7) * 2 + (ri & 1), 1.0, 0.0
    ).astype(bf16)

    back[...] = jnp.where(
        ci == (ri & 1) * 128 + ((ri & 127) >> 1) * 2 + (ri >> 7), 1.0, 0.0
    ).astype(bf16)
    msend[...] = dot(pm[...], mid[...].reshape(TOK, D)).astype(bf16).reshape(NSEQ, 4, D)

    pl.semaphore_wait(barrier, NSEQ - 1 + 3)

    def zcopy(block, way, step):
        to = (z + 1) % NZ if way == 0 else (z + NZ - 1) % NZ
        return pltpu.make_async_remote_copy(
            src_ref=zbuf.at[block], dst_ref=zbuf.at[block],
            send_sem=zsend_sem.at[way, step], recv_sem=zrecv_sem.at[way, step],
            device_id=seq_dev(y, to),
        )

    def scatter(src, dst, k, lo, hi):
        def one(j, carry):
            to = peer(j)
            pltpu.make_async_remote_copy(
                src_ref=src.at[to], dst_ref=dst.at[s],
                send_sem=asend_sem.at[k], recv_sem=arecv_sem.at[k],
                device_id={"seq": to},
            ).start()
            return carry
        lax.fori_loop(lo, hi, one, 0)

    def wait_scatter(ref, sem, k):
        part = ref.at[pl.ds(0, NSEQ - 1)]
        pltpu.make_async_copy(part, part, sem.at[k]).wait()

    def fill(zz, carry):
        lane = iota((224, QW), 0) - 96
        live = (lane >= 0) & (lane < 27)
        hit = live & (iota((224, QW), 1) == lane + 27 * zz)
        eq[zz] = jnp.where(hit, 1.0, 0.0).astype(bf16)
        lane = iota((224, OW), 0) - 96
        live = (lane >= 0) & (lane < 18)
        hit = live & (iota((224, OW), 1) == lane + 18 * zz + 32 * y)
        eo[zz] = jnp.where(hit, 1.0, 0.0).astype(bf16)
        return carry

    for step in range(8):
        if step > 0:
            zcopy((z + NZ - step) % NZ, 0, step - 1).wait_recv()
        cp = zcopy((z + NZ - step) % NZ, 0, step)
        cp.start()
        pending.append(cp)
        if step > 0:
            zcopy((z + step) % NZ, 1, step - 1).wait_recv()
        if step < 7:
            cp = zcopy((z + step) % NZ, 1, step)
            cp.start()
            pending.append(cp)
        scatter(msend, mrecv, 0, 3 * step, 3 * step + 3)
        lax.fori_loop(2 * step, 2 * step + 2, fill, 0)
    zcopy((z + NZ - 8) % NZ, 0, 7).wait_recv()

    def unpack(at, q_ref, o_ref):
        whole = jnp.concatenate([zbuf[i, at:at + 64] for i in range(NZ)], 1)

        def pick(table, g):
            lo = 96 - 32 * g
            return dot(whole, table[:, lo:lo + 128, :].reshape(NZ * 128, -1)).astype(bf16)

        o_ref[y, c, x] = jnp.concatenate([pick(eo, 2)[16:64], pick(eo, 3)[0:32]], 0)
        q_ref[y, c, x] = jnp.concatenate([pick(eq, 0), pick(eq, 1), pick(eq, 2)[0:16]], 0)

    jobs_t = [
        (0, o_t, "y", 0, 48, 32), (1, o_t, "x", 48, 32, 16),
        (2, q_t, "y", 0, 80, 48), (3, q_t, "x", 80, 64, 32),
    ]
    jobs_s = [
        (4, o_s, "y", 0, 48, 32), (5, o_s, "x", 48, 32, 16),
        (6, q_s, "y", 0, 80, 48), (7, q_s, "x", 80, 64, 32),
    ]

    def view(job, phase, rel, half, core):
        _, ref, first, r, n, m = job
        lo, size = {"all": (r, n), "a": (r, m), "b": (r + m, n - m)}[half]
        rows = pl.ds(lo, size)
        axis = first if phase == 0 else ("x" if first == "y" else "y")
        if axis == "x":
            return ref.at[y if phase == 0 else slice(None), core, (x + rel) % NX, rows]
        return ref.at[(y + rel) % NY, core, x if phase == 0 else slice(None), rows]

    def hop(job, phase, rel, half, way, slot):
        first = job[2]
        axis = first if phase == 0 else ("x" if first == "y" else "y")
        step = 1 if way == 0 else 3
        dev = x_dev((x + step) % NX) if axis == "x" else seq_dev((y + step) % NY, z)
        ref = view(job, phase, rel, half, c)
        return pltpu.make_async_remote_copy(
            src_ref=ref, dst_ref=ref,
            send_sem=jsend_sem.at[job[0], phase * 4 + slot],
            recv_sem=jrecv_sem.at[job[0], phase * 4 + slot],
            device_id=dev,
        )

    def go(cp):
        cp.start()
        pending.append(cp)

    def first_step(job, phase):
        go(hop(job, phase, 0, "all", 0, 0))
        go(hop(job, phase, 0, "all", 1, 1))

    def pass_on(job, phase):
        hop(job, phase, 3, "all", 0, 0).wait_recv()
        go(hop(job, phase, 3, "a", 0, 2))
        hop(job, phase, 1, "all", 1, 1).wait_recv()
        go(hop(job, phase, 1, "b", 1, 3))

    def last_step(job, phase):
        hop(job, phase, 2, "a", 0, 2).wait_recv()
        hop(job, phase, 2, "b", 1, 3).wait_recv()

    def share(job, rel, core):
        ref = view(job, 1, rel, "all", core)
        return pltpu.make_async_remote_copy(
            src_ref=ref, dst_ref=ref,
            send_sem=jsend_sem.at[job[0], 8 + rel], recv_sem=jrecv_sem.at[job[0], 8 + rel],
            device_id={"dp": x * 2 + other},
        )

    def share_wait(job):
        for rel in range(4):
            share(job, rel, other).wait_recv()

    def live_cot(f):
        cell = iota((128, 1), 0) * 0 + (2 * s + f)
        return jnp.where(cell < frames[0], cot[f].astype(f32), 0.0)

    def out_rows(o_ref, yy):
        return jnp.concatenate([o_ref[yy, d % 2, d // 2] for d in range(HEADS)], 0)

    def qkv_rows(q_ref, yy):
        return jnp.concatenate([q_ref[yy, d % 2, d // 2] for d in range(8)], 0)

    def out_back(gated, o_ref):
        total = None
        for yy in range(NY):
            term = dot(gated[:, 256 * yy:256 * yy + OW], out_rows(o_ref, yy), NT)
            total = term if total is None else total + term
        return total.astype(bf16)

    def open_second(job):
        last_step(job, 0)
        first_step(job, 1)
        go(share(job, 0, c))

    def on_second(job):
        pass_on(job, 1)
        go(share(job, 3, c))
        go(share(job, 1, c))

    def end_second(job):
        last_step(job, 1)
        go(share(job, 2, c))

    def each(f, jobs, *args):
        for job in jobs:
            f(job, *args)

    jobs_o, jobs_q = jobs_t[:2], jobs_t[2:]
    unpack(0, q_t, o_t)
    each(first_step, jobs_t, 0)
    scatter(msend, mrecv, 0, 24, 37)
    unpack(64, q_s, o_s)
    each(pass_on, jobs_o, 0)
    each(open_second, jobs_o)
    each(pass_on, jobs_q, 0)
    scatter(msend, mrecv, 0, 37, 50)
    each(on_second, jobs_o)
    each(open_second, jobs_q)
    scatter(msend, mrecv, 0, 50, 60)
    scatter(msend, mrecv, 0, 61, 64)
    each(end_second, jobs_o)
    each(first_step, jobs_s, 0)

    each(share_wait, jobs_o)
    for f in range(2):
        normin[f * 128:(f + 1) * 128, :] = (live_cot(f) * mod[5]).astype(bf16)
    dout[...] = out_back(normin, o_t)
    dsend[...] = dot(pm[...], dout[...]).astype(bf16).reshape(NSEQ, 4, HEADS * HP)
    scatter(dsend, drecv, 1, 0, 60)
    scatter(dsend, drecv, 1, 61, 64)
    mrecv[s] = msend[s]
    drecv[s] = dsend[s]
    each(on_second, jobs_q)
    each(pass_on, jobs_s, 0)
    each(end_second, jobs_q)
    each(open_second, jobs_s)

    def project(q_ref):
        def body(yy, carry):
            lanes = pl.ds(pl.multiple_of(yy * QW, QW), QW)
            qkv[:, lanes] = dot(normin[...], qkv_rows(q_ref, yy)).astype(bf16)
            return carry
        lax.fori_loop(0, NY, body, 0)

    def project_back(q_ref, lo, n):
        acc[lo:lo + n, :] = jnp.zeros((n, D), f32)

        def body(yy, carry):
            lanes = pl.ds(pl.multiple_of(yy * QW, QW), QW)
            acc[lo:lo + n, :] += dot(dqkv[lo:lo + n, lanes], qkv_rows(q_ref, yy), NT)
            return carry
        lax.fori_loop(0, NY, body, 0)

    def attend(masked):
        def body(b, carry):
            rows = pl.ds(pl.multiple_of(b * 128, 128), 128)
            for h in range(HEADS):
                q = qkv[rows, head_at(h):head_at(h) + HDIM]
                k = qkv[rows, head_at(8 + h):head_at(8 + h) + HDIM]
                scores = dot(q, k, NT) * HDIM ** -0.5
                if masked:
                    scores = jnp.where(iota((128, 128), 1) < frames[0], scores, -1e30)
                e = jnp.exp(scores - jnp.max(scores, -1, keepdims=True))
                probs[b * HEADS + h] = e / jnp.sum(e, -1, keepdims=True)
            return carry
        lax.fori_loop(0, 2, body, 0)

    def attend_back(lo, hi):
        def body(b, carry):
            rows = pl.ds(pl.multiple_of(b * 128, 128), 128)
            for h in range(HEADS):
                q = qkv[rows, head_at(h):head_at(h) + HDIM]
                k = qkv[rows, head_at(8 + h):head_at(8 + h) + HDIM]
                v = qkv[rows, head_at(16 + h):head_at(16 + h) + HDIM]
                up = dout[rows, HP * h:HP * h + HDIM]
                p = probs[b * HEADS + h]
                dv = dot(p.astype(bf16), up, TN)
                dp_ = dot(up, v, NT)
                delta = jnp.sum(p * dp_, -1, keepdims=True)
                ds = (p * (dp_ - delta)).astype(bf16)
                dq = dot(ds, k) * HDIM ** -0.5
                dk = dot(ds, q, TN) * HDIM ** -0.5
                dqkv[rows, head_at(h):head_at(h) + HDIM] = dq.astype(bf16)
                dqkv[rows, head_at(8 + h):head_at(8 + h) + HDIM] = dk.astype(bf16)
                dqkv[rows, head_at(16 + h):head_at(16 + h) + HDIM] = dv.astype(bf16)
            return carry
        lax.fori_loop(lo, hi, body, 0)

    dqkv[...] = jnp.zeros((TOK, NY * QW), bf16)

    def own_norms(i, carry):
        rows = pl.ds(pl.multiple_of(i * 64, 64), 64)
        f, r = i // 2, pl.ds(pl.multiple_of((i % 2) * 64, 64), 64)
        nm_t[rows, :], rs_t[rows, :] = norm_stats(mid[f, r, :].astype(f32))
        nm_s[rows, :], rs_s[rows, :] = norm_stats(inp[f, r, :].astype(f32))
        return carry
    lax.fori_loop(0, 4, own_norms, 0)

    wait_scatter(mrecv, arecv_sem, 0)
    acc[...] = dot(pr[...], mrecv[...].reshape(TOK, D))

    def patch_norm(i, carry):
        rows = pl.ds(pl.multiple_of(i * 64, 64), 64)
        normed, _ = norm_stats(acc[rows, :])
        normin[rows, :] = (normed * (1.0 + mod[4]) + mod[3]).astype(bf16)
        return carry
    lax.fori_loop(0, 4, patch_norm, 0)
    each(share_wait, jobs_q)
    project(q_t)
    attend(True)
    each(on_second, jobs_s)
    wait_scatter(drecv, arecv_sem, 1)
    dout[...] = dot(pr[...], drecv[...].reshape(TOK, HEADS * HP)).astype(bf16)
    for b in range(2):
        attend_back(b, b + 1)
        project_back(q_t, 128 * b, 128)
        rsend[b] = acc[128 * b:128 * b + 128, :].astype(bf16).reshape(NSEQ, 2, D)
        scatter(rsend.at[b], rrecv.at[b], 2 + b, 0, 60)
        scatter(rsend.at[b], rrecv.at[b], 2 + b, 61, 64)
        rrecv[b, s] = rsend[b, s]

    each(end_second, jobs_s)

    def frame_norm(i, carry):
        rows = pl.ds(pl.multiple_of(i * 64, 64), 64)
        normin[rows, :] = (nm_s[rows, :] * (1.0 + mod[1]) + mod[0]).astype(bf16)
        return carry
    lax.fori_loop(0, 4, frame_norm, 0)
    each(share_wait, jobs_s)
    project(q_s)
    attend(False)

    for b in range(2):
        wait_scatter(rrecv.at[b], arecv_sem, 2 + b)
    acc[...] = dot(back[...], rrecv[...].reshape(TOK, D))

    def mid_grad(i, carry):
        rows = pl.ds(pl.multiple_of(i * 64, 64), 64)
        f, r = i // 2, pl.ds(pl.multiple_of((i % 2) * 64, 64), 64)
        cell = iota((64, 1), 0) * 0 + (2 * s + f)
        masked = jnp.where(cell < frames[0], cot[f, r, :].astype(f32), 0.0)
        grad = masked + norm_back(acc[rows, :], nm_t[rows, :], rs_t[rows, :], 1.0 + mod[4])
        dmid[rows, :] = grad
        normin[rows, :] = (grad * mod[2]).astype(bf16)
        return carry
    lax.fori_loop(0, 4, mid_grad, 0)
    dout[...] = out_back(normin, o_s)
    attend_back(0, 2)
    project_back(q_s, 0, TOK)

    def last_grad(i, carry):
        rows = pl.ds(pl.multiple_of(i * 64, 64), 64)
        f, r = i // 2, pl.ds(pl.multiple_of((i % 2) * 64, 64), 64)
        dnorm = acc[rows, :].astype(bf16).astype(f32)
        grad = norm_back(dnorm, nm_s[rows, :], rs_s[rows, :], 1.0 + mod[1])
        result[f, r, :] = (dmid[rows, :] + grad).astype(bf16)
        return carry
    lax.fori_loop(0, 4, last_grad, 0)

    for cp in pending:
        cp.wait_send()
    wait_scatter(msend, asend_sem, 0)
    wait_scatter(dsend, asend_sem, 1)
    for b in range(2):
        wait_scatter(rsend.at[b], asend_sem, 2 + b)


def per_device(inputs, mid_inputs, cotangent, modulation, frames, qkv_s, out_s, qkv_t, out_t):
    vmem = pl.BlockSpec(memory_space=pltpu.VMEM)
    dma = pltpu.SemaphoreType.DMA
    out = pl.pallas_call(
        kernel,
        out_shape=jax.ShapeDtypeStruct((2, 128, D), bf16),
        in_specs=[vmem] * 4 + [pl.BlockSpec(memory_space=pltpu.SMEM)] + [vmem] * 4,
        out_specs=vmem,
        scratch_shapes=[
            pltpu.VMEM((NZ, 128, 128), bf16),
            pltpu.VMEM((NZ, 224, QW), bf16),
            pltpu.VMEM((NZ, 224, OW), bf16),
            pltpu.VMEM((NY, 2, NX, 144, QW), bf16),
            pltpu.VMEM((NY, 2, NX, HP, OW), bf16),
            pltpu.VMEM((NY, 2, NX, 144, QW), bf16),
            pltpu.VMEM((NY, 2, NX, HP, OW), bf16),
            pltpu.VMEM((NSEQ, 4, D), bf16),
            pltpu.VMEM((NSEQ, 4, D), bf16),
            pltpu.VMEM((NSEQ, 4, HEADS * HP), bf16),
            pltpu.VMEM((NSEQ, 4, HEADS * HP), bf16),
            pltpu.VMEM((2, NSEQ, 2, D), bf16),
            pltpu.VMEM((2, NSEQ, 2, D), bf16),
            pltpu.VMEM((TOK, TOK), bf16),
            pltpu.VMEM((TOK, TOK), bf16),
            pltpu.VMEM((TOK, TOK), bf16),
            pltpu.VMEM((TOK, D), bf16),
            pltpu.VMEM((TOK, NY * QW), bf16),
            pltpu.VMEM((TOK, NY * QW), bf16),
            pltpu.VMEM((TOK, HEADS * HP), bf16),
            pltpu.VMEM((2 * HEADS, 128, 128), f32),
            pltpu.VMEM((TOK, D), f32),
            pltpu.VMEM((TOK, D), f32),
            pltpu.VMEM((TOK, 1), f32),
            pltpu.VMEM((TOK, D), f32),
            pltpu.VMEM((TOK, 1), f32),
            pltpu.VMEM((TOK, D), f32),
            dma((2, 8)), dma((2, 8)), dma((8, 12)), dma((8, 12)), dma((4,)), dma((4,)),
        ],
        compiler_params=pltpu.CompilerParams(
            collective_id=0, has_side_effects=True, vmem_limit_bytes=56 * 1024 * 1024
        ),
        name="blocks_grad",
    )(
        inputs[0], mid_inputs[0], cotangent[0], modulation.reshape(6, 1, D), frames,
        qkv_s.T, out_s.T, qkv_t.T, out_t.T,
    )
    return out[None]


def solution(mesh):
    big = P("dp", "seq", None, None)
    weight = P("dp", "seq")
    return jax.shard_map(
        per_device,
        mesh=mesh,
        in_specs=(big, big, big, P("dp", None, None), P("dp")) + (weight,) * 4,
        out_specs=big,
        check_vma=False,
    )
```

```python
import jax
import jax.numpy as jnp
from jax import lax
from jax.experimental import pallas as pl
from jax.experimental.pallas import tpu as pltpu
from jax.sharding import PartitionSpec as P

HDIM = 72
HEADS = 8
D = 1152
EPS = 1e-06
TOK = 256
NY, NX, NZ = 4, 4, 16
NSEQ = NY * NZ
QW = 512
OW = 384
HP = 80
f32, bf16 = jnp.float32, jnp.bfloat16

NN = (((1,), (0,)), ((), ()))
NT = (((1,), (1,)), ((), ()))
TN = (((0,), (0,)), ((), ()))


def dot(a, b, dims=NN):
    return lax.dot_general(a, b, dims, preferred_element_type=f32)


def iota(shape, axis):
    return lax.broadcasted_iota(jnp.int32, shape, axis)


def head_at(n):
    return (n // 6) * QW + (n % 6) * HDIM


def norm_stats(x):
    center = jnp.mean(x, -1, keepdims=True)
    diff = x - center
    spread = jnp.mean(diff * diff, -1, keepdims=True)
    rstd = lax.rsqrt(spread + EPS)
    return diff * rstd, rstd


def norm_back(dnorm, normed, rstd, gain):
    g = dnorm * gain
    return rstd * (
        g
        - jnp.mean(g, -1, keepdims=True)
        - normed * jnp.mean(g * normed, -1, keepdims=True)
    )


def kernel(
    inp, mid, cot, mod, frames, qkv_s, out_s, qkv_t, out_t, result,
    zbuf, eq, eo, q_t, o_t, q_s, o_s,
    msend, mrecv, dsend, drecv, rsend, rrecv,
    pm, pr, back, normin, qkv, dqkv, dout, probs, acc, nm_t, rs_t, nm_s, rs_s, dmid,
    zsend_sem, zrecv_sem, jsend_sem, jrecv_sem, asend_sem, arecv_sem,
):
    dp = lax.axis_index("dp")
    s = lax.axis_index("seq")
    x, c = dp // 2, dp % 2
    y, z = s // NZ, s % NZ
    other = 1 - c
    pending = []

    def seq_dev(yy, zz):
        return {"seq": yy * NZ + zz}

    def x_dev(xx):
        return {"dp": xx * 2 + c}

    far = [(8, dy) for dy in range(NY)]
    near = [(dz, dy) for dy in range(NY) for dz in (0, 1)]
    beside = [(0, dy) for dy in range(1, NY)]

    def peer(dz, dy):
        return lax.rem(y + dy, NY) * NZ + lax.rem(z + dz, NZ)

    def each_peer(f):
        for dz, dy in far:
            f(peer(dz, dy))

        def body(i, carry):
            at = (lax.rem(z + 7 - i, NZ), lax.rem(z + NZ - 7 + i, NZ))
            for way, dy in near:
                f(lax.rem(y + dy, NY) * NZ + at[way])
            return carry
        lax.fori_loop(0, 7, body, 0)
        for dz, dy in beside:
            f(peer(dz, dy))

    barrier = pltpu.get_barrier_semaphore()

    for xx in ((x + 1) % NX, (x + 3) % NX):
        pl.semaphore_signal(barrier, inc=1, device_id=x_dev(xx))
    pl.semaphore_signal(barrier, inc=1, device_id={"dp": x * 2 + other})
    each_peer(lambda to: pl.semaphore_signal(barrier, inc=1, device_id={"seq": to}))

    def pack(qkv_ref, out_ref):
        q, o = qkv_ref[...], out_ref[...]

        def place(rows, g):
            hit = iota((rows, 128), 1) == iota((rows, 128), 0) + 32 * g
            return jnp.where(hit, 1.0, 0.0).astype(bf16)

        q0 = dot(q, place(27, 0), TN)[0:64]
        q1 = dot(q, place(27, 1), TN)[64:128]
        q2 = dot(q, place(27, 2), TN)[128:144]
        o2 = dot(o, place(18, 2), TN)[0:48]
        o3 = dot(o, place(18, 3), TN)[48:72]
        full = q0 + q1 + jnp.concatenate([q2, o2], 0)
        full = full + jnp.concatenate([o3, jnp.zeros((40, 128), f32)], 0)
        return full.astype(bf16)

    zbuf[z, 0:64] = pack(qkv_t, out_t)
    zbuf[z, 64:128] = pack(qkv_s, out_s)

    ri, ci = iota((TOK, TOK), 0), iota((TOK, TOK), 1)
    pm[...] = jnp.where(ci == (ri & 1) * 128 + (ri >> 2) * 2 + ((ri >> 1) & 1), 1.0, 0.0).astype(bf16)
    pr[...] = jnp.where(
        ci == ((ri & 127) >> 1) * 4 + (ri >> 7) * 2 + (ri & 1), 1.0, 0.0
    ).astype(bf16)

    back[...] = jnp.where(
        ci == (ri & 1) * 128 + ((ri & 127) >> 1) * 2 + (ri >> 7), 1.0, 0.0
    ).astype(bf16)
    msend[...] = dot(pm[...], mid[...].reshape(TOK, D)).astype(bf16).reshape(NSEQ, 4, D)

    pl.semaphore_wait(barrier, NSEQ - 1 + 3)

    def zcopy(block, way, step):
        to = (z + 1) % NZ if way == 0 else (z + NZ - 1) % NZ
        return pltpu.make_async_remote_copy(
            src_ref=zbuf.at[block], dst_ref=zbuf.at[block],
            send_sem=zsend_sem.at[way, step], recv_sem=zrecv_sem.at[way, step],
            device_id=seq_dev(y, to),
        )

    def send_to(src, dst, k, to):
        pltpu.make_async_remote_copy(
            src_ref=src.at[to], dst_ref=dst.at[s],
            send_sem=asend_sem.at[k], recv_sem=arecv_sem.at[k],
            device_id={"seq": to},
        ).start()

    def scatter(src, dst, k):
        each_peer(lambda to: send_to(src, dst, k, to))

    order = far + [(d, dy) for m in range(7, 0, -1) for dy in range(NY) for d in (m, NZ - m)] + beside

    def send_mid(lo, hi):
        for dz, dy in order[lo:hi]:
            send_to(msend, mrecv, 0, peer(dz, dy))

    def wait_scatter(ref, sem, k):
        part = ref.at[pl.ds(0, NSEQ - 1)]
        pltpu.make_async_copy(part, part, sem.at[k]).wait()

    def fill(zz, carry):
        lane = iota((224, QW), 0) - 96
        live = (lane >= 0) & (lane < 27)
        hit = live & (iota((224, QW), 1) == lane + 27 * zz)
        eq[zz] = jnp.where(hit, 1.0, 0.0).astype(bf16)
        lane = iota((224, OW), 0) - 96
        live = (lane >= 0) & (lane < 18)
        hit = live & (iota((224, OW), 1) == lane + 18 * zz + 32 * y)
        eo[zz] = jnp.where(hit, 1.0, 0.0).astype(bf16)
        return carry

    for step in range(8):
        if step > 0:
            zcopy((z + NZ - step) % NZ, 0, step - 1).wait_recv()
        cp = zcopy((z + NZ - step) % NZ, 0, step)
        cp.start()
        pending.append(cp)
        if step > 0:
            zcopy((z + step) % NZ, 1, step - 1).wait_recv()
        if step < 7:
            cp = zcopy((z + step) % NZ, 1, step)
            cp.start()
            pending.append(cp)
        send_mid(3 * step, 3 * step + 3)
        lax.fori_loop(2 * step, 2 * step + 2, fill, 0)
    zcopy((z + NZ - 8) % NZ, 0, 7).wait_recv()

    def unpack(at, q_ref, o_ref):
        whole = jnp.concatenate([zbuf[i, at:at + 64] for i in range(NZ)], 1)

        def pick(table, g):
            lo = 96 - 32 * g
            return dot(whole, table[:, lo:lo + 128, :].reshape(NZ * 128, -1)).astype(bf16)

        o_ref[y, c, x] = jnp.concatenate([pick(eo, 2)[16:64], pick(eo, 3)[0:32]], 0)
        q_ref[y, c, x] = jnp.concatenate([pick(eq, 0), pick(eq, 1), pick(eq, 2)[0:16]], 0)

    jobs_t = [
        (0, o_t, "y", 0, 48, 32), (1, o_t, "x", 48, 32, 16),
        (2, q_t, "y", 0, 80, 48), (3, q_t, "x", 80, 64, 32),
    ]
    jobs_s = [
        (4, o_s, "y", 0, 48, 32), (5, o_s, "x", 48, 32, 16),
        (6, q_s, "y", 0, 80, 48), (7, q_s, "x", 80, 64, 32),
    ]

    def view(job, phase, rel, half, core):
        _, ref, first, r, n, m = job
        lo, size = {"all": (r, n), "a": (r, m), "b": (r + m, n - m)}[half]
        rows = pl.ds(lo, size)
        axis = first if phase == 0 else ("x" if first == "y" else "y")
        if axis == "x":
            return ref.at[y if phase == 0 else slice(None), core, (x + rel) % NX, rows]
        return ref.at[(y + rel) % NY, core, x if phase == 0 else slice(None), rows]

    def hop(job, phase, rel, half, way, slot):
        first = job[2]
        axis = first if phase == 0 else ("x" if first == "y" else "y")
        step = 1 if way == 0 else 3
        dev = x_dev((x + step) % NX) if axis == "x" else seq_dev((y + step) % NY, z)
        ref = view(job, phase, rel, half, c)
        return pltpu.make_async_remote_copy(
            src_ref=ref, dst_ref=ref,
            send_sem=jsend_sem.at[job[0], phase * 4 + slot],
            recv_sem=jrecv_sem.at[job[0], phase * 4 + slot],
            device_id=dev,
        )

    def go(cp):
        cp.start()
        pending.append(cp)

    def first_step(job, phase):
        go(hop(job, phase, 0, "all", 0, 0))
        go(hop(job, phase, 0, "all", 1, 1))

    def pass_on(job, phase):
        hop(job, phase, 3, "all", 0, 0).wait_recv()
        go(hop(job, phase, 3, "a", 0, 2))
        hop(job, phase, 1, "all", 1, 1).wait_recv()
        go(hop(job, phase, 1, "b", 1, 3))

    def last_step(job, phase):
        hop(job, phase, 2, "a", 0, 2).wait_recv()
        hop(job, phase, 2, "b", 1, 3).wait_recv()

    def share(job, rel, core):
        ref = view(job, 1, rel, "all", core)
        return pltpu.make_async_remote_copy(
            src_ref=ref, dst_ref=ref,
            send_sem=jsend_sem.at[job[0], 8 + rel], recv_sem=jrecv_sem.at[job[0], 8 + rel],
            device_id={"dp": x * 2 + other},
        )

    def share_wait(job):
        for rel in range(4):
            share(job, rel, other).wait_recv()

    def live_cot(f):
        cell = iota((128, 1), 0) * 0 + (2 * s + f)
        return jnp.where(cell < frames[0], cot[f].astype(f32), 0.0)

    def out_rows(o_ref, yy):
        return jnp.concatenate([o_ref[yy, d % 2, d // 2] for d in range(HEADS)], 0)

    def qkv_rows(q_ref, yy):
        return jnp.concatenate([q_ref[yy, d % 2, d // 2] for d in range(8)], 0)

    def out_back(gated, o_ref):
        total = None
        for yy in range(NY):
            term = dot(gated[:, 256 * yy:256 * yy + OW], out_rows(o_ref, yy), NT)
            total = term if total is None else total + term
        return total.astype(bf16)

    def open_second(job):
        last_step(job, 0)
        first_step(job, 1)
        go(share(job, 0, c))

    def on_second(job):
        pass_on(job, 1)
        go(share(job, 3, c))
        go(share(job, 1, c))

    def end_second(job):
        last_step(job, 1)
        go(share(job, 2, c))

    def each(f, jobs, *args):
        for job in jobs:
            f(job, *args)

    jobs_o, jobs_q = jobs_t[:2], jobs_t[2:]
    unpack(0, q_t, o_t)
    each(first_step, jobs_t, 0)
    send_mid(24, 37)
    unpack(64, q_s, o_s)
    each(pass_on, jobs_o, 0)
    each(open_second, jobs_o)
    each(pass_on, jobs_q, 0)
    send_mid(37, 50)
    each(on_second, jobs_o)
    each(open_second, jobs_q)
    send_mid(50, 63)
    each(end_second, jobs_o)
    each(first_step, jobs_s, 0)

    each(share_wait, jobs_o)
    for f in range(2):
        normin[f * 128:(f + 1) * 128, :] = (live_cot(f) * mod[5]).astype(bf16)
    dout[...] = out_back(normin, o_t)
    for b in range(2):
        part = dot(back[128 * b:128 * b + 128, :], dout[...])
        dsend[b] = part.astype(bf16).reshape(NSEQ, 2, HEADS * HP)
        scatter(dsend.at[b], drecv.at[b], 1 + b)
        drecv[b, s] = dsend[b, s]
    mrecv[s] = msend[s]
    each(on_second, jobs_q)
    each(pass_on, jobs_s, 0)
    each(end_second, jobs_q)
    each(open_second, jobs_s)

    def project(q_ref):
        def body(yy, carry):
            lanes = pl.ds(pl.multiple_of(yy * QW, QW), QW)
            qkv[:, lanes] = dot(normin[...], qkv_rows(q_ref, yy)).astype(bf16)
            return carry
        lax.fori_loop(0, NY, body, 0)

    def project_back(q_ref, lo, n):
        acc[lo:lo + n, :] = jnp.zeros((n, D), f32)

        def body(yy, carry):
            lanes = pl.ds(pl.multiple_of(yy * QW, QW), QW)
            acc[lo:lo + n, :] += dot(dqkv[lo:lo + n, lanes], qkv_rows(q_ref, yy), NT)
            return carry
        lax.fori_loop(0, NY, body, 0)

    def attend(masked):
        def body(b, carry):
            rows = pl.ds(pl.multiple_of(b * 128, 128), 128)
            for h in range(HEADS):
                q = qkv[rows, head_at(h):head_at(h) + HDIM]
                k = qkv[rows, head_at(8 + h):head_at(8 + h) + HDIM]
                scores = dot(q, k, NT) * HDIM ** -0.5
                if masked:
                    scores = jnp.where(iota((128, 128), 1) < frames[0], scores, -1e30)
                e = jnp.exp(scores - jnp.max(scores, -1, keepdims=True))
                probs[b * HEADS + h] = e / jnp.sum(e, -1, keepdims=True)
            return carry
        lax.fori_loop(0, 2, body, 0)

    def attend_back(lo, hi):
        def body(b, carry):
            rows = pl.ds(pl.multiple_of(b * 128, 128), 128)
            for h in range(HEADS):
                q = qkv[rows, head_at(h):head_at(h) + HDIM]
                k = qkv[rows, head_at(8 + h):head_at(8 + h) + HDIM]
                v = qkv[rows, head_at(16 + h):head_at(16 + h) + HDIM]
                up = dout[rows, HP * h:HP * h + HDIM]
                p = probs[b * HEADS + h]
                dv = dot(p.astype(bf16), up, TN)
                dp_ = dot(up, v, NT)
                delta = jnp.sum(p * dp_, -1, keepdims=True)
                ds = (p * (dp_ - delta)).astype(bf16)
                dq = dot(ds, k) * HDIM ** -0.5
                dk = dot(ds, q, TN) * HDIM ** -0.5
                dqkv[rows, head_at(h):head_at(h) + HDIM] = dq.astype(bf16)
                dqkv[rows, head_at(8 + h):head_at(8 + h) + HDIM] = dk.astype(bf16)
                dqkv[rows, head_at(16 + h):head_at(16 + h) + HDIM] = dv.astype(bf16)
            return carry
        lax.fori_loop(lo, hi, body, 0)

    dqkv[...] = jnp.zeros((TOK, NY * QW), bf16)

    def own_norms(i, carry):
        rows = pl.ds(pl.multiple_of(i * 64, 64), 64)
        f, r = i // 2, pl.ds(pl.multiple_of((i % 2) * 64, 64), 64)
        nm_t[rows, :], rs_t[rows, :] = norm_stats(mid[f, r, :].astype(f32))
        nm_s[rows, :], rs_s[rows, :] = norm_stats(inp[f, r, :].astype(f32))
        return carry
    lax.fori_loop(0, 4, own_norms, 0)

    wait_scatter(mrecv, arecv_sem, 0)
    acc[...] = dot(pr[...], mrecv[...].reshape(TOK, D))

    def patch_norm(i, carry):
        rows = pl.ds(pl.multiple_of(i * 64, 64), 64)
        normed, _ = norm_stats(acc[rows, :])
        normin[rows, :] = (normed * (1.0 + mod[4]) + mod[3]).astype(bf16)
        return carry
    lax.fori_loop(0, 4, patch_norm, 0)
    each(share_wait, jobs_q)
    project(q_t)
    attend(True)
    for b in range(2):
        wait_scatter(drecv.at[b], arecv_sem, 1 + b)
        dout[128 * b:128 * b + 128, :] = drecv[b].reshape(128, HEADS * HP)
        attend_back(b, b + 1)
        project_back(q_t, 128 * b, 128)
        rsend[b] = acc[128 * b:128 * b + 128, :].astype(bf16).reshape(NSEQ, 2, D)
        scatter(rsend.at[b], rrecv.at[b], 3 + b)
        rrecv[b, s] = rsend[b, s]
        if b == 0:
            each(on_second, jobs_s)

    each(end_second, jobs_s)

    def frame_norm(i, carry):
        rows = pl.ds(pl.multiple_of(i * 64, 64), 64)
        normin[rows, :] = (nm_s[rows, :] * (1.0 + mod[1]) + mod[0]).astype(bf16)
        return carry
    lax.fori_loop(0, 4, frame_norm, 0)
    each(share_wait, jobs_s)
    project(q_s)
    attend(False)

    for b in range(2):
        wait_scatter(rrecv.at[b], arecv_sem, 3 + b)
    acc[...] = dot(back[...], rrecv[...].reshape(TOK, D))

    def mid_grad(i, carry):
        rows = pl.ds(pl.multiple_of(i * 64, 64), 64)
        f, r = i // 2, pl.ds(pl.multiple_of((i % 2) * 64, 64), 64)
        cell = iota((64, 1), 0) * 0 + (2 * s + f)
        masked = jnp.where(cell < frames[0], cot[f, r, :].astype(f32), 0.0)
        grad = masked + norm_back(acc[rows, :], nm_t[rows, :], rs_t[rows, :], 1.0 + mod[4])
        dmid[rows, :] = grad
        normin[rows, :] = (grad * mod[2]).astype(bf16)
        return carry
    lax.fori_loop(0, 4, mid_grad, 0)
    dout[...] = out_back(normin, o_s)
    attend_back(0, 2)
    project_back(q_s, 0, TOK)

    def last_grad(i, carry):
        rows = pl.ds(pl.multiple_of(i * 64, 64), 64)
        f, r = i // 2, pl.ds(pl.multiple_of((i % 2) * 64, 64), 64)
        dnorm = acc[rows, :].astype(bf16).astype(f32)
        grad = norm_back(dnorm, nm_s[rows, :], rs_s[rows, :], 1.0 + mod[1])
        result[f, r, :] = (dmid[rows, :] + grad).astype(bf16)
        return carry
    lax.fori_loop(0, 4, last_grad, 0)

    for cp in pending:
        cp.wait_send()
    wait_scatter(msend, asend_sem, 0)
    for b in range(2):
        wait_scatter(dsend.at[b], asend_sem, 1 + b)
        wait_scatter(rsend.at[b], asend_sem, 3 + b)


def per_device(inputs, mid_inputs, cotangent, modulation, frames, qkv_s, out_s, qkv_t, out_t):
    vmem = pl.BlockSpec(memory_space=pltpu.VMEM)
    dma = pltpu.SemaphoreType.DMA
    out = pl.pallas_call(
        kernel,
        out_shape=jax.ShapeDtypeStruct((2, 128, D), bf16),
        in_specs=[vmem] * 4 + [pl.BlockSpec(memory_space=pltpu.SMEM)] + [vmem] * 4,
        out_specs=vmem,
        scratch_shapes=[
            pltpu.VMEM((NZ, 128, 128), bf16),
            pltpu.VMEM((NZ, 224, QW), bf16),
            pltpu.VMEM((NZ, 224, OW), bf16),
            pltpu.VMEM((NY, 2, NX, 144, QW), bf16),
            pltpu.VMEM((NY, 2, NX, HP, OW), bf16),
            pltpu.VMEM((NY, 2, NX, 144, QW), bf16),
            pltpu.VMEM((NY, 2, NX, HP, OW), bf16),
            pltpu.VMEM((NSEQ, 4, D), bf16),
            pltpu.VMEM((NSEQ, 4, D), bf16),
            pltpu.VMEM((2, NSEQ, 2, HEADS * HP), bf16),
            pltpu.VMEM((2, NSEQ, 2, HEADS * HP), bf16),
            pltpu.VMEM((2, NSEQ, 2, D), bf16),
            pltpu.VMEM((2, NSEQ, 2, D), bf16),
            pltpu.VMEM((TOK, TOK), bf16),
            pltpu.VMEM((TOK, TOK), bf16),
            pltpu.VMEM((TOK, TOK), bf16),
            pltpu.VMEM((TOK, D), bf16),
            pltpu.VMEM((TOK, NY * QW), bf16),
            pltpu.VMEM((TOK, NY * QW), bf16),
            pltpu.VMEM((TOK, HEADS * HP), bf16),
            pltpu.VMEM((2 * HEADS, 128, 128), f32),
            pltpu.VMEM((TOK, D), f32),
            pltpu.VMEM((TOK, D), f32),
            pltpu.VMEM((TOK, 1), f32),
            pltpu.VMEM((TOK, D), f32),
            pltpu.VMEM((TOK, 1), f32),
            pltpu.VMEM((TOK, D), f32),
            dma((2, 8)), dma((2, 8)), dma((8, 12)), dma((8, 12)), dma((5,)), dma((5,)),
        ],
        compiler_params=pltpu.CompilerParams(
            collective_id=0, has_side_effects=True, vmem_limit_bytes=42 * 1024 * 1024
        ),
        name="blocks_grad",
    )(
        inputs[0], mid_inputs[0], cotangent[0], modulation.reshape(6, 1, D), frames,
        qkv_s.T, out_s.T, qkv_t.T, out_t.T,
    )
    return out[None]


def solution(mesh):
    big = P("dp", "seq", None, None)
    weight = P("dp", "seq")
    return jax.shard_map(
        per_device,
        mesh=mesh,
        in_specs=(big, big, big, P("dp", None, None), P("dp")) + (weight,) * 4,
        out_specs=big,
        check_vma=False,
    )
```

```python
import jax
import jax.numpy as jnp
from jax import lax
from jax.experimental import pallas as pl
from jax.experimental.pallas import tpu as pltpu
from jax.sharding import PartitionSpec as P

HDIM = 72
HEADS = 8
D = 1152
EPS = 1e-06
TOK = 256
NY, NX, NZ = 4, 4, 16
NSEQ = NY * NZ
QW = 512
OW = 384
HP = 80
f32, bf16 = jnp.float32, jnp.bfloat16

NN = (((1,), (0,)), ((), ()))
NT = (((1,), (1,)), ((), ()))
TN = (((0,), (0,)), ((), ()))


def dot(a, b, dims=NN):
    return lax.dot_general(a, b, dims, preferred_element_type=f32)


def iota(shape, axis):
    return lax.broadcasted_iota(jnp.int32, shape, axis)


def head_at(n):
    return (n // 6) * QW + (n % 6) * HDIM


def norm_stats(x):
    center = jnp.mean(x, -1, keepdims=True)
    diff = x - center
    spread = jnp.mean(diff * diff, -1, keepdims=True)
    rstd = lax.rsqrt(spread + EPS)
    return diff * rstd, rstd


def norm_back(dnorm, normed, rstd, gain):
    g = dnorm * gain
    return rstd * (
        g
        - jnp.mean(g, -1, keepdims=True)
        - normed * jnp.mean(g * normed, -1, keepdims=True)
    )


def kernel(
    inp_hbm, mid_hbm, cot_hbm, mod_hbm, frames, qkv_s_hbm, out_s_hbm, qkv_t_hbm, out_t_hbm, result,
    inp, mid, cot, mod, qkv_s, out_s, qkv_t, out_t, load_sem,
    zbuf, eq, eo, q_t, o_t, q_s, o_s,
    msend, mrecv, dsend, drecv, rsend, rrecv,
    pm, pr, back, normin, qkv, dqkv, dout, probs, acc, nm_t, rs_t, nm_s, rs_s, dmid,
    zsend_sem, zrecv_sem, jsend_sem, jrecv_sem, asend_sem, arecv_sem,
):
    dp = lax.axis_index("dp")
    s = lax.axis_index("seq")
    x, c = dp // 2, dp % 2
    y, z = s // NZ, s % NZ
    other = 1 - c
    pending = []

    loads = [
        pltpu.make_async_copy(src, dst, load_sem.at[i])
        for i, (src, dst) in enumerate((
            (qkv_t_hbm, qkv_t), (out_t_hbm, out_t), (qkv_s_hbm, qkv_s), (out_s_hbm, out_s),
            (mid_hbm, mid), (cot_hbm, cot), (mod_hbm, mod), (inp_hbm, inp),
        ))
    ]
    for cp in loads:
        cp.start()

    def seq_dev(yy, zz):
        return {"seq": yy * NZ + zz}

    def x_dev(xx):
        return {"dp": xx * 2 + c}

    far = [(8, dy) for dy in range(NY)]
    near = [(dz, dy) for dy in range(NY) for dz in (0, 1)]
    beside = [(0, dy) for dy in range(1, NY)]

    def peer(dz, dy):
        return lax.rem(y + dy, NY) * NZ + lax.rem(z + dz, NZ)

    def each_peer(f):
        for dz, dy in far:
            f(peer(dz, dy))

        def body(i, carry):
            at = (lax.rem(z + 7 - i, NZ), lax.rem(z + NZ - 7 + i, NZ))
            for way, dy in near:
                f(lax.rem(y + dy, NY) * NZ + at[way])
            return carry
        lax.fori_loop(0, 7, body, 0)
        for dz, dy in beside:
            f(peer(dz, dy))

    barrier = pltpu.get_barrier_semaphore()

    for xx in ((x + 1) % NX, (x + 3) % NX):
        pl.semaphore_signal(barrier, inc=1, device_id=x_dev(xx))
    pl.semaphore_signal(barrier, inc=1, device_id={"dp": x * 2 + other})
    each_peer(lambda to: pl.semaphore_signal(barrier, inc=1, device_id={"seq": to}))

    def pack(qkv_ref, out_ref):
        q, o = qkv_ref[...], out_ref[...]

        def place(rows, g):
            hit = iota((rows, 128), 1) == iota((rows, 128), 0) + 32 * g
            return jnp.where(hit, 1.0, 0.0).astype(bf16)

        q0 = dot(q, place(27, 0), TN)[0:64]
        q1 = dot(q, place(27, 1), TN)[64:128]
        q2 = dot(q, place(27, 2), TN)[128:144]
        o2 = dot(o, place(18, 2), TN)[0:48]
        o3 = dot(o, place(18, 3), TN)[48:72]
        full = q0 + q1 + jnp.concatenate([q2, o2], 0)
        full = full + jnp.concatenate([o3, jnp.zeros((40, 128), f32)], 0)
        return full.astype(bf16)

    for cp in loads[:4]:
        cp.wait()
    zbuf[z, 0] = pack(qkv_t, out_t)
    zbuf[z, 1] = pack(qkv_s, out_s)

    ri, ci = iota((TOK, TOK), 0), iota((TOK, TOK), 1)
    pm[...] = jnp.where(ci == (ri & 1) * 128 + (ri >> 2) * 2 + ((ri >> 1) & 1), 1.0, 0.0).astype(bf16)
    pr[...] = jnp.where(
        ci == ((ri & 127) >> 1) * 4 + (ri >> 7) * 2 + (ri & 1), 1.0, 0.0
    ).astype(bf16)

    back[...] = jnp.where(
        ci == (ri & 1) * 128 + ((ri & 127) >> 1) * 2 + (ri >> 7), 1.0, 0.0
    ).astype(bf16)
    loads[4].wait()
    msend[...] = dot(pm[...], mid[...].reshape(TOK, D)).astype(bf16).reshape(NSEQ, 4, D)

    pl.semaphore_wait(barrier, NSEQ - 1 + 3)

    def zcopy(block, way, step):
        to = lax.rem(z + 1, NZ) if way == 0 else lax.rem(z + NZ - 1, NZ)
        ref = zbuf.at[block]
        return pltpu.make_async_remote_copy(
            src_ref=ref, dst_ref=ref,
            send_sem=zsend_sem.at[way, step], recv_sem=zrecv_sem.at[way, step],
            device_id=seq_dev(y, to),
        )

    def ring_step(step):
        for way, block in ((0, lax.rem(z + NZ - step, NZ)), (1, lax.rem(z + step, NZ))):
            if step > 0 and not (way == 1 and step == 8):
                zcopy(block, way, step - 1).wait_recv()
            if step < 8 - way:
                cp = zcopy(block, way, step)
                cp.start()
                pending.append(cp)

    def send_to(src, dst, k, to):
        pltpu.make_async_remote_copy(
            src_ref=src.at[to], dst_ref=dst.at[s],
            send_sem=asend_sem.at[k], recv_sem=arecv_sem.at[k],
            device_id={"seq": to},
        ).start()

    def scatter(src, dst, k):
        each_peer(lambda to: send_to(src, dst, k, to))

    order = far + [(d, dy) for m in range(7, 0, -1) for dy in range(NY) for d in (m, NZ - m)] + beside

    def send_mid(lo, hi):
        for dz, dy in order[lo:hi]:
            send_to(msend, mrecv, 0, peer(dz, dy))

    def wait_scatter(ref, sem, k):
        part = ref.at[pl.ds(0, NSEQ - 1)]
        pltpu.make_async_copy(part, part, sem.at[k]).wait()

    def fill(zz, carry):
        lane = iota((224, QW), 0) - 96
        live = (lane >= 0) & (lane < 27)
        hit = live & (iota((224, QW), 1) == lane + 27 * zz)
        eq[zz] = jnp.where(hit, 1.0, 0.0).astype(bf16)
        lane = iota((224, OW), 0) - 96
        live = (lane >= 0) & (lane < 18)
        hit = live & (iota((224, OW), 1) == lane + 18 * zz + 32 * y)
        eo[zz] = jnp.where(hit, 1.0, 0.0).astype(bf16)
        return carry

    for step in range(8):
        ring_step(step)
        send_mid(step, step + 1)
        lax.fori_loop(2 * step, 2 * step + 2, fill, 0)
    ring_step(8)

    def unpack(kind, q_ref, o_ref):
        whole = jnp.concatenate([zbuf[i, kind] for i in range(NZ)], 1)

        def pick(table, g):
            lo = 96 - 32 * g
            return dot(whole, table[:, lo:lo + 128, :].reshape(NZ * 128, -1)).astype(bf16)

        o_ref[y, c, x] = jnp.concatenate([pick(eo, 2)[16:64], pick(eo, 3)[0:32]], 0)
        q_ref[y, c, x] = jnp.concatenate([pick(eq, 0), pick(eq, 1), pick(eq, 2)[0:16]], 0)

    jobs_t = [
        (0, o_t, "y", 0, 32, 16), (1, o_t, "x", 32, 48, 32),
        (2, q_t, "y", 0, 80, 48), (3, q_t, "x", 80, 64, 32),
    ]
    jobs_s = [
        (4, o_s, "y", 0, 32, 16), (5, o_s, "x", 32, 48, 32),
        (6, q_s, "y", 0, 80, 48), (7, q_s, "x", 80, 64, 32),
    ]

    def view(job, phase, rel, half, core):
        _, ref, first, r, n, m = job
        lo, size = {"all": (r, n), "a": (r, m), "b": (r + m, n - m)}[half]
        rows = pl.ds(lo, size)
        axis = first if phase == 0 else ("x" if first == "y" else "y")
        if axis == "x":
            return ref.at[y if phase == 0 else slice(None), core, (x + rel) % NX, rows]
        return ref.at[(y + rel) % NY, core, x if phase == 0 else slice(None), rows]

    def hop(job, phase, rel, half, way, slot):
        first = job[2]
        axis = first if phase == 0 else ("x" if first == "y" else "y")
        step = 1 if way == 0 else 3
        dev = x_dev((x + step) % NX) if axis == "x" else seq_dev((y + step) % NY, z)
        ref = view(job, phase, rel, half, c)
        return pltpu.make_async_remote_copy(
            src_ref=ref, dst_ref=ref,
            send_sem=jsend_sem.at[job[0], phase * 4 + slot],
            recv_sem=jrecv_sem.at[job[0], phase * 4 + slot],
            device_id=dev,
        )

    def go(cp):
        cp.start()
        pending.append(cp)

    def first_step(job, phase):
        go(hop(job, phase, 0, "all", 0, 0))
        go(hop(job, phase, 0, "all", 1, 1))

    def pass_on(job, phase):
        hop(job, phase, 3, "all", 0, 0).wait_recv()
        go(hop(job, phase, 3, "a", 0, 2))
        hop(job, phase, 1, "all", 1, 1).wait_recv()
        go(hop(job, phase, 1, "b", 1, 3))

    def last_step(job, phase):
        hop(job, phase, 2, "a", 0, 2).wait_recv()
        hop(job, phase, 2, "b", 1, 3).wait_recv()

    def share(job, rel, core):
        ref = view(job, 1, rel, "all", core)
        return pltpu.make_async_remote_copy(
            src_ref=ref, dst_ref=ref,
            send_sem=jsend_sem.at[job[0], 8 + rel], recv_sem=jrecv_sem.at[job[0], 8 + rel],
            device_id={"dp": x * 2 + other},
        )

    def share_wait(job):
        for rel in range(4):
            share(job, rel, other).wait_recv()

    def live_cot(f):
        cell = iota((128, 1), 0) * 0 + (2 * s + f)
        return jnp.where(cell < frames[0], cot[f].astype(f32), 0.0)

    def out_rows(o_ref, yy):
        return jnp.concatenate([o_ref[yy, d % 2, d // 2] for d in range(HEADS)], 0)

    def qkv_rows(q_ref, yy):
        return jnp.concatenate([q_ref[yy, d % 2, d // 2] for d in range(8)], 0)

    def out_back(gated, o_ref):
        total = None
        for yy in range(NY):
            term = dot(gated[:, 256 * yy:256 * yy + OW], out_rows(o_ref, yy), NT)
            total = term if total is None else total + term
        return total.astype(bf16)

    def open_second(job):
        last_step(job, 0)
        first_step(job, 1)
        go(share(job, 0, c))

    def on_second(job):
        pass_on(job, 1)
        go(share(job, 3, c))
        go(share(job, 1, c))

    def end_second(job):
        last_step(job, 1)
        go(share(job, 2, c))

    def each(f, jobs, *args):
        for job in jobs:
            f(job, *args)

    jobs_o, jobs_q = jobs_t[:2], jobs_t[2:]
    unpack(0, q_t, o_t)
    each(first_step, jobs_t, 0)
    send_mid(8, 20)
    unpack(1, q_s, o_s)
    each(pass_on, jobs_o, 0)
    each(open_second, jobs_o)
    send_mid(20, 32)
    each(pass_on, jobs_q, 0)
    send_mid(32, 44)
    each(on_second, jobs_o)
    each(open_second, jobs_q)
    send_mid(44, 63)
    for cp in loads[5:]:
        cp.wait()
    for f in range(2):
        normin[f * 128:(f + 1) * 128, :] = (live_cot(f) * mod[5]).astype(bf16)
    each(end_second, jobs_o)
    each(first_step, jobs_s, 0)

    each(share_wait, jobs_o)
    dout[...] = out_back(normin, o_t)
    for b in range(2):
        part = dot(back[128 * b:128 * b + 128, :], dout[...])
        dsend[b] = part.astype(bf16).reshape(NSEQ, 2, HEADS * HP)
        scatter(dsend.at[b], drecv.at[b], 1 + b)
        drecv[b, s] = dsend[b, s]
    mrecv[s] = msend[s]
    each(on_second, jobs_q)
    each(pass_on, jobs_s, 0)
    each(end_second, jobs_q)
    each(open_second, jobs_s)

    def project(q_ref):
        def body(yy, carry):
            lanes = pl.ds(pl.multiple_of(yy * QW, QW), QW)
            qkv[:, lanes] = dot(normin[...], qkv_rows(q_ref, yy)).astype(bf16)
            return carry
        lax.fori_loop(0, NY, body, 0)

    def project_back(q_ref, lo, n):
        acc[lo:lo + n, :] = jnp.zeros((n, D), f32)

        def body(yy, carry):
            lanes = pl.ds(pl.multiple_of(yy * QW, QW), QW)
            acc[lo:lo + n, :] += dot(dqkv[lo:lo + n, lanes], qkv_rows(q_ref, yy), NT)
            return carry
        lax.fori_loop(0, NY, body, 0)

    def attend(masked, lo=0, hi=2):
        def body(b, carry):
            rows = pl.ds(pl.multiple_of(b * 128, 128), 128)
            for h in range(HEADS):
                q = qkv[rows, head_at(h):head_at(h) + HDIM]
                k = qkv[rows, head_at(8 + h):head_at(8 + h) + HDIM]
                scores = dot(k, q, NT) * HDIM ** -0.5
                if masked:
                    scores = jnp.where(iota((128, 128), 0) < frames[0], scores, -1e30)
                e = jnp.exp(scores - jnp.max(scores, 0, keepdims=True))
                probs[b * HEADS + h] = e / jnp.sum(e, 0, keepdims=True)
            return carry
        lax.fori_loop(lo, hi, body, 0)

    def attend_back(lo, hi):
        def body(b, carry):
            rows = pl.ds(pl.multiple_of(b * 128, 128), 128)
            for h in range(HEADS):
                q = qkv[rows, head_at(h):head_at(h) + HDIM]
                k = qkv[rows, head_at(8 + h):head_at(8 + h) + HDIM]
                v = qkv[rows, head_at(16 + h):head_at(16 + h) + HDIM]
                up = dout[rows, HP * h:HP * h + HDIM]
                p = probs[b * HEADS + h]
                dv = dot(p.astype(bf16), up)
                dp_ = dot(v, up, NT)
                delta = jnp.sum(p * dp_, 0, keepdims=True)
                ds = (p * (dp_ - delta)).astype(bf16)
                dq = dot(ds, k, TN) * HDIM ** -0.5
                dk = dot(ds, q) * HDIM ** -0.5
                dqkv[rows, head_at(h):head_at(h) + HDIM] = dq.astype(bf16)
                dqkv[rows, head_at(8 + h):head_at(8 + h) + HDIM] = dk.astype(bf16)
                dqkv[rows, head_at(16 + h):head_at(16 + h) + HDIM] = dv.astype(bf16)
            return carry
        lax.fori_loop(lo, hi, body, 0)

    dqkv[...] = jnp.zeros((TOK, NY * QW), bf16)

    def own_norms(i, carry):
        rows = pl.ds(pl.multiple_of(i * 64, 64), 64)
        f, r = i // 2, pl.ds(pl.multiple_of((i % 2) * 64, 64), 64)
        nm_t[rows, :], rs_t[rows, :] = norm_stats(mid[f, r, :].astype(f32))
        nm_s[rows, :], rs_s[rows, :] = norm_stats(inp[f, r, :].astype(f32))
        return carry
    lax.fori_loop(0, 4, own_norms, 0)

    wait_scatter(mrecv, arecv_sem, 0)
    acc[...] = dot(pr[...], mrecv[...].reshape(TOK, D))

    def patch_norm(i, carry):
        rows = pl.ds(pl.multiple_of(i * 64, 64), 64)
        normed, _ = norm_stats(acc[rows, :])
        normin[rows, :] = (normed * (1.0 + mod[4]) + mod[3]).astype(bf16)
        return carry
    lax.fori_loop(0, 4, patch_norm, 0)
    each(share_wait, jobs_q)
    project(q_t)
    for b in range(2):
        attend(True, b, b + 1)
        wait_scatter(drecv.at[b], arecv_sem, 1 + b)
        dout[128 * b:128 * b + 128, :] = drecv[b].reshape(128, HEADS * HP)
        attend_back(b, b + 1)
        project_back(q_t, 128 * b, 128)
        rsend[b] = acc[128 * b:128 * b + 128, :].astype(bf16).reshape(NSEQ, 2, D)
        scatter(rsend.at[b], rrecv.at[b], 3 + b)
        rrecv[b, s] = rsend[b, s]
        if b == 0:
            each(on_second, jobs_s)

    each(end_second, jobs_s)

    def frame_norm(i, carry):
        rows = pl.ds(pl.multiple_of(i * 64, 64), 64)
        normin[rows, :] = (nm_s[rows, :] * (1.0 + mod[1]) + mod[0]).astype(bf16)
        return carry
    lax.fori_loop(0, 4, frame_norm, 0)
    each(share_wait, jobs_s)
    project(q_s)
    attend(False)

    wait_scatter(rrecv.at[0], arecv_sem, 3)
    acc[...] = dot(back[:, 0:128], rrecv[0].reshape(128, D))
    wait_scatter(rrecv.at[1], arecv_sem, 4)
    acc[...] += dot(back[:, 128:256], rrecv[1].reshape(128, D))

    def mid_grad(i, carry):
        rows = pl.ds(pl.multiple_of(i * 64, 64), 64)
        f, r = i // 2, pl.ds(pl.multiple_of((i % 2) * 64, 64), 64)
        cell = iota((64, 1), 0) * 0 + (2 * s + f)
        masked = jnp.where(cell < frames[0], cot[f, r, :].astype(f32), 0.0)
        grad = masked + norm_back(acc[rows, :], nm_t[rows, :], rs_t[rows, :], 1.0 + mod[4])
        dmid[rows, :] = grad
        normin[rows, :] = (grad * mod[2]).astype(bf16)
        return carry
    lax.fori_loop(0, 4, mid_grad, 0)
    dout[...] = out_back(normin, o_s)
    attend_back(0, 2)
    project_back(q_s, 0, TOK)

    def last_grad(i, carry):
        rows = pl.ds(pl.multiple_of(i * 64, 64), 64)
        f, r = i // 2, pl.ds(pl.multiple_of((i % 2) * 64, 64), 64)
        dnorm = acc[rows, :].astype(bf16).astype(f32)
        grad = norm_back(dnorm, nm_s[rows, :], rs_s[rows, :], 1.0 + mod[1])
        result[f, r, :] = (dmid[rows, :] + grad).astype(bf16)
        return carry
    lax.fori_loop(0, 4, last_grad, 0)

    for cp in pending:
        cp.wait_send()
    wait_scatter(msend, asend_sem, 0)
    for b in range(2):
        wait_scatter(dsend.at[b], asend_sem, 1 + b)
        wait_scatter(rsend.at[b], asend_sem, 3 + b)


def per_device(inputs, mid_inputs, cotangent, modulation, frames, qkv_s, out_s, qkv_t, out_t):
    vmem, hbm = pl.BlockSpec(memory_space=pltpu.VMEM), pl.BlockSpec(memory_space=pltpu.HBM)
    dma = pltpu.SemaphoreType.DMA
    out = pl.pallas_call(
        kernel,
        out_shape=jax.ShapeDtypeStruct((2, 128, D), bf16),
        in_specs=[hbm] * 4 + [pl.BlockSpec(memory_space=pltpu.SMEM)] + [hbm] * 4,
        out_specs=vmem,
        scratch_shapes=[
            pltpu.VMEM((2, 128, D), bf16),
            pltpu.VMEM((2, 128, D), bf16),
            pltpu.VMEM((2, 128, D), bf16),
            pltpu.VMEM((6, 1, D), f32),
            pltpu.VMEM((27, 144), bf16),
            pltpu.VMEM((18, 72), bf16),
            pltpu.VMEM((27, 144), bf16),
            pltpu.VMEM((18, 72), bf16),
            dma((8,)),
            pltpu.VMEM((NZ, 2, 64, 128), bf16),
            pltpu.VMEM((NZ, 224, QW), bf16),
            pltpu.VMEM((NZ, 224, OW), bf16),
            pltpu.VMEM((NY, 2, NX, 144, QW), bf16),
            pltpu.VMEM((NY, 2, NX, HP, OW), bf16),
            pltpu.VMEM((NY, 2, NX, 144, QW), bf16),
            pltpu.VMEM((NY, 2, NX, HP, OW), bf16),
            pltpu.VMEM((NSEQ, 4, D), bf16),
            pltpu.VMEM((NSEQ, 4, D), bf16),
            pltpu.VMEM((2, NSEQ, 2, HEADS * HP), bf16),
            pltpu.VMEM((2, NSEQ, 2, HEADS * HP), bf16),
            pltpu.VMEM((2, NSEQ, 2, D), bf16),
            pltpu.VMEM((2, NSEQ, 2, D), bf16),
            pltpu.VMEM((TOK, TOK), bf16),
            pltpu.VMEM((TOK, TOK), bf16),
            pltpu.VMEM((TOK, TOK), bf16),
            pltpu.VMEM((TOK, D), bf16),
            pltpu.VMEM((TOK, NY * QW), bf16),
            pltpu.VMEM((TOK, NY * QW), bf16),
            pltpu.VMEM((TOK, HEADS * HP), bf16),
            pltpu.VMEM((2 * HEADS, 128, 128), f32),
            pltpu.VMEM((TOK, D), f32),
            pltpu.VMEM((TOK, D), f32),
            pltpu.VMEM((TOK, 1), f32),
            pltpu.VMEM((TOK, D), f32),
            pltpu.VMEM((TOK, 1), f32),
            pltpu.VMEM((TOK, D), f32),
            dma((2, 8)), dma((2, 8)), dma((8, 12)), dma((8, 12)), dma((5,)), dma((5,)),
        ],
        compiler_params=pltpu.CompilerParams(
            collective_id=0, has_side_effects=True, vmem_limit_bytes=56 * 1024 * 1024
        ),
        name="blocks_grad",
    )(
        inputs[0], mid_inputs[0], cotangent[0], modulation.reshape(6, 1, D), frames,
        qkv_s.T, out_s.T, qkv_t.T, out_t.T,
    )
    return out[None]


def solution(mesh):
    big = P("dp", "seq", None, None)
    weight = P("dp", "seq")
    return jax.shard_map(
        per_device,
        mesh=mesh,
        in_specs=(big, big, big, P("dp", None, None), P("dp")) + (weight,) * 4,
        out_specs=big,
        check_vma=False,
    )
```

```python
import jax
import jax.numpy as jnp
from jax import lax
from jax.experimental import pallas as pl
from jax.experimental.pallas import tpu as pltpu
from jax.sharding import PartitionSpec as P

HDIM = 72
HEADS = 8
D = 1152
EPS = 1e-06
TOK = 256
NY, NX, NZ = 4, 4, 16
NSEQ = NY * NZ
QW = 512
OW = 384
HP = 80
f32, bf16 = jnp.float32, jnp.bfloat16

NN = (((1,), (0,)), ((), ()))
NT = (((1,), (1,)), ((), ()))
TN = (((0,), (0,)), ((), ()))


def dot(a, b, dims=NN):
    return lax.dot_general(a, b, dims, preferred_element_type=f32)


def iota(shape, axis):
    return lax.broadcasted_iota(jnp.int32, shape, axis)


def head_at(n):
    return (n // 6) * QW + (n % 6) * HDIM


def norm_stats(x):
    center = jnp.mean(x, -1, keepdims=True)
    diff = x - center
    spread = jnp.mean(diff * diff, -1, keepdims=True)
    rstd = lax.rsqrt(spread + EPS)
    return diff * rstd, rstd


def norm_back(dnorm, normed, rstd, gain):
    g = dnorm * gain
    return rstd * (
        g
        - jnp.mean(g, -1, keepdims=True)
        - normed * jnp.mean(g * normed, -1, keepdims=True)
    )


def kernel(
    inp_hbm, mid_hbm, cot_hbm, mod_hbm, frames, qkv_s_hbm, out_s_hbm, qkv_t_hbm, out_t_hbm, result,
    inp, mid, cot, mod, qkv_s, out_s, qkv_t, out_t, load_sem,
    zbuf, eq, eo, q_t, o_t, q_s, o_s,
    msend, mrecv, dsend, drecv, rsend, rrecv,
    pm, pr, back, normin, qkv, dqkv, dout, probs, acc, nm_t, rs_t, nm_s, rs_s, dmid,
    zsend_sem, zrecv_sem, jsend_sem, jrecv_sem, asend_sem, arecv_sem,
):
    dp = lax.axis_index("dp")
    s = lax.axis_index("seq")
    x, c = dp // 2, dp % 2
    y, z = s // NZ, s % NZ
    other = 1 - c
    pending = []

    loads = [
        pltpu.make_async_copy(src, dst, load_sem.at[i])
        for i, (src, dst) in enumerate((
            (qkv_t_hbm, qkv_t), (out_t_hbm, out_t), (qkv_s_hbm, qkv_s), (out_s_hbm, out_s),
            (mid_hbm, mid), (cot_hbm, cot), (mod_hbm, mod), (inp_hbm, inp),
        ))
    ]
    for cp in loads:
        cp.start()

    def seq_dev(yy, zz):
        return {"seq": yy * NZ + zz}

    def x_dev(xx):
        return {"dp": xx * 2 + c}

    far = [(8, dy) for dy in range(NY)]
    near = [(dz, dy) for dy in range(NY) for dz in (0, 1)]
    beside = [(0, dy) for dy in range(1, NY)]

    def peer(dz, dy):
        return lax.rem(y + dy, NY) * NZ + lax.rem(z + dz, NZ)

    def each_peer(f):
        for dz, dy in far:
            f(peer(dz, dy))

        def body(i, carry):
            at = (lax.rem(z + 7 - i, NZ), lax.rem(z + NZ - 7 + i, NZ))
            for way, dy in near:
                f(lax.rem(y + dy, NY) * NZ + at[way])
            return carry
        lax.fori_loop(0, 7, body, 0)
        for dz, dy in beside:
            f(peer(dz, dy))

    barrier = pltpu.get_barrier_semaphore()

    for xx in ((x + 1) % NX, (x + 3) % NX):
        pl.semaphore_signal(barrier, inc=1, device_id=x_dev(xx))
    pl.semaphore_signal(barrier, inc=1, device_id={"dp": x * 2 + other})
    each_peer(lambda to: pl.semaphore_signal(barrier, inc=1, device_id={"seq": to}))

    def pack(qkv_ref, out_ref):
        q, o = qkv_ref[...], out_ref[...]

        def place(rows, g):
            hit = iota((rows, 128), 1) == iota((rows, 128), 0) + 32 * g
            return jnp.where(hit, 1.0, 0.0).astype(bf16)

        q0 = dot(q, place(27, 0), TN)[0:64]
        q1 = dot(q, place(27, 1), TN)[64:128]
        q2 = dot(q, place(27, 2), TN)[128:144]
        o2 = dot(o, place(18, 2), TN)[0:48]
        o3 = dot(o, place(18, 3), TN)[48:72]
        full = q0 + q1 + jnp.concatenate([q2, o2], 0)
        full = full + jnp.concatenate([o3, jnp.zeros((40, 128), f32)], 0)
        return full.astype(bf16)

    for cp in loads[:4]:
        cp.wait()
    zbuf[z, 0] = pack(qkv_t, out_t)
    zbuf[z, 1] = pack(qkv_s, out_s)

    ri, ci = iota((TOK, TOK), 0), iota((TOK, TOK), 1)
    pm[...] = jnp.where(ci == (ri & 1) * 128 + (ri >> 2) * 2 + ((ri >> 1) & 1), 1.0, 0.0).astype(bf16)
    pr[...] = jnp.where(
        ci == ((ri & 127) >> 1) * 4 + (ri >> 7) * 2 + (ri & 1), 1.0, 0.0
    ).astype(bf16)

    back[...] = jnp.where(
        ci == (ri & 1) * 128 + ((ri & 127) >> 1) * 2 + (ri >> 7), 1.0, 0.0
    ).astype(bf16)
    dqkv[...] = jnp.zeros((TOK, NY * QW), bf16)
    loads[4].wait()
    msend[...] = dot(pm[...], mid[...].reshape(TOK, D)).astype(bf16).reshape(NSEQ, 4, D)

    pl.semaphore_wait(barrier, NSEQ - 1 + 3)

    def zcopy(kind, block, way, step):
        to = lax.rem(z + 1, NZ) if way == 0 else lax.rem(z + NZ - 1, NZ)
        ref = zbuf.at[block, kind]
        return pltpu.make_async_remote_copy(
            src_ref=ref, dst_ref=ref,
            send_sem=zsend_sem.at[kind, way, step], recv_sem=zrecv_sem.at[kind, way, step],
            device_id=seq_dev(y, to),
        )

    def ring_step(kind, step):
        for way, block in ((0, lax.rem(z + NZ - step, NZ)), (1, lax.rem(z + step, NZ))):
            if step > 0 and not (way == 1 and step == 8):
                zcopy(kind, block, way, step - 1).wait_recv()
            if step < 8 - way:
                cp = zcopy(kind, block, way, step)
                cp.start()
                pending.append(cp)

    def send_to(src, dst, k, to):
        pltpu.make_async_remote_copy(
            src_ref=src.at[to], dst_ref=dst.at[s],
            send_sem=asend_sem.at[k], recv_sem=arecv_sem.at[k],
            device_id={"seq": to},
        ).start()

    def scatter(src, dst, k):
        each_peer(lambda to: send_to(src, dst, k, to))

    order = far + [(d, dy) for m in range(7, 0, -1) for dy in range(NY) for d in (m, NZ - m)] + beside

    def send_mid(lo, hi):
        for dz, dy in order[lo:hi]:
            send_to(msend, mrecv, 0, peer(dz, dy))

    def wait_scatter(ref, sem, k):
        part = ref.at[pl.ds(0, NSEQ - 1)]
        pltpu.make_async_copy(part, part, sem.at[k]).wait()

    def fill(zz, carry):
        lane = iota((224, QW), 0) - 96
        live = (lane >= 0) & (lane < 27)
        hit = live & (iota((224, QW), 1) == lane + 27 * zz)
        eq[zz] = jnp.where(hit, 1.0, 0.0).astype(bf16)
        lane = iota((224, OW), 0) - 96
        live = (lane >= 0) & (lane < 18)
        hit = live & (iota((224, OW), 1) == lane + 18 * zz + 32 * y)
        eo[zz] = jnp.where(hit, 1.0, 0.0).astype(bf16)
        return carry

    def own_norms(i, carry):
        rows = pl.ds(pl.multiple_of(i * 64, 64), 64)
        f, r = i // 2, pl.ds(pl.multiple_of((i % 2) * 64, 64), 64)
        nm_t[rows, :], rs_t[rows, :] = norm_stats(mid[f, r, :].astype(f32))
        nm_s[rows, :], rs_s[rows, :] = norm_stats(inp[f, r, :].astype(f32))
        return carry

    def live_cot(f):
        cell = iota((128, 1), 0) * 0 + (2 * s + f)
        return jnp.where(cell < frames[0], cot[f].astype(f32), 0.0)

    for step in range(8):
        ring_step(0, step)
        ring_step(1, step)
        send_mid(step, step + 1)
        lax.fori_loop(2 * step, 2 * step + 2, fill, 0)
        if step == 1:
            for cp in loads[5:]:
                cp.wait()
        if step in (2, 3):
            f = step - 2
            normin[f * 128:(f + 1) * 128, :] = (live_cot(f) * mod[5]).astype(bf16)
        if step > 3:
            lax.fori_loop(step - 4, step - 3, own_norms, 0)
    ring_step(0, 8)

    def unpack(kind, ref):
        whole = jnp.concatenate([zbuf[i, kind] for i in range(NZ)], 1)
        table = eo if ref is o_t or ref is o_s else eq

        def pick(g):
            lo = 96 - 32 * g
            return dot(whole, table[:, lo:lo + 128, :].reshape(NZ * 128, -1)).astype(bf16)

        if table is eo:
            ref[y, c, x] = jnp.concatenate([pick(2)[16:64], pick(3)[0:32]], 0)
        else:
            ref[y, c, x] = jnp.concatenate([pick(0), pick(1), pick(2)[0:16]], 0)

    jobs_t = [
        (0, o_t, "y", 0, 32, 16), (1, o_t, "x", 32, 48, 32),
        (2, q_t, "y", 0, 80, 48), (3, q_t, "x", 80, 64, 32),
    ]
    jobs_s = [
        (4, o_s, "y", 0, 32, 16), (5, o_s, "x", 32, 48, 32),
        (6, q_s, "y", 0, 80, 48), (7, q_s, "x", 80, 64, 32),
    ]

    def view(job, phase, rel, half, core):
        _, ref, first, r, n, m = job
        lo, size = {"all": (r, n), "a": (r, m), "b": (r + m, n - m)}[half]
        rows = pl.ds(lo, size)
        axis = first if phase == 0 else ("x" if first == "y" else "y")
        if axis == "x":
            return ref.at[y if phase == 0 else slice(None), core, (x + rel) % NX, rows]
        return ref.at[(y + rel) % NY, core, x if phase == 0 else slice(None), rows]

    def hop(job, phase, rel, half, way, slot):
        first = job[2]
        axis = first if phase == 0 else ("x" if first == "y" else "y")
        step = 1 if way == 0 else 3
        dev = x_dev((x + step) % NX) if axis == "x" else seq_dev((y + step) % NY, z)
        ref = view(job, phase, rel, half, c)
        return pltpu.make_async_remote_copy(
            src_ref=ref, dst_ref=ref,
            send_sem=jsend_sem.at[job[0], phase * 4 + slot],
            recv_sem=jrecv_sem.at[job[0], phase * 4 + slot],
            device_id=dev,
        )

    def go(cp):
        cp.start()
        pending.append(cp)

    def first_step(job, phase):
        go(hop(job, phase, 0, "all", 0, 0))
        go(hop(job, phase, 0, "all", 1, 1))

    def pass_on(job, phase):
        hop(job, phase, 3, "all", 0, 0).wait_recv()
        go(hop(job, phase, 3, "a", 0, 2))
        hop(job, phase, 1, "all", 1, 1).wait_recv()
        go(hop(job, phase, 1, "b", 1, 3))

    def last_step(job, phase):
        hop(job, phase, 2, "a", 0, 2).wait_recv()
        hop(job, phase, 2, "b", 1, 3).wait_recv()

    def share(job, rel, core):
        ref = view(job, 1, rel, "all", core)
        return pltpu.make_async_remote_copy(
            src_ref=ref, dst_ref=ref,
            send_sem=jsend_sem.at[job[0], 8 + rel], recv_sem=jrecv_sem.at[job[0], 8 + rel],
            device_id={"dp": x * 2 + other},
        )

    def share_wait(job):
        for rel in range(4):
            share(job, rel, other).wait_recv()

    def out_rows(o_ref, yy):
        return jnp.concatenate([o_ref[yy, d % 2, d // 2] for d in range(HEADS)], 0)

    def qkv_rows(q_ref, yy):
        return jnp.concatenate([q_ref[yy, d % 2, d // 2] for d in range(8)], 0)

    def out_back(gated, o_ref):
        total = None
        for yy in range(NY):
            term = dot(gated[:, 256 * yy:256 * yy + OW], out_rows(o_ref, yy), NT)
            total = term if total is None else total + term
        return total.astype(bf16)

    def open_second(job):
        last_step(job, 0)
        first_step(job, 1)
        go(share(job, 0, c))

    def on_second(job):
        pass_on(job, 1)
        go(share(job, 3, c))
        go(share(job, 1, c))

    def end_second(job):
        last_step(job, 1)
        go(share(job, 2, c))

    def each(f, jobs, *args):
        for job in jobs:
            f(job, *args)

    jobs_o, jobs_q = jobs_t[:2], jobs_t[2:]
    unpack(0, o_t)
    each(first_step, jobs_o, 0)
    unpack(0, q_t)
    each(first_step, jobs_q, 0)
    send_mid(8, 20)
    ring_step(1, 8)
    unpack(1, o_s)
    unpack(1, q_s)
    each(pass_on, jobs_o, 0)
    each(open_second, jobs_o)
    send_mid(20, 32)
    each(pass_on, jobs_q, 0)
    send_mid(32, 44)
    each(on_second, jobs_o)
    each(open_second, jobs_q)
    send_mid(44, 63)
    each(end_second, jobs_o)
    each(first_step, jobs_s, 0)

    each(share_wait, jobs_o)
    dout[...] = out_back(normin, o_t)
    for b in range(2):
        part = dot(back[128 * b:128 * b + 128, :], dout[...])
        dsend[b] = part.astype(bf16).reshape(NSEQ, 2, HEADS * HP)
        scatter(dsend.at[b], drecv.at[b], 1 + b)
        drecv[b, s] = dsend[b, s]
    mrecv[s] = msend[s]
    each(on_second, jobs_q)
    each(end_second, jobs_q)

    def project(q_ref, lo, n):
        def body(yy, carry):
            lanes = pl.ds(pl.multiple_of(yy * QW, QW), QW)
            qkv[lo:lo + n, lanes] = dot(normin[lo:lo + n, :], qkv_rows(q_ref, yy)).astype(bf16)
            return carry
        lax.fori_loop(0, NY, body, 0)

    def project_back(q_ref, lo, n):
        acc[lo:lo + n, :] = jnp.zeros((n, D), f32)

        def body(yy, carry):
            lanes = pl.ds(pl.multiple_of(yy * QW, QW), QW)
            acc[lo:lo + n, :] += dot(dqkv[lo:lo + n, lanes], qkv_rows(q_ref, yy), NT)
            return carry
        lax.fori_loop(0, NY, body, 0)

    def attend(masked, lo=0, hi=2):
        def body(b, carry):
            rows = pl.ds(pl.multiple_of(b * 128, 128), 128)
            for h in range(HEADS):
                q = qkv[rows, head_at(h):head_at(h) + HDIM]
                k = qkv[rows, head_at(8 + h):head_at(8 + h) + HDIM]
                scores = dot(k, q, NT) * HDIM ** -0.5
                if masked:
                    scores = jnp.where(iota((128, 128), 0) < frames[0], scores, -1e30)
                e = jnp.exp(scores - jnp.max(scores, 0, keepdims=True))
                probs[b * HEADS + h] = e / jnp.sum(e, 0, keepdims=True)
            return carry
        lax.fori_loop(lo, hi, body, 0)

    def attend_back(lo, hi):
        def body(b, carry):
            rows = pl.ds(pl.multiple_of(b * 128, 128), 128)
            for h in range(HEADS):
                q = qkv[rows, head_at(h):head_at(h) + HDIM]
                k = qkv[rows, head_at(8 + h):head_at(8 + h) + HDIM]
                v = qkv[rows, head_at(16 + h):head_at(16 + h) + HDIM]
                up = dout[rows, HP * h:HP * h + HDIM]
                p = probs[b * HEADS + h]
                dv = dot(p.astype(bf16), up)
                dp_ = dot(v, up, NT)
                delta = jnp.sum(p * dp_, 0, keepdims=True)
                ds = (p * (dp_ - delta)).astype(bf16)
                dq = dot(ds, k, TN) * HDIM ** -0.5
                dk = dot(ds, q) * HDIM ** -0.5
                dqkv[rows, head_at(h):head_at(h) + HDIM] = dq.astype(bf16)
                dqkv[rows, head_at(8 + h):head_at(8 + h) + HDIM] = dk.astype(bf16)
                dqkv[rows, head_at(16 + h):head_at(16 + h) + HDIM] = dv.astype(bf16)
            return carry
        lax.fori_loop(lo, hi, body, 0)

    wait_scatter(mrecv, arecv_sem, 0)
    acc[...] = dot(pr[...], mrecv[...].reshape(TOK, D))

    def patch_norm(i, carry):
        rows = pl.ds(pl.multiple_of(i * 64, 64), 64)
        normed, _ = norm_stats(acc[rows, :])
        normin[rows, :] = (normed * (1.0 + mod[4]) + mod[3]).astype(bf16)
        return carry
    lax.fori_loop(0, 4, patch_norm, 0)
    each(pass_on, jobs_s, 0)
    each(open_second, jobs_s)
    each(share_wait, jobs_q)
    for b in range(2):
        project(q_t, 128 * b, 128)
        attend(True, b, b + 1)
        wait_scatter(drecv.at[b], arecv_sem, 1 + b)
        dout[128 * b:128 * b + 128, :] = drecv[b].reshape(128, HEADS * HP)
        attend_back(b, b + 1)
        project_back(q_t, 128 * b, 128)
        rsend[b] = acc[128 * b:128 * b + 128, :].astype(bf16).reshape(NSEQ, 2, D)
        scatter(rsend.at[b], rrecv.at[b], 3 + b)
        rrecv[b, s] = rsend[b, s]
        if b == 0:
            each(on_second, jobs_s)

    each(end_second, jobs_s)

    def frame_norm(i, carry):
        rows = pl.ds(pl.multiple_of(i * 64, 64), 64)
        normin[rows, :] = (nm_s[rows, :] * (1.0 + mod[1]) + mod[0]).astype(bf16)
        return carry
    lax.fori_loop(0, 4, frame_norm, 0)
    each(share_wait, jobs_s)
    project(q_s, 0, TOK)
    attend(False)

    wait_scatter(rrecv.at[0], arecv_sem, 3)
    acc[...] = dot(back[:, 0:128], rrecv[0].reshape(128, D))
    wait_scatter(rrecv.at[1], arecv_sem, 4)
    acc[...] += dot(back[:, 128:256], rrecv[1].reshape(128, D))

    def mid_grad(i, carry):
        rows = pl.ds(pl.multiple_of(i * 64, 64), 64)
        f, r = i // 2, pl.ds(pl.multiple_of((i % 2) * 64, 64), 64)
        cell = iota((64, 1), 0) * 0 + (2 * s + f)
        masked = jnp.where(cell < frames[0], cot[f, r, :].astype(f32), 0.0)
        grad = masked + norm_back(acc[rows, :], nm_t[rows, :], rs_t[rows, :], 1.0 + mod[4])
        dmid[rows, :] = grad
        normin[rows, :] = (grad * mod[2]).astype(bf16)
        return carry
    lax.fori_loop(0, 4, mid_grad, 0)
    dout[...] = out_back(normin, o_s)
    attend_back(0, 2)
    project_back(q_s, 0, TOK)

    def last_grad(i, carry):
        rows = pl.ds(pl.multiple_of(i * 64, 64), 64)
        f, r = i // 2, pl.ds(pl.multiple_of((i % 2) * 64, 64), 64)
        dnorm = acc[rows, :].astype(bf16).astype(f32)
        grad = norm_back(dnorm, nm_s[rows, :], rs_s[rows, :], 1.0 + mod[1])
        result[f, r, :] = (dmid[rows, :] + grad).astype(bf16)
        return carry
    lax.fori_loop(0, 4, last_grad, 0)

    for cp in pending:
        cp.wait_send()
    wait_scatter(msend, asend_sem, 0)
    for b in range(2):
        wait_scatter(dsend.at[b], asend_sem, 1 + b)
        wait_scatter(rsend.at[b], asend_sem, 3 + b)


def per_device(inputs, mid_inputs, cotangent, modulation, frames, qkv_s, out_s, qkv_t, out_t):
    vmem, hbm = pl.BlockSpec(memory_space=pltpu.VMEM), pl.BlockSpec(memory_space=pltpu.HBM)
    dma = pltpu.SemaphoreType.DMA
    out = pl.pallas_call(
        kernel,
        out_shape=jax.ShapeDtypeStruct((2, 128, D), bf16),
        in_specs=[hbm] * 4 + [pl.BlockSpec(memory_space=pltpu.SMEM)] + [hbm] * 4,
        out_specs=vmem,
        scratch_shapes=[
            pltpu.VMEM((2, 128, D), bf16),
            pltpu.VMEM((2, 128, D), bf16),
            pltpu.VMEM((2, 128, D), bf16),
            pltpu.VMEM((6, 1, D), f32),
            pltpu.VMEM((27, 144), bf16),
            pltpu.VMEM((18, 72), bf16),
            pltpu.VMEM((27, 144), bf16),
            pltpu.VMEM((18, 72), bf16),
            dma((8,)),
            pltpu.VMEM((NZ, 2, 64, 128), bf16),
            pltpu.VMEM((NZ, 224, QW), bf16),
            pltpu.VMEM((NZ, 224, OW), bf16),
            pltpu.VMEM((NY, 2, NX, 144, QW), bf16),
            pltpu.VMEM((NY, 2, NX, HP, OW), bf16),
            pltpu.VMEM((NY, 2, NX, 144, QW), bf16),
            pltpu.VMEM((NY, 2, NX, HP, OW), bf16),
            pltpu.VMEM((NSEQ, 4, D), bf16),
            pltpu.VMEM((NSEQ, 4, D), bf16),
            pltpu.VMEM((2, NSEQ, 2, HEADS * HP), bf16),
            pltpu.VMEM((2, NSEQ, 2, HEADS * HP), bf16),
            pltpu.VMEM((2, NSEQ, 2, D), bf16),
            pltpu.VMEM((2, NSEQ, 2, D), bf16),
            pltpu.VMEM((TOK, TOK), bf16),
            pltpu.VMEM((TOK, TOK), bf16),
            pltpu.VMEM((TOK, TOK), bf16),
            pltpu.VMEM((TOK, D), bf16),
            pltpu.VMEM((TOK, NY * QW), bf16),
            pltpu.VMEM((TOK, NY * QW), bf16),
            pltpu.VMEM((TOK, HEADS * HP), bf16),
            pltpu.VMEM((2 * HEADS, 128, 128), f32),
            pltpu.VMEM((TOK, D), f32),
            pltpu.VMEM((TOK, D), f32),
            pltpu.VMEM((TOK, 1), f32),
            pltpu.VMEM((TOK, D), f32),
            pltpu.VMEM((TOK, 1), f32),
            pltpu.VMEM((TOK, D), f32),
            dma((2, 2, 8)), dma((2, 2, 8)), dma((8, 12)), dma((8, 12)), dma((5,)), dma((5,)),
        ],
        compiler_params=pltpu.CompilerParams(
            collective_id=0, has_side_effects=True, vmem_limit_bytes=56 * 1024 * 1024
        ),
        name="blocks_grad",
    )(
        inputs[0], mid_inputs[0], cotangent[0], modulation.reshape(6, 1, D), frames,
        qkv_s.T, out_s.T, qkv_t.T, out_t.T,
    )
    return out[None]


def solution(mesh):
    big = P("dp", "seq", None, None)
    weight = P("dp", "seq")
    return jax.shard_map(
        per_device,
        mesh=mesh,
        in_specs=(big, big, big, P("dp", None, None), P("dp")) + (weight,) * 4,
        out_specs=big,
        check_vma=False,
    )
```

```python
import jax
import jax.numpy as jnp
from jax import lax
from jax.experimental import pallas as pl
from jax.experimental.pallas import tpu as pltpu
from jax.sharding import PartitionSpec as P

HDIM = 72
HEADS = 8
D = 1152
EPS = 1e-06
TOK = 256
NY, NX, NZ = 4, 4, 16
NSEQ = NY * NZ
QW = 512
OW = 384
HP = 80
f32, bf16 = jnp.float32, jnp.bfloat16

NN = (((1,), (0,)), ((), ()))
NT = (((1,), (1,)), ((), ()))
TN = (((0,), (0,)), ((), ()))


def dot(a, b, dims=NN):
    return lax.dot_general(a, b, dims, preferred_element_type=f32)


def iota(shape, axis):
    return lax.broadcasted_iota(jnp.int32, shape, axis)


def head_at(n):
    return (n // 6) * QW + (n % 6) * HDIM


def norm_stats(x):
    center = jnp.mean(x, -1, keepdims=True)
    diff = x - center
    spread = jnp.mean(diff * diff, -1, keepdims=True)
    rstd = lax.rsqrt(spread + EPS)
    return diff * rstd, rstd


def norm_back(dnorm, normed, rstd, gain):
    g = dnorm * gain
    return rstd * (
        g
        - jnp.mean(g, -1, keepdims=True)
        - normed * jnp.mean(g * normed, -1, keepdims=True)
    )


def kernel(
    inp_hbm, mid_hbm, cot_hbm, mod_hbm, frames, qkv_s_hbm, out_s_hbm, qkv_t_hbm, out_t_hbm, result,
    inp, mid, cot, mod, qkv_s, out_s, qkv_t, out_t, load_sem,
    zbuf, eq, eo, q_t, o_t, q_s, o_s,
    msend, mrecv, dsend, drecv, rsend, rrecv,
    pm, pr, back, normin, qkv, dqkv, dout, probs, acc, nm_t, rs_t, nm_s, rs_s, dmid,
    zsend_sem, zrecv_sem, jsend_sem, jrecv_sem, asend_sem, arecv_sem,
):
    dp = lax.axis_index("dp")
    s = lax.axis_index("seq")
    x, c = dp // 2, dp % 2
    y, z = s // NZ, s % NZ
    other = 1 - c
    pending = []

    loads = [
        pltpu.make_async_copy(src, dst, load_sem.at[i])
        for i, (src, dst) in enumerate((
            (qkv_t_hbm, qkv_t), (out_t_hbm, out_t), (qkv_s_hbm, qkv_s), (out_s_hbm, out_s),
            (mid_hbm, mid), (cot_hbm, cot), (mod_hbm, mod), (inp_hbm, inp),
        ))
    ]
    for cp in loads:
        cp.start()

    def seq_dev(yy, zz):
        return {"seq": yy * NZ + zz}

    def x_dev(xx):
        return {"dp": xx * 2 + c}

    far = [(8, dy) for dy in range(NY)]
    near = [(dz, dy) for dy in range(NY) for dz in (0, 1)]
    beside = [(0, dy) for dy in range(1, NY)]

    def peer(dz, dy):
        return lax.rem(y + dy, NY) * NZ + lax.rem(z + dz, NZ)

    def each_peer(f):
        for dz, dy in far:
            f(peer(dz, dy))

        def body(i, carry):
            at = (lax.rem(z + 7 - i, NZ), lax.rem(z + NZ - 7 + i, NZ))
            for way, dy in near:
                f(lax.rem(y + dy, NY) * NZ + at[way])
            return carry
        lax.fori_loop(0, 7, body, 0)
        for dz, dy in beside:
            f(peer(dz, dy))

    barrier = pltpu.get_barrier_semaphore()

    for xx in ((x + 1) % NX, (x + 3) % NX):
        pl.semaphore_signal(barrier, inc=1, device_id=x_dev(xx))
    pl.semaphore_signal(barrier, inc=1, device_id={"dp": x * 2 + other})
    each_peer(lambda to: pl.semaphore_signal(barrier, inc=1, device_id={"seq": to}))

    def pack(qkv_ref, out_ref):
        q, o = qkv_ref[...], out_ref[...]

        def place(rows, g):
            hit = iota((rows, 128), 1) == iota((rows, 128), 0) + 32 * g
            return jnp.where(hit, 1.0, 0.0).astype(bf16)

        q0 = dot(q, place(27, 0), TN)[0:64]
        q1 = dot(q, place(27, 1), TN)[64:128]
        q2 = dot(q, place(27, 2), TN)[128:144]
        o2 = dot(o, place(18, 2), TN)[0:48]
        o3 = dot(o, place(18, 3), TN)[48:72]
        full = q0 + q1 + jnp.concatenate([q2, o2], 0)
        full = full + jnp.concatenate([o3, jnp.zeros((40, 128), f32)], 0)
        return full.astype(bf16)

    for cp in loads[:4]:
        cp.wait()
    zbuf[z, 0] = pack(qkv_t, out_t)
    zbuf[z, 1] = pack(qkv_s, out_s)

    ri, ci = iota((TOK, TOK), 0), iota((TOK, TOK), 1)
    pm[...] = jnp.where(ci == (ri & 1) * 128 + (ri >> 2) * 2 + ((ri >> 1) & 1), 1.0, 0.0).astype(bf16)
    pr[...] = jnp.where(
        ci == ((ri & 127) >> 1) * 4 + (ri >> 7) * 2 + (ri & 1), 1.0, 0.0
    ).astype(bf16)

    back[...] = jnp.where(
        ci == (ri & 1) * 128 + ((ri & 127) >> 1) * 2 + (ri >> 7), 1.0, 0.0
    ).astype(bf16)
    dqkv[...] = jnp.zeros((TOK, NY * QW), bf16)
    loads[4].wait()
    msend[...] = dot(pm[...], mid[...].reshape(TOK, D)).astype(bf16).reshape(NSEQ, 4, D)

    pl.semaphore_wait(barrier, NSEQ - 1 + 3)

    def zcopy(kind, block, way, step):
        to = lax.rem(z + 1, NZ) if way == 0 else lax.rem(z + NZ - 1, NZ)
        ref = zbuf.at[block, kind]
        return pltpu.make_async_remote_copy(
            src_ref=ref, dst_ref=ref,
            send_sem=zsend_sem.at[kind, way, step], recv_sem=zrecv_sem.at[kind, way, step],
            device_id=seq_dev(y, to),
        )

    def ring_step(kind, step):
        for way, block in ((0, lax.rem(z + NZ - step, NZ)), (1, lax.rem(z + step, NZ))):
            if step > 0 and not (way == 1 and step == 8):
                zcopy(kind, block, way, step - 1).wait_recv()
            if step < 8 - way:
                cp = zcopy(kind, block, way, step)
                cp.start()
                pending.append(cp)

    def send_to(src, dst, k, to):
        pltpu.make_async_remote_copy(
            src_ref=src.at[to], dst_ref=dst.at[s],
            send_sem=asend_sem.at[k], recv_sem=arecv_sem.at[k],
            device_id={"seq": to},
        ).start()

    def scatter(src, dst, k):
        each_peer(lambda to: send_to(src, dst, k, to))

    order = far + [(d, dy) for m in range(7, 0, -1) for dy in range(NY) for d in (m, NZ - m)] + beside

    def send_mid(lo, hi):
        for dz, dy in order[lo:hi]:
            send_to(msend, mrecv, 0, peer(dz, dy))

    def wait_scatter(ref, sem, k):
        part = ref.at[pl.ds(0, NSEQ - 1)]
        pltpu.make_async_copy(part, part, sem.at[k]).wait()

    def fill(zz, carry):
        lane = iota((224, QW), 0) - 96
        live = (lane >= 0) & (lane < 27)
        hit = live & (iota((224, QW), 1) == lane + 27 * zz)
        eq[zz] = jnp.where(hit, 1.0, 0.0).astype(bf16)
        lane = iota((224, OW), 0) - 96
        live = (lane >= 0) & (lane < 18)
        hit = live & (iota((224, OW), 1) == lane + 18 * zz + 32 * y)
        eo[zz] = jnp.where(hit, 1.0, 0.0).astype(bf16)
        return carry

    def own_norms(i, carry):
        rows = pl.ds(pl.multiple_of(i * 64, 64), 64)
        f, r = i // 2, pl.ds(pl.multiple_of((i % 2) * 64, 64), 64)
        nm_t[rows, :], rs_t[rows, :] = norm_stats(mid[f, r, :].astype(f32))
        nm_s[rows, :], rs_s[rows, :] = norm_stats(inp[f, r, :].astype(f32))
        return carry

    def live_cot(f):
        cell = iota((128, 1), 0) * 0 + (2 * s + f)
        return jnp.where(cell < frames[0], cot[f].astype(f32), 0.0)

    for step in range(8):
        ring_step(0, step)
        ring_step(1, step)
        send_mid(3 * step, 3 * step + 3)
        lax.fori_loop(2 * step, 2 * step + 2, fill, 0)
        if step == 1:
            for cp in loads[5:]:
                cp.wait()
        if step in (2, 3):
            f = step - 2
            normin[f * 128:(f + 1) * 128, :] = (live_cot(f) * mod[5]).astype(bf16)
        if step > 3:
            lax.fori_loop(step - 4, step - 3, own_norms, 0)
    ring_step(0, 8)

    def unpack(kind, ref):
        whole = jnp.concatenate([zbuf[i, kind] for i in range(NZ)], 1)
        table = eo if ref is o_t or ref is o_s else eq

        def pick(g):
            lo = 96 - 32 * g
            return dot(whole, table[:, lo:lo + 128, :].reshape(NZ * 128, -1)).astype(bf16)

        if table is eo:
            ref[y, c, x] = jnp.concatenate([pick(2)[16:64], pick(3)[0:32]], 0)
        else:
            ref[y, c, x] = jnp.concatenate([pick(0), pick(1), pick(2)[0:16]], 0)

    jobs_t = [
        (0, o_t, "y", 0, 32, 16), (1, o_t, "x", 32, 48, 32),
        (2, q_t, "y", 0, 80, 48), (3, q_t, "x", 80, 64, 32),
    ]
    jobs_s = [
        (4, o_s, "y", 0, 32, 16), (5, o_s, "x", 32, 48, 32),
        (6, q_s, "y", 0, 80, 48), (7, q_s, "x", 80, 64, 32),
    ]

    def view(job, phase, rel, half, core):
        _, ref, first, r, n, m = job
        lo, size = {"all": (r, n), "a": (r, m), "b": (r + m, n - m)}[half]
        rows = pl.ds(lo, size)
        axis = first if phase == 0 else ("x" if first == "y" else "y")
        if axis == "x":
            return ref.at[y if phase == 0 else slice(None), core, (x + rel) % NX, rows]
        return ref.at[(y + rel) % NY, core, x if phase == 0 else slice(None), rows]

    def hop(job, phase, rel, half, way, slot):
        first = job[2]
        axis = first if phase == 0 else ("x" if first == "y" else "y")
        step = 1 if way == 0 else 3
        dev = x_dev((x + step) % NX) if axis == "x" else seq_dev((y + step) % NY, z)
        ref = view(job, phase, rel, half, c)
        return pltpu.make_async_remote_copy(
            src_ref=ref, dst_ref=ref,
            send_sem=jsend_sem.at[job[0], phase * 4 + slot],
            recv_sem=jrecv_sem.at[job[0], phase * 4 + slot],
            device_id=dev,
        )

    def go(cp):
        cp.start()
        pending.append(cp)

    def first_step(job, phase):
        go(hop(job, phase, 0, "all", 0, 0))
        go(hop(job, phase, 0, "all", 1, 1))

    def pass_on(job, phase):
        hop(job, phase, 3, "all", 0, 0).wait_recv()
        go(hop(job, phase, 3, "a", 0, 2))
        hop(job, phase, 1, "all", 1, 1).wait_recv()
        go(hop(job, phase, 1, "b", 1, 3))

    def last_step(job, phase):
        hop(job, phase, 2, "a", 0, 2).wait_recv()
        hop(job, phase, 2, "b", 1, 3).wait_recv()

    def share(job, rel, core):
        ref = view(job, 1, rel, "all", core)
        return pltpu.make_async_remote_copy(
            src_ref=ref, dst_ref=ref,
            send_sem=jsend_sem.at[job[0], 8 + rel], recv_sem=jrecv_sem.at[job[0], 8 + rel],
            device_id={"dp": x * 2 + other},
        )

    def share_wait(job):
        for rel in range(4):
            share(job, rel, other).wait_recv()

    def out_rows(o_ref, yy):
        return jnp.concatenate([o_ref[yy, d % 2, d // 2] for d in range(HEADS)], 0)

    def qkv_rows(q_ref, yy):
        return jnp.concatenate([q_ref[yy, d % 2, d // 2] for d in range(8)], 0)

    def out_back(gated, o_ref):
        total = None
        for yy in range(NY):
            term = dot(gated[:, 256 * yy:256 * yy + OW], out_rows(o_ref, yy), NT)
            total = term if total is None else total + term
        return total.astype(bf16)

    def open_second(job):
        last_step(job, 0)
        first_step(job, 1)
        go(share(job, 0, c))

    def on_second(job):
        pass_on(job, 1)
        go(share(job, 3, c))
        go(share(job, 1, c))

    def end_second(job):
        last_step(job, 1)
        go(share(job, 2, c))

    def each(f, jobs, *args):
        for job in jobs:
            f(job, *args)

    jobs_o, jobs_q = jobs_t[:2], jobs_t[2:]
    unpack(0, o_t)
    each(first_step, jobs_o, 0)
    unpack(0, q_t)
    each(first_step, jobs_q, 0)
    send_mid(24, 40)
    ring_step(1, 8)
    unpack(1, o_s)
    unpack(1, q_s)
    each(pass_on, jobs_o, 0)
    each(open_second, jobs_o)
    send_mid(40, 54)
    each(pass_on, jobs_q, 0)
    send_mid(54, 63)
    each(on_second, jobs_o)
    each(open_second, jobs_q)
    each(end_second, jobs_o)
    each(first_step, jobs_s, 0)

    each(share_wait, jobs_o)
    dout[...] = out_back(normin, o_t)
    for b in range(2):
        part = dot(back[128 * b:128 * b + 128, :], dout[...])
        dsend[b] = part.astype(bf16).reshape(NSEQ, 2, HEADS * HP)
        scatter(dsend.at[b], drecv.at[b], 1 + b)
        drecv[b, s] = dsend[b, s]
    mrecv[s] = msend[s]
    each(on_second, jobs_q)
    each(end_second, jobs_q)

    def project(q_ref, lo, n):
        def body(yy, carry):
            lanes = pl.ds(pl.multiple_of(yy * QW, QW), QW)
            qkv[lo:lo + n, lanes] = dot(normin[lo:lo + n, :], qkv_rows(q_ref, yy)).astype(bf16)
            return carry
        lax.fori_loop(0, NY, body, 0)

    def project_back(q_ref, lo, n):
        acc[lo:lo + n, :] = jnp.zeros((n, D), f32)

        def body(yy, carry):
            lanes = pl.ds(pl.multiple_of(yy * QW, QW), QW)
            acc[lo:lo + n, :] += dot(dqkv[lo:lo + n, lanes], qkv_rows(q_ref, yy), NT)
            return carry
        lax.fori_loop(0, NY, body, 0)

    def attend(masked, lo=0, hi=2):
        def body(b, carry):
            rows = pl.ds(pl.multiple_of(b * 128, 128), 128)
            for h in range(HEADS):
                q = qkv[rows, head_at(h):head_at(h) + HDIM]
                k = qkv[rows, head_at(8 + h):head_at(8 + h) + HDIM]
                scores = dot(k, q, NT) * HDIM ** -0.5
                if masked:
                    scores = jnp.where(iota((128, 128), 0) < frames[0], scores, -1e30)
                e = jnp.exp(scores - jnp.max(scores, 0, keepdims=True))
                probs[b * HEADS + h] = e / jnp.sum(e, 0, keepdims=True)
            return carry
        lax.fori_loop(lo, hi, body, 0)

    def attend_back(lo, hi):
        def body(b, carry):
            rows = pl.ds(pl.multiple_of(b * 128, 128), 128)
            for h in range(HEADS):
                q = qkv[rows, head_at(h):head_at(h) + HDIM]
                k = qkv[rows, head_at(8 + h):head_at(8 + h) + HDIM]
                v = qkv[rows, head_at(16 + h):head_at(16 + h) + HDIM]
                up = dout[rows, HP * h:HP * h + HDIM]
                p = probs[b * HEADS + h]
                dv = dot(p.astype(bf16), up)
                dp_ = dot(v, up, NT)
                delta = jnp.sum(p * dp_, 0, keepdims=True)
                ds = (p * (dp_ - delta)).astype(bf16)
                dq = dot(ds, k, TN) * HDIM ** -0.5
                dk = dot(ds, q) * HDIM ** -0.5
                dqkv[rows, head_at(h):head_at(h) + HDIM] = dq.astype(bf16)
                dqkv[rows, head_at(8 + h):head_at(8 + h) + HDIM] = dk.astype(bf16)
                dqkv[rows, head_at(16 + h):head_at(16 + h) + HDIM] = dv.astype(bf16)
            return carry
        lax.fori_loop(lo, hi, body, 0)

    wait_scatter(mrecv, arecv_sem, 0)
    acc[...] = dot(pr[...], mrecv[...].reshape(TOK, D))

    def patch_norm(i, carry):
        rows = pl.ds(pl.multiple_of(i * 64, 64), 64)
        normed, _ = norm_stats(acc[rows, :])
        normin[rows, :] = (normed * (1.0 + mod[4]) + mod[3]).astype(bf16)
        return carry
    lax.fori_loop(0, 4, patch_norm, 0)
    each(pass_on, jobs_s, 0)
    each(open_second, jobs_s)
    each(share_wait, jobs_q)
    for b in range(2):
        project(q_t, 128 * b, 128)
        attend(True, b, b + 1)
        wait_scatter(drecv.at[b], arecv_sem, 1 + b)
        dout[128 * b:128 * b + 128, :] = drecv[b].reshape(128, HEADS * HP)
        attend_back(b, b + 1)
        project_back(q_t, 128 * b, 128)
        rsend[b] = acc[128 * b:128 * b + 128, :].astype(bf16).reshape(NSEQ, 2, D)
        scatter(rsend.at[b], rrecv.at[b], 3 + b)
        rrecv[b, s] = rsend[b, s]
        if b == 0:
            each(on_second, jobs_s)

    each(end_second, jobs_s)

    def frame_norm(i, carry):
        rows = pl.ds(pl.multiple_of(i * 64, 64), 64)
        normin[rows, :] = (nm_s[rows, :] * (1.0 + mod[1]) + mod[0]).astype(bf16)
        return carry
    lax.fori_loop(0, 4, frame_norm, 0)
    each(share_wait, jobs_s)
    project(q_s, 0, TOK)
    attend(False)

    wait_scatter(rrecv.at[0], arecv_sem, 3)
    acc[...] = dot(back[:, 0:128], rrecv[0].reshape(128, D))
    wait_scatter(rrecv.at[1], arecv_sem, 4)
    acc[...] += dot(back[:, 128:256], rrecv[1].reshape(128, D))

    def mid_grad(i, carry):
        rows = pl.ds(pl.multiple_of(i * 64, 64), 64)
        f, r = i // 2, pl.ds(pl.multiple_of((i % 2) * 64, 64), 64)
        cell = iota((64, 1), 0) * 0 + (2 * s + f)
        masked = jnp.where(cell < frames[0], cot[f, r, :].astype(f32), 0.0)
        grad = masked + norm_back(acc[rows, :], nm_t[rows, :], rs_t[rows, :], 1.0 + mod[4])
        dmid[rows, :] = grad
        normin[rows, :] = (grad * mod[2]).astype(bf16)
        return carry
    lax.fori_loop(0, 4, mid_grad, 0)
    dout[...] = out_back(normin, o_s)
    attend_back(0, 2)
    project_back(q_s, 0, TOK)

    def last_grad(i, carry):
        rows = pl.ds(pl.multiple_of(i * 64, 64), 64)
        f, r = i // 2, pl.ds(pl.multiple_of((i % 2) * 64, 64), 64)
        dnorm = acc[rows, :].astype(bf16).astype(f32)
        grad = norm_back(dnorm, nm_s[rows, :], rs_s[rows, :], 1.0 + mod[1])
        result[f, r, :] = (dmid[rows, :] + grad).astype(bf16)
        return carry
    lax.fori_loop(0, 4, last_grad, 0)

    for cp in pending:
        cp.wait_send()
    wait_scatter(msend, asend_sem, 0)
    for b in range(2):
        wait_scatter(dsend.at[b], asend_sem, 1 + b)
        wait_scatter(rsend.at[b], asend_sem, 3 + b)


def per_device(inputs, mid_inputs, cotangent, modulation, frames, qkv_s, out_s, qkv_t, out_t):
    vmem, hbm = pl.BlockSpec(memory_space=pltpu.VMEM), pl.BlockSpec(memory_space=pltpu.HBM)
    dma = pltpu.SemaphoreType.DMA
    out = pl.pallas_call(
        kernel,
        out_shape=jax.ShapeDtypeStruct((2, 128, D), bf16),
        in_specs=[hbm] * 4 + [pl.BlockSpec(memory_space=pltpu.SMEM)] + [hbm] * 4,
        out_specs=vmem,
        scratch_shapes=[
            pltpu.VMEM((2, 128, D), bf16),
            pltpu.VMEM((2, 128, D), bf16),
            pltpu.VMEM((2, 128, D), bf16),
            pltpu.VMEM((6, 1, D), f32),
            pltpu.VMEM((27, 144), bf16),
            pltpu.VMEM((18, 72), bf16),
            pltpu.VMEM((27, 144), bf16),
            pltpu.VMEM((18, 72), bf16),
            dma((8,)),
            pltpu.VMEM((NZ, 2, 64, 128), bf16),
            pltpu.VMEM((NZ, 224, QW), bf16),
            pltpu.VMEM((NZ, 224, OW), bf16),
            pltpu.VMEM((NY, 2, NX, 144, QW), bf16),
            pltpu.VMEM((NY, 2, NX, HP, OW), bf16),
            pltpu.VMEM((NY, 2, NX, 144, QW), bf16),
            pltpu.VMEM((NY, 2, NX, HP, OW), bf16),
            pltpu.VMEM((NSEQ, 4, D), bf16),
            pltpu.VMEM((NSEQ, 4, D), bf16),
            pltpu.VMEM((2, NSEQ, 2, HEADS * HP), bf16),
            pltpu.VMEM((2, NSEQ, 2, HEADS * HP), bf16),
            pltpu.VMEM((2, NSEQ, 2, D), bf16),
            pltpu.VMEM((2, NSEQ, 2, D), bf16),
            pltpu.VMEM((TOK, TOK), bf16),
            pltpu.VMEM((TOK, TOK), bf16),
            pltpu.VMEM((TOK, TOK), bf16),
            pltpu.VMEM((TOK, D), bf16),
            pltpu.VMEM((TOK, NY * QW), bf16),
            pltpu.VMEM((TOK, NY * QW), bf16),
            pltpu.VMEM((TOK, HEADS * HP), bf16),
            pltpu.VMEM((2 * HEADS, 128, 128), f32),
            pltpu.VMEM((TOK, D), f32),
            pltpu.VMEM((TOK, D), f32),
            pltpu.VMEM((TOK, 1), f32),
            pltpu.VMEM((TOK, D), f32),
            pltpu.VMEM((TOK, 1), f32),
            pltpu.VMEM((TOK, D), f32),
            dma((2, 2, 8)), dma((2, 2, 8)), dma((8, 12)), dma((8, 12)), dma((5,)), dma((5,)),
        ],
        compiler_params=pltpu.CompilerParams(
            collective_id=0, has_side_effects=True, vmem_limit_bytes=56 * 1024 * 1024
        ),
        name="blocks_grad",
    )(
        inputs[0], mid_inputs[0], cotangent[0], modulation.reshape(6, 1, D), frames,
        qkv_s.T, out_s.T, qkv_t.T, out_t.T,
    )
    return out[None]


def solution(mesh):
    big = P("dp", "seq", None, None)
    weight = P("dp", "seq")
    return jax.shard_map(
        per_device,
        mesh=mesh,
        in_specs=(big, big, big, P("dp", None, None), P("dp")) + (weight,) * 4,
        out_specs=big,
        check_vma=False,
    )
```

```python
import jax
import jax.numpy as jnp
from jax import lax
from jax.experimental import pallas as pl
from jax.experimental.pallas import tpu as pltpu
from jax.sharding import PartitionSpec as P

HDIM = 72
HEADS = 8
D = 1152
EPS = 1e-06
TOK = 256
NY, NX, NZ = 4, 4, 16
NSEQ = NY * NZ
QW = 512
OW = 384
HP = 80
f32, bf16 = jnp.float32, jnp.bfloat16

NN = (((1,), (0,)), ((), ()))
NT = (((1,), (1,)), ((), ()))
TN = (((0,), (0,)), ((), ()))


def dot(a, b, dims=NN):
    return lax.dot_general(a, b, dims, preferred_element_type=f32)


def iota(shape, axis):
    return lax.broadcasted_iota(jnp.int32, shape, axis)


def head_at(n):
    return (n // 6) * QW + (n % 6) * HDIM


def norm_stats(x):
    center = jnp.mean(x, -1, keepdims=True)
    diff = x - center
    spread = jnp.mean(diff * diff, -1, keepdims=True)
    rstd = lax.rsqrt(spread + EPS)
    return diff * rstd, rstd


def norm_back(dnorm, normed, rstd, gain):
    g = dnorm * gain
    return rstd * (
        g
        - jnp.mean(g, -1, keepdims=True)
        - normed * jnp.mean(g * normed, -1, keepdims=True)
    )


def kernel(
    inp_hbm, mid_hbm, cot_hbm, mod_hbm, frames, qkv_s_hbm, out_s_hbm, qkv_t_hbm, out_t_hbm, result,
    inp, mid, cot, mod, qkv_s, out_s, qkv_t, out_t, load_sem,
    z_qt, z_s, z_ot, eq, eo, q_t, o_t, q_s, o_s,
    msend, mrecv, dsend, drecv, rsend, rrecv,
    pm, pr, back, normin, qkv, dqkv, dout, probs, acc, nm_t, rs_t, nm_s, rs_s, dmid,
    osem, zsend_sem, zrecv_sem, jsend_sem, jrecv_sem, asend_sem, arecv_sem,
):
    dp = lax.axis_index("dp")
    s = lax.axis_index("seq")
    x, c = dp // 2, dp % 2
    y, z = s // NZ, s % NZ
    other = 1 - c
    pending = []

    loads = [
        pltpu.make_async_copy(src, dst, load_sem.at[i])
        for i, (src, dst) in enumerate((
            (qkv_t_hbm, qkv_t), (out_t_hbm, out_t), (qkv_s_hbm, qkv_s), (out_s_hbm, out_s),
            (mid_hbm, mid), (cot_hbm, cot), (mod_hbm, mod), (inp_hbm, inp),
        ))
    ]
    for cp in loads:
        cp.start()

    def seq_dev(yy, zz):
        return {"seq": yy * NZ + zz}

    def x_dev(xx):
        return {"dp": xx * 2 + c}

    far = [(8, dy) for dy in range(NY)]
    near = [(dz, dy) for dy in range(NY) for dz in (0, 1)]
    beside = [(0, dy) for dy in range(1, NY)]

    def peer(dz, dy):
        return lax.rem(y + dy, NY) * NZ + lax.rem(z + dz, NZ)

    def each_peer(f):
        for dz, dy in far:
            f(peer(dz, dy))

        def body(i, carry):
            at = (lax.rem(z + 7 - i, NZ), lax.rem(z + NZ - 7 + i, NZ))
            for way, dy in near:
                f(lax.rem(y + dy, NY) * NZ + at[way])
            return carry
        lax.fori_loop(0, 7, body, 0)
        for dz, dy in beside:
            f(peer(dz, dy))

    barrier = pltpu.get_barrier_semaphore()

    for xx in ((x + 1) % NX, (x + 3) % NX):
        pl.semaphore_signal(barrier, inc=1, device_id=x_dev(xx))
    pl.semaphore_signal(barrier, inc=1, device_id={"dp": x * 2 + other})
    each_peer(lambda to: pl.semaphore_signal(barrier, inc=1, device_id={"seq": to}))

    def pack(ref, group, lanes):
        w = ref[...]
        n, rows = w.shape
        total = None
        for g in range(-(-rows // group)):
            hit = iota((n, 128), 1) == iota((n, 128), 0) + lanes * g
            part = dot(w, jnp.where(hit, 1.0, 0.0).astype(bf16), TN)[group * g:group * (g + 1)]
            if part.shape[0] < group:
                part = jnp.concatenate([part, jnp.zeros((group - part.shape[0], 128), f32)], 0)
            total = part if total is None else total + part
        return total.astype(bf16)

    for cp in loads[:4]:
        cp.wait()
    z_ot[z] = pack(out_t, 16, 24)
    z_qt[z] = pack(qkv_t, 48, 32)
    z_s[z, 0:48] = pack(qkv_s, 48, 32)
    z_s[z, 48:64] = pack(out_s, 16, 24)

    ri, ci = iota((TOK, TOK), 0), iota((TOK, TOK), 1)
    pm[...] = jnp.where(ci == (ri & 1) * 128 + (ri >> 2) * 2 + ((ri >> 1) & 1), 1.0, 0.0).astype(bf16)
    pr[...] = jnp.where(
        ci == ((ri & 127) >> 1) * 4 + (ri >> 7) * 2 + (ri & 1), 1.0, 0.0
    ).astype(bf16)

    back[...] = jnp.where(
        ci == (ri & 1) * 128 + ((ri & 127) >> 1) * 2 + (ri >> 7), 1.0, 0.0
    ).astype(bf16)
    dqkv[...] = jnp.zeros((TOK, NY * QW), bf16)
    loads[4].wait()
    msend[...] = dot(pm[...], mid[...].reshape(TOK, D)).astype(bf16).reshape(NSEQ, 4, D)

    pl.semaphore_wait(barrier, NSEQ - 1 + 3)

    def zcopy(kind, block, way, step):
        to = lax.rem(z + 1, NZ) if way == 0 else lax.rem(z + NZ - 1, NZ)
        ref = (z_qt, z_s)[kind].at[block]
        return pltpu.make_async_remote_copy(
            src_ref=ref, dst_ref=ref,
            send_sem=zsend_sem.at[kind, way, step], recv_sem=zrecv_sem.at[kind, way, step],
            device_id=seq_dev(y, to),
        )

    def ring_step(kind, step):
        for way, block in ((0, lax.rem(z + NZ - step, NZ)), (1, lax.rem(z + step, NZ))):
            if step > 0 and not (way == 1 and step == 8):
                zcopy(kind, block, way, step - 1).wait_recv()
            if step < 8 - way:
                cp = zcopy(kind, block, way, step)
                cp.start()
                pending.append(cp)

    def send_to(src, dst, k, to):
        pltpu.make_async_remote_copy(
            src_ref=src.at[to], dst_ref=dst.at[s],
            send_sem=asend_sem.at[k], recv_sem=arecv_sem.at[k],
            device_id={"seq": to},
        ).start()

    def scatter(src, dst, k):
        each_peer(lambda to: send_to(src, dst, k, to))

    order = far + [(d, dy) for m in range(7, 0, -1) for dy in range(NY) for d in (m, NZ - m)] + beside

    def send_mid(lo, hi):
        for dz, dy in order[lo:hi]:
            send_to(msend, mrecv, 0, peer(dz, dy))

    def wait_scatter(ref, sem, k):
        part = ref.at[pl.ds(0, NSEQ - 1)]
        pltpu.make_async_copy(part, part, sem.at[k]).wait()

    def fill_q(zz, carry):
        lane, col = iota((128, QW), 0), iota((128, QW), 1)
        at = lane & 31
        hit = (at < 27) & (lane < 96) & (col == at + 27 * zz)
        eq[zz] = jnp.where(hit, 1.0, 0.0).astype(bf16)
        return carry

    def fill_o(zz, carry):
        lane, col = iota((128, OW), 0), iota((128, OW), 1)
        at = lane
        for g in range(1, 5):
            at = jnp.where(lane >= 24 * g, lane - 24 * g, at)
        hit = (at < 18) & (col == at + 18 * zz + 32 * y)
        eo[zz] = jnp.where(hit, 1.0, 0.0).astype(bf16)
        return carry

    def own_norms(i, carry):
        rows = pl.ds(pl.multiple_of(i * 64, 64), 64)
        f, r = i // 2, pl.ds(pl.multiple_of((i % 2) * 64, 64), 64)
        nm_t[rows, :], rs_t[rows, :] = norm_stats(mid[f, r, :].astype(f32))
        nm_s[rows, :], rs_s[rows, :] = norm_stats(inp[f, r, :].astype(f32))
        return carry

    def live_cot(f):
        cell = iota((128, 1), 0) * 0 + (2 * s + f)
        return jnp.where(cell < frames[0], cot[f].astype(f32), 0.0)

    def whole_of(ref, lo, hi):
        return jnp.concatenate([ref[i, lo:hi] for i in range(NZ)], 1)

    def unpack(whole, table, group, lanes, count):
        lane = iota(whole.shape, 1) & 127
        parts = []
        for g in range(count):
            live = (lane >= lanes * g) & (lane < lanes * (g + 1))
            parts.append(jnp.where(live, whole, jnp.zeros_like(whole)))
        lhs = jnp.concatenate(parts, 0)
        return dot(lhs, table[...].reshape(NZ * 128, -1)).astype(bf16)

    def unpack_q(whole):
        return unpack(whole, eq, 48, 32, 3)

    def unpack_o(whole):
        return unpack(whole, eo, 16, 24, 5)

    def o_to(to):
        pltpu.make_async_remote_copy(
            src_ref=z_ot.at[z], dst_ref=z_ot.at[z], send_sem=osem.at[0], recv_sem=osem.at[1],
            device_id=seq_dev(y, to),
        ).start()

    def o_wait(k):
        part = z_ot.at[pl.ds(0, NZ - 1)]
        pltpu.make_async_copy(part, part, osem.at[k]).wait()

    jobs_t = [
        (0, o_t, "y", 0, 32, 16), (1, o_t, "x", 32, 48, 32),
        (2, q_t, "y", 0, 80, 48), (3, q_t, "x", 80, 64, 32),
    ]
    jobs_s = [
        (4, o_s, "y", 0, 32, 16), (5, o_s, "x", 32, 48, 32),
        (6, q_s, "y", 0, 80, 48), (7, q_s, "x", 80, 64, 32),
    ]

    def view(job, phase, rel, half, core):
        _, ref, first, r, n, m = job
        lo, size = {"all": (r, n), "a": (r, m), "b": (r + m, n - m)}[half]
        rows = pl.ds(lo, size)
        axis = first if phase == 0 else ("x" if first == "y" else "y")
        if axis == "x":
            return ref.at[y if phase == 0 else slice(None), core, (x + rel) % NX, rows]
        return ref.at[(y + rel) % NY, core, x if phase == 0 else slice(None), rows]

    def hop(job, phase, rel, half, way, slot):
        first = job[2]
        axis = first if phase == 0 else ("x" if first == "y" else "y")
        step = 1 if way == 0 else 3
        dev = x_dev((x + step) % NX) if axis == "x" else seq_dev((y + step) % NY, z)
        ref = view(job, phase, rel, half, c)
        return pltpu.make_async_remote_copy(
            src_ref=ref, dst_ref=ref,
            send_sem=jsend_sem.at[job[0], phase * 4 + slot],
            recv_sem=jrecv_sem.at[job[0], phase * 4 + slot],
            device_id=dev,
        )

    def go(cp):
        cp.start()
        pending.append(cp)

    def first_step(job, phase):
        go(hop(job, phase, 0, "all", 0, 0))
        go(hop(job, phase, 0, "all", 1, 1))

    def pass_on(job, phase):
        hop(job, phase, 3, "all", 0, 0).wait_recv()
        go(hop(job, phase, 3, "a", 0, 2))
        hop(job, phase, 1, "all", 1, 1).wait_recv()
        go(hop(job, phase, 1, "b", 1, 3))

    def last_step(job, phase):
        hop(job, phase, 2, "a", 0, 2).wait_recv()
        hop(job, phase, 2, "b", 1, 3).wait_recv()

    def share(job, rel, core):
        ref = view(job, 1, rel, "all", core)
        return pltpu.make_async_remote_copy(
            src_ref=ref, dst_ref=ref,
            send_sem=jsend_sem.at[job[0], 8 + rel], recv_sem=jrecv_sem.at[job[0], 8 + rel],
            device_id={"dp": x * 2 + other},
        )

    def share_wait(job):
        for rel in range(4):
            share(job, rel, other).wait_recv()

    def out_rows(o_ref, yy):
        return jnp.concatenate([o_ref[yy, d % 2, d // 2] for d in range(HEADS)], 0)

    def qkv_rows(q_ref, yy):
        return jnp.concatenate([q_ref[yy, d % 2, d // 2] for d in range(8)], 0)

    def out_back(gated, o_ref):
        total = None
        for yy in range(NY):
            term = dot(gated[:, 256 * yy:256 * yy + OW], out_rows(o_ref, yy), NT)
            total = term if total is None else total + term
        return total.astype(bf16)

    def open_second(job):
        last_step(job, 0)
        first_step(job, 1)
        go(share(job, 0, c))

    def on_second(job):
        pass_on(job, 1)
        go(share(job, 3, c))
        go(share(job, 1, c))

    def end_second(job):
        last_step(job, 1)
        go(share(job, 2, c))

    def each(f, jobs, *args):
        for job in jobs:
            f(job, *args)

    jobs_o, jobs_q = jobs_t[:2], jobs_t[2:]

    for m in range(8, 0, -1):
        o_to(lax.rem(z + m, NZ))
        if m < 8:
            o_to(lax.rem(z + NZ - m, NZ))
    for step in range(8):
        ring_step(0, step)
        ring_step(1, step)
        send_mid(2 * step, 2 * step + 2)
        if step == 0:
            lax.fori_loop(0, NZ, fill_o, 0)
        else:
            lax.fori_loop(3 * step - 3, min(3 * step, NZ), fill_q, 0)
        if step == 1:
            for cp in loads[5:]:
                cp.wait()
        if step == 2:
            o_wait(1)
            o_t[y, c, x] = unpack_o(whole_of(z_ot, 0, 16))
            each(first_step, jobs_o, 0)
        if step in (3, 6):
            f = step // 3 - 1
            normin[f * 128:(f + 1) * 128, :] = (live_cot(f) * mod[5]).astype(bf16)
        if step == 4:
            each(pass_on, jobs_o, 0)
        if step == 5:
            each(open_second, jobs_o)
        if step == 7:
            each(on_second, jobs_o)
    ring_step(0, 8)
    q_t[y, c, x] = unpack_q(whole_of(z_qt, 0, 48))
    each(first_step, jobs_q, 0)
    send_mid(16, 63)
    each(end_second, jobs_o)

    each(share_wait, jobs_o)
    dout[...] = out_back(normin, o_t)
    for b in range(2):
        part = dot(back[128 * b:128 * b + 128, :], dout[...])
        dsend[b] = part.astype(bf16).reshape(NSEQ, 2, HEADS * HP)
        scatter(dsend.at[b], drecv.at[b], 1 + b)
        drecv[b, s] = dsend[b, s]
    mrecv[s] = msend[s]
    each(pass_on, jobs_q, 0)
    ring_step(1, 8)
    o_s[y, c, x] = unpack_o(whole_of(z_s, 48, 64))
    q_s[y, c, x] = unpack_q(whole_of(z_s, 0, 48))
    each(open_second, jobs_q)
    each(first_step, jobs_s, 0)
    lax.fori_loop(0, 4, own_norms, 0)
    each(on_second, jobs_q)
    each(end_second, jobs_q)

    def project(q_ref, lo, n):
        def body(yy, carry):
            lanes = pl.ds(pl.multiple_of(yy * QW, QW), QW)
            qkv[lo:lo + n, lanes] = dot(normin[lo:lo + n, :], qkv_rows(q_ref, yy)).astype(bf16)
            return carry
        lax.fori_loop(0, NY, body, 0)

    def project_back(q_ref, lo, n):
        acc[lo:lo + n, :] = jnp.zeros((n, D), f32)

        def body(yy, carry):
            lanes = pl.ds(pl.multiple_of(yy * QW, QW), QW)
            acc[lo:lo + n, :] += dot(dqkv[lo:lo + n, lanes], qkv_rows(q_ref, yy), NT)
            return carry
        lax.fori_loop(0, NY, body, 0)

    def attend(masked, lo=0, hi=2):
        def body(b, carry):
            rows = pl.ds(pl.multiple_of(b * 128, 128), 128)
            for h in range(HEADS):
                q = qkv[rows, head_at(h):head_at(h) + HDIM]
                k = qkv[rows, head_at(8 + h):head_at(8 + h) + HDIM]
                scores = dot(k, q, NT) * HDIM ** -0.5
                if masked:
                    scores = jnp.where(iota((128, 128), 0) < frames[0], scores, -1e30)
                e = jnp.exp(scores - jnp.max(scores, 0, keepdims=True))
                probs[b * HEADS + h] = e / jnp.sum(e, 0, keepdims=True)
            return carry
        lax.fori_loop(lo, hi, body, 0)

    def attend_back(lo, hi):
        def body(b, carry):
            rows = pl.ds(pl.multiple_of(b * 128, 128), 128)
            for h in range(HEADS):
                q = qkv[rows, head_at(h):head_at(h) + HDIM]
                k = qkv[rows, head_at(8 + h):head_at(8 + h) + HDIM]
                v = qkv[rows, head_at(16 + h):head_at(16 + h) + HDIM]
                up = dout[rows, HP * h:HP * h + HDIM]
                p = probs[b * HEADS + h]
                dv = dot(p.astype(bf16), up)
                dp_ = dot(v, up, NT)
                delta = jnp.sum(p * dp_, 0, keepdims=True)
                ds = (p * (dp_ - delta)).astype(bf16)
                dq = dot(ds, k, TN) * HDIM ** -0.5
                dk = dot(ds, q) * HDIM ** -0.5
                dqkv[rows, head_at(h):head_at(h) + HDIM] = dq.astype(bf16)
                dqkv[rows, head_at(8 + h):head_at(8 + h) + HDIM] = dk.astype(bf16)
                dqkv[rows, head_at(16 + h):head_at(16 + h) + HDIM] = dv.astype(bf16)
            return carry
        lax.fori_loop(lo, hi, body, 0)

    wait_scatter(mrecv, arecv_sem, 0)
    acc[...] = dot(pr[...], mrecv[...].reshape(TOK, D))

    def patch_norm(i, carry):
        rows = pl.ds(pl.multiple_of(i * 64, 64), 64)
        normed, _ = norm_stats(acc[rows, :])
        normin[rows, :] = (normed * (1.0 + mod[4]) + mod[3]).astype(bf16)
        return carry
    lax.fori_loop(0, 4, patch_norm, 0)
    each(pass_on, jobs_s, 0)
    each(open_second, jobs_s)
    each(share_wait, jobs_q)
    for b in range(2):
        project(q_t, 128 * b, 128)
        attend(True, b, b + 1)
        wait_scatter(drecv.at[b], arecv_sem, 1 + b)
        dout[128 * b:128 * b + 128, :] = drecv[b].reshape(128, HEADS * HP)
        attend_back(b, b + 1)
        project_back(q_t, 128 * b, 128)
        rsend[b] = acc[128 * b:128 * b + 128, :].astype(bf16).reshape(NSEQ, 2, D)
        scatter(rsend.at[b], rrecv.at[b], 3 + b)
        rrecv[b, s] = rsend[b, s]
        if b == 0:
            each(on_second, jobs_s)

    each(end_second, jobs_s)

    def frame_norm(i, carry):
        rows = pl.ds(pl.multiple_of(i * 64, 64), 64)
        normin[rows, :] = (nm_s[rows, :] * (1.0 + mod[1]) + mod[0]).astype(bf16)
        return carry
    lax.fori_loop(0, 4, frame_norm, 0)
    each(share_wait, jobs_s)
    project(q_s, 0, TOK)
    attend(False)

    for cp in pending:
        cp.wait_send()
    o_wait(0)
    wait_scatter(msend, asend_sem, 0)
    for b in range(2):
        wait_scatter(dsend.at[b], asend_sem, 1 + b)

    wait_scatter(rrecv.at[0], arecv_sem, 3)
    acc[...] = dot(back[:, 0:128], rrecv[0].reshape(128, D))
    wait_scatter(rrecv.at[1], arecv_sem, 4)
    acc[...] += dot(back[:, 128:256], rrecv[1].reshape(128, D))

    def mid_grad(i, carry):
        rows = pl.ds(pl.multiple_of(i * 64, 64), 64)
        f, r = i // 2, pl.ds(pl.multiple_of((i % 2) * 64, 64), 64)
        cell = iota((64, 1), 0) * 0 + (2 * s + f)
        masked = jnp.where(cell < frames[0], cot[f, r, :].astype(f32), 0.0)
        grad = masked + norm_back(acc[rows, :], nm_t[rows, :], rs_t[rows, :], 1.0 + mod[4])
        dmid[rows, :] = grad
        normin[rows, :] = (grad * mod[2]).astype(bf16)
        return carry
    lax.fori_loop(0, 4, mid_grad, 0)
    dout[...] = out_back(normin, o_s)
    attend_back(0, 2)
    project_back(q_s, 0, TOK)

    def last_grad(i, carry):
        rows = pl.ds(pl.multiple_of(i * 64, 64), 64)
        f, r = i // 2, pl.ds(pl.multiple_of((i % 2) * 64, 64), 64)
        dnorm = acc[rows, :].astype(bf16).astype(f32)
        grad = norm_back(dnorm, nm_s[rows, :], rs_s[rows, :], 1.0 + mod[1])
        result[f, r, :] = (dmid[rows, :] + grad).astype(bf16)
        return carry
    lax.fori_loop(0, 4, last_grad, 0)

    for b in range(2):
        wait_scatter(rsend.at[b], asend_sem, 3 + b)


def per_device(inputs, mid_inputs, cotangent, modulation, frames, qkv_s, out_s, qkv_t, out_t):
    vmem, hbm = pl.BlockSpec(memory_space=pltpu.VMEM), pl.BlockSpec(memory_space=pltpu.HBM)
    dma = pltpu.SemaphoreType.DMA
    out = pl.pallas_call(
        kernel,
        out_shape=jax.ShapeDtypeStruct((2, 128, D), bf16),
        in_specs=[hbm] * 4 + [pl.BlockSpec(memory_space=pltpu.SMEM)] + [hbm] * 4,
        out_specs=vmem,
        scratch_shapes=[
            pltpu.VMEM((2, 128, D), bf16),
            pltpu.VMEM((2, 128, D), bf16),
            pltpu.VMEM((2, 128, D), bf16),
            pltpu.VMEM((6, 1, D), f32),
            pltpu.VMEM((27, 144), bf16),
            pltpu.VMEM((18, 72), bf16),
            pltpu.VMEM((27, 144), bf16),
            pltpu.VMEM((18, 72), bf16),
            dma((8,)),
            pltpu.VMEM((NZ, 48, 128), bf16),
            pltpu.VMEM((NZ, 64, 128), bf16),
            pltpu.VMEM((NZ, 16, 128), bf16),
            pltpu.VMEM((NZ, 128, QW), bf16),
            pltpu.VMEM((NZ, 128, OW), bf16),
            pltpu.VMEM((NY, 2, NX, 144, QW), bf16),
            pltpu.VMEM((NY, 2, NX, HP, OW), bf16),
            pltpu.VMEM((NY, 2, NX, 144, QW), bf16),
            pltpu.VMEM((NY, 2, NX, HP, OW), bf16),
            pltpu.VMEM((NSEQ, 4, D), bf16),
            pltpu.VMEM((NSEQ, 4, D), bf16),
            pltpu.VMEM((2, NSEQ, 2, HEADS * HP), bf16),
            pltpu.VMEM((2, NSEQ, 2, HEADS * HP), bf16),
            pltpu.VMEM((2, NSEQ, 2, D), bf16),
            pltpu.VMEM((2, NSEQ, 2, D), bf16),
            pltpu.VMEM((TOK, TOK), bf16),
            pltpu.VMEM((TOK, TOK), bf16),
            pltpu.VMEM((TOK, TOK), bf16),
            pltpu.VMEM((TOK, D), bf16),
            pltpu.VMEM((TOK, NY * QW), bf16),
            pltpu.VMEM((TOK, NY * QW), bf16),
            pltpu.VMEM((TOK, HEADS * HP), bf16),
            pltpu.VMEM((2 * HEADS, 128, 128), f32),
            pltpu.VMEM((TOK, D), f32),
            pltpu.VMEM((TOK, D), f32),
            pltpu.VMEM((TOK, 1), f32),
            pltpu.VMEM((TOK, D), f32),
            pltpu.VMEM((TOK, 1), f32),
            pltpu.VMEM((TOK, D), f32),
            dma((2,)), dma((2, 2, 8)), dma((2, 2, 8)), dma((8, 12)), dma((8, 12)), dma((5,)), dma((5,)),
        ],
        compiler_params=pltpu.CompilerParams(
            collective_id=0, has_side_effects=True, vmem_limit_bytes=56 * 1024 * 1024
        ),
        name="blocks_grad",
    )(
        inputs[0], mid_inputs[0], cotangent[0], modulation.reshape(6, 1, D), frames,
        qkv_s.T, out_s.T, qkv_t.T, out_t.T,
    )
    return out[None]


def solution(mesh):
    big = P("dp", "seq", None, None)
    weight = P("dp", "seq")
    return jax.shard_map(
        per_device,
        mesh=mesh,
        in_specs=(big, big, big, P("dp", None, None), P("dp")) + (weight,) * 4,
        out_specs=big,
        check_vma=False,
    )
```

```python
import jax
import jax.numpy as jnp
from jax import lax
from jax.experimental import pallas as pl
from jax.experimental.pallas import tpu as pltpu
from jax.sharding import PartitionSpec as P

HDIM = 72
HEADS = 8
D = 1152
EPS = 1e-06
TOK = 256
NY, NX, NZ = 4, 4, 16
NSEQ = NY * NZ
QW = 512
OW = 384
HP = 80
f32, bf16 = jnp.float32, jnp.bfloat16

NN = (((1,), (0,)), ((), ()))
NT = (((1,), (1,)), ((), ()))
TN = (((0,), (0,)), ((), ()))


def dot(a, b, dims=NN):
    return lax.dot_general(a, b, dims, preferred_element_type=f32)


def iota(shape, axis):
    return lax.broadcasted_iota(jnp.int32, shape, axis)


def head_at(n):
    return (n // 6) * QW + (n % 6) * HDIM


def norm_stats(x):
    center = jnp.mean(x, -1, keepdims=True)
    diff = x - center
    spread = jnp.mean(diff * diff, -1, keepdims=True)
    rstd = lax.rsqrt(spread + EPS)
    return diff * rstd, rstd


def norm_back(dnorm, normed, rstd, gain):
    g = dnorm * gain
    return rstd * (
        g
        - jnp.mean(g, -1, keepdims=True)
        - normed * jnp.mean(g * normed, -1, keepdims=True)
    )


def kernel(
    inp_hbm, mid_hbm, cot_hbm, mod_hbm, frames, qkv_s_hbm, out_s_hbm, qkv_t_hbm, out_t_hbm, result,
    inp, mid, cot, mod, qkv_s, out_s, qkv_t, out_t, load_sem,
    z_qt, z_s, z_ot, eq, eo, q_t, o_t, q_s, o_s,
    msend, mrecv, dsend, drecv, rsend, rrecv,
    pm, pr, back, normin, qkv, dqkv, dout, probs, acc, nm_t, rs_t, nm_s, rs_s, dmid,
    osem, zsend_sem, zrecv_sem, jsend_sem, jrecv_sem, asend_sem, arecv_sem,
):
    dp = lax.axis_index("dp")
    s = lax.axis_index("seq")
    x, c = dp // 2, dp % 2
    y, z = s // NZ, s % NZ
    other = 1 - c
    pending = []

    loads = [
        pltpu.make_async_copy(src, dst, load_sem.at[i])
        for i, (src, dst) in enumerate((
            (qkv_t_hbm, qkv_t), (out_t_hbm, out_t), (qkv_s_hbm, qkv_s), (out_s_hbm, out_s),
            (mid_hbm, mid), (cot_hbm, cot), (mod_hbm, mod), (inp_hbm, inp),
        ))
    ]
    for cp in loads:
        cp.start()

    def seq_dev(yy, zz):
        return {"seq": yy * NZ + zz}

    def x_dev(xx):
        return {"dp": xx * 2 + c}

    far = [(8, dy) for dy in range(NY)]
    near = [(dz, dy) for dy in range(NY) for dz in (0, 1)]
    beside = [(0, dy) for dy in range(1, NY)]

    def peer(dz, dy):
        return lax.rem(y + dy, NY) * NZ + lax.rem(z + dz, NZ)

    def each_peer(f):
        for dz, dy in far:
            f(peer(dz, dy))

        def body(i, carry):
            at = (lax.rem(z + 7 - i, NZ), lax.rem(z + NZ - 7 + i, NZ))
            for way, dy in near:
                f(lax.rem(y + dy, NY) * NZ + at[way])
            return carry
        lax.fori_loop(0, 7, body, 0)
        for dz, dy in beside:
            f(peer(dz, dy))

    barrier = pltpu.get_barrier_semaphore()

    for xx in ((x + 1) % NX, (x + 3) % NX):
        pl.semaphore_signal(barrier, inc=1, device_id=x_dev(xx))
    pl.semaphore_signal(barrier, inc=1, device_id={"dp": x * 2 + other})
    each_peer(lambda to: pl.semaphore_signal(barrier, inc=1, device_id={"seq": to}))

    def pack(ref, group, lanes):
        w = ref[...]
        n, rows = w.shape
        total = None
        for g in range(-(-rows // group)):
            hit = iota((n, 128), 1) == iota((n, 128), 0) + lanes * g
            part = dot(w, jnp.where(hit, 1.0, 0.0).astype(bf16), TN)[group * g:group * (g + 1)]
            if part.shape[0] < group:
                part = jnp.concatenate([part, jnp.zeros((group - part.shape[0], 128), f32)], 0)
            total = part if total is None else total + part
        return total.astype(bf16)

    for cp in loads[:4]:
        cp.wait()
    z_ot[z] = pack(out_t, 16, 24)
    z_qt[z] = pack(qkv_t, 48, 32)
    z_s[z, 0:48] = pack(qkv_s, 48, 32)
    z_s[z, 48:64] = pack(out_s, 16, 24)

    ri, ci = iota((TOK, TOK), 0), iota((TOK, TOK), 1)
    pm[...] = jnp.where(ci == (ri & 1) * 128 + (ri >> 2) * 2 + ((ri >> 1) & 1), 1.0, 0.0).astype(bf16)
    pr[...] = jnp.where(
        ci == ((ri & 127) >> 1) * 4 + (ri >> 7) * 2 + (ri & 1), 1.0, 0.0
    ).astype(bf16)

    back[...] = jnp.where(
        ci == (ri & 1) * 128 + ((ri & 127) >> 1) * 2 + (ri >> 7), 1.0, 0.0
    ).astype(bf16)
    dqkv[...] = jnp.zeros((TOK, NY * QW), bf16)
    loads[4].wait()
    msend[...] = dot(pm[...], mid[...].reshape(TOK, D)).astype(bf16).reshape(NSEQ, 4, D)

    pl.semaphore_wait(barrier, NSEQ - 1 + 3)

    def zcopy(kind, way, dist, block):
        hop = min(dist, 2)
        to = lax.rem(z + hop, NZ) if way == 0 else lax.rem(z + NZ - hop, NZ)
        ref = (z_qt, z_s)[kind].at[block]
        return pltpu.make_async_remote_copy(
            src_ref=ref, dst_ref=ref,
            send_sem=zsend_sem.at[kind, way, dist - 1], recv_sem=zrecv_sem.at[kind, way, dist - 1],
            device_id=seq_dev(y, to),
        )

    def ring_send(kind, way, dist, block):
        cp = zcopy(kind, way, dist, block)
        cp.start()
        pending.append(cp)

    def ring_step(kind, step):
        if step == 0:
            for dist in (1, 2):
                for way in (0, 1):
                    ring_send(kind, way, dist, z)
            return
        for dist in (2 * step - 1, 2 * step):
            for way, block in ((0, lax.rem(z + NZ - dist, NZ)), (1, lax.rem(z + dist, NZ))):
                if dist > 8 - way:
                    continue
                zcopy(kind, way, dist, block).wait_recv()
                if dist + 2 <= 8 - way:
                    ring_send(kind, way, dist + 2, block)

    def send_to(src, dst, k, to):
        pltpu.make_async_remote_copy(
            src_ref=src.at[to], dst_ref=dst.at[s],
            send_sem=asend_sem.at[k], recv_sem=arecv_sem.at[k],
            device_id={"seq": to},
        ).start()

    def scatter(src, dst, k):
        each_peer(lambda to: send_to(src, dst, k, to))

    order = far + [(d, dy) for m in range(7, 0, -1) for dy in range(NY) for d in (m, NZ - m)] + beside

    def send_mid(lo, hi):
        for dz, dy in order[lo:hi]:
            send_to(msend, mrecv, 0, peer(dz, dy))

    def wait_scatter(ref, sem, k):
        part = ref.at[pl.ds(0, NSEQ - 1)]
        pltpu.make_async_copy(part, part, sem.at[k]).wait()

    def fill_q(zz, carry):
        lane, col = iota((128, QW), 0), iota((128, QW), 1)
        at = lane & 31
        hit = (at < 27) & (lane < 96) & (col == at + 27 * zz)
        eq[zz] = jnp.where(hit, 1.0, 0.0).astype(bf16)
        return carry

    def fill_o(zz, carry):
        lane, col = iota((128, OW), 0), iota((128, OW), 1)
        at = lane
        for g in range(1, 5):
            at = jnp.where(lane >= 24 * g, lane - 24 * g, at)
        hit = (at < 18) & (col == at + 18 * zz + 32 * y)
        eo[zz] = jnp.where(hit, 1.0, 0.0).astype(bf16)
        return carry

    def own_norms(i, carry):
        rows = pl.ds(pl.multiple_of(i * 64, 64), 64)
        f, r = i // 2, pl.ds(pl.multiple_of((i % 2) * 64, 64), 64)
        nm_t[rows, :], rs_t[rows, :] = norm_stats(mid[f, r, :].astype(f32))
        nm_s[rows, :], rs_s[rows, :] = norm_stats(inp[f, r, :].astype(f32))
        return carry

    def live_cot(f):
        cell = iota((128, 1), 0) * 0 + (2 * s + f)
        return jnp.where(cell < frames[0], cot[f].astype(f32), 0.0)

    def whole_of(ref, lo, hi):
        return jnp.concatenate([ref[i, lo:hi] for i in range(NZ)], 1)

    def unpack(whole, table, group, lanes, count):
        lane = iota(whole.shape, 1) & 127
        parts = []
        for g in range(count):
            live = (lane >= lanes * g) & (lane < lanes * (g + 1))
            parts.append(jnp.where(live, whole, jnp.zeros_like(whole)))
        lhs = jnp.concatenate(parts, 0)
        return dot(lhs, table[...].reshape(NZ * 128, -1)).astype(bf16)

    def unpack_q(whole):
        return unpack(whole, eq, 48, 32, 3)

    def unpack_o(whole):
        return unpack(whole, eo, 16, 24, 5)

    def o_to(to):
        pltpu.make_async_remote_copy(
            src_ref=z_ot.at[z], dst_ref=z_ot.at[z], send_sem=osem.at[0], recv_sem=osem.at[1],
            device_id=seq_dev(y, to),
        ).start()

    def o_wait(k):
        part = z_ot.at[pl.ds(0, NZ - 1)]
        pltpu.make_async_copy(part, part, osem.at[k]).wait()

    jobs_t = [
        (0, o_t, "y", 0, 32, 16), (1, o_t, "x", 32, 48, 32),
        (2, q_t, "y", 0, 80, 48), (3, q_t, "x", 80, 64, 32),
    ]
    jobs_s = [
        (4, o_s, "y", 0, 32, 16), (5, o_s, "x", 32, 48, 32),
        (6, q_s, "y", 0, 80, 48), (7, q_s, "x", 80, 64, 32),
    ]

    def view(job, phase, rel, half, core, elem):
        _, ref, first, r, n, m = job
        lo, size = {"all": (r, n), "a": (r, m), "b": (r + m, n - m)}[half]
        rows = pl.ds(lo, size)
        along = {"x": x, "y": y}
        if phase == 0:
            along[first] = lax.rem(along[first] + rel, NX)
        else:
            second = "x" if first == "y" else "y"
            along[second] = lax.rem(along[second] + rel, NX)
            along[first] = slice(None) if elem is None else lax.rem(along[first] + elem, NX)
        return ref.at[along["y"], core, along["x"], rows]

    def hop(job, phase, rel, half, way, slot, elem=0):
        first = job[2]
        axis = first if phase == 0 else ("x" if first == "y" else "y")
        step = 1 if way == 0 else 3
        dev = x_dev(lax.rem(x + step, NX)) if axis == "x" else seq_dev(lax.rem(y + step, NY), z)
        ref = view(job, phase, rel, half, c, elem)
        at = slot if phase == 0 else 4 + 4 * elem + slot
        return pltpu.make_async_remote_copy(
            src_ref=ref, dst_ref=ref,
            send_sem=jsend_sem.at[job[0], at], recv_sem=jrecv_sem.at[job[0], at],
            device_id=dev,
        )

    def go(cp):
        cp.start()
        pending.append(cp)

    def first_step(job, phase, elem=0):
        go(hop(job, phase, 0, "all", 0, 0, elem))
        go(hop(job, phase, 0, "all", 1, 1, elem))

    def pass_left(job, phase, elem=0):
        hop(job, phase, 3, "all", 0, 0, elem).wait_recv()
        go(hop(job, phase, 3, "a", 0, 2, elem))

    def pass_right(job, phase, elem=0):
        hop(job, phase, 1, "all", 1, 1, elem).wait_recv()
        go(hop(job, phase, 1, "b", 1, 3, elem))

    def last_step(job, phase, elem=0):
        hop(job, phase, 2, "a", 0, 2, elem).wait_recv()
        hop(job, phase, 2, "b", 1, 3, elem).wait_recv()

    def share(job, rel, core):
        ref = view(job, 1, rel, "all", core, None)
        return pltpu.make_async_remote_copy(
            src_ref=ref, dst_ref=ref,
            send_sem=jsend_sem.at[job[0], 20 + rel], recv_sem=jrecv_sem.at[job[0], 20 + rel],
            device_id={"dp": x * 2 + other},
        )

    def share_wait(job):
        for rel in range(4):
            share(job, rel, other).wait_recv()

    def out_rows(o_ref, yy):
        return jnp.concatenate([o_ref[yy, d % 2, d // 2] for d in range(HEADS)], 0)

    def qkv_rows(q_ref, yy):
        return jnp.concatenate([q_ref[yy, d % 2, d // 2] for d in range(8)], 0)

    def out_back(gated, o_ref):
        total = None
        for yy in range(NY):
            term = dot(gated[:, 256 * yy:256 * yy + OW], out_rows(o_ref, yy), NT)
            total = term if total is None else total + term
        return total.astype(bf16)

    def begin(job):
        first_step(job, 0)
        first_step(job, 1, 0)

    def second(job):
        pass_left(job, 0)
        first_step(job, 1, 3)
        pass_right(job, 0)
        first_step(job, 1, 1)

    def third(job):
        last_step(job, 0)
        first_step(job, 1, 2)
        pass_left(job, 1, 0)
        pass_right(job, 1, 0)
        go(share(job, 0, c))

    def fourth(job):
        for elem in (3, 1, 2):
            pass_left(job, 1, elem)
            pass_right(job, 1, elem)
        go(share(job, 3, c))
        go(share(job, 1, c))

    def fifth(job):
        for elem in (0, 3, 1, 2):
            last_step(job, 1, elem)
        go(share(job, 2, c))

    def each(f, jobs, *args):
        for job in jobs:
            f(job, *args)

    jobs_o, jobs_q = jobs_t[:2], jobs_t[2:]

    for m in range(8, 0, -1):
        o_to(lax.rem(z + m, NZ))
        if m < 8:
            o_to(lax.rem(z + NZ - m, NZ))
    ring_step(0, 0)
    ring_step(1, 0)
    send_mid(0, 8)
    lax.fori_loop(0, NZ, fill_o, 0)
    for cp in loads[5:]:
        cp.wait()
    ring_step(0, 1)
    ring_step(1, 1)
    send_mid(8, 12)
    o_wait(1)
    o_t[y, c, x] = unpack_o(whole_of(z_ot, 0, 16))
    each(begin, jobs_o)
    lax.fori_loop(0, NZ, fill_q, 0)
    ring_step(0, 2)
    ring_step(1, 2)
    send_mid(12, 16)
    each(second, jobs_o)
    ring_step(0, 3)
    ring_step(1, 3)
    send_mid(16, 20)
    for f in range(2):
        normin[f * 128:(f + 1) * 128, :] = (live_cot(f) * mod[5]).astype(bf16)
    ring_step(0, 4)
    q_t[y, c, x] = unpack_q(whole_of(z_qt, 0, 48))
    each(begin, jobs_q)
    each(third, jobs_o)
    send_mid(20, 40)
    ring_step(1, 4)
    o_s[y, c, x] = unpack_o(whole_of(z_s, 48, 64))
    q_s[y, c, x] = unpack_q(whole_of(z_s, 0, 48))
    each(second, jobs_q)
    send_mid(40, 63)
    each(fourth, jobs_o)
    each(third, jobs_q)
    each(fifth, jobs_o)

    each(share_wait, jobs_o)
    dout[...] = out_back(normin, o_t)
    for b in range(2):
        part = dot(back[128 * b:128 * b + 128, :], dout[...])
        dsend[b] = part.astype(bf16).reshape(NSEQ, 2, HEADS * HP)
        scatter(dsend.at[b], drecv.at[b], 1 + b)
        drecv[b, s] = dsend[b, s]
    mrecv[s] = msend[s]
    each(begin, jobs_s)
    lax.fori_loop(0, 4, own_norms, 0)
    each(fourth, jobs_q)
    each(fifth, jobs_q)

    def project(q_ref, lo, n):
        def body(yy, carry):
            lanes = pl.ds(pl.multiple_of(yy * QW, QW), QW)
            qkv[lo:lo + n, lanes] = dot(normin[lo:lo + n, :], qkv_rows(q_ref, yy)).astype(bf16)
            return carry
        lax.fori_loop(0, NY, body, 0)

    def project_back(q_ref, lo, n):
        acc[lo:lo + n, :] = jnp.zeros((n, D), f32)

        def body(yy, carry):
            lanes = pl.ds(pl.multiple_of(yy * QW, QW), QW)
            acc[lo:lo + n, :] += dot(dqkv[lo:lo + n, lanes], qkv_rows(q_ref, yy), NT)
            return carry
        lax.fori_loop(0, NY, body, 0)

    def attend(masked, lo=0, hi=2):
        def body(b, carry):
            rows = pl.ds(pl.multiple_of(b * 128, 128), 128)
            for h in range(HEADS):
                q = qkv[rows, head_at(h):head_at(h) + HDIM]
                k = qkv[rows, head_at(8 + h):head_at(8 + h) + HDIM]
                scores = dot(k, q, NT) * HDIM ** -0.5
                if masked:
                    scores = jnp.where(iota((128, 128), 0) < frames[0], scores, -1e30)
                e = jnp.exp(scores - jnp.max(scores, 0, keepdims=True))
                probs[b * HEADS + h] = e / jnp.sum(e, 0, keepdims=True)
            return carry
        lax.fori_loop(lo, hi, body, 0)

    def attend_back(lo, hi):
        def body(b, carry):
            rows = pl.ds(pl.multiple_of(b * 128, 128), 128)
            for h in range(HEADS):
                q = qkv[rows, head_at(h):head_at(h) + HDIM]
                k = qkv[rows, head_at(8 + h):head_at(8 + h) + HDIM]
                v = qkv[rows, head_at(16 + h):head_at(16 + h) + HDIM]
                up = dout[rows, HP * h:HP * h + HDIM]
                p = probs[b * HEADS + h]
                dv = dot(p.astype(bf16), up)
                dp_ = dot(v, up, NT)
                delta = jnp.sum(p * dp_, 0, keepdims=True)
                ds = (p * (dp_ - delta)).astype(bf16)
                dq = dot(ds, k, TN) * HDIM ** -0.5
                dk = dot(ds, q) * HDIM ** -0.5
                dqkv[rows, head_at(h):head_at(h) + HDIM] = dq.astype(bf16)
                dqkv[rows, head_at(8 + h):head_at(8 + h) + HDIM] = dk.astype(bf16)
                dqkv[rows, head_at(16 + h):head_at(16 + h) + HDIM] = dv.astype(bf16)
            return carry
        lax.fori_loop(lo, hi, body, 0)

    wait_scatter(mrecv, arecv_sem, 0)
    acc[...] = dot(pr[...], mrecv[...].reshape(TOK, D))

    def patch_norm(i, carry):
        rows = pl.ds(pl.multiple_of(i * 64, 64), 64)
        normed, _ = norm_stats(acc[rows, :])
        normin[rows, :] = (normed * (1.0 + mod[4]) + mod[3]).astype(bf16)
        return carry
    lax.fori_loop(0, 4, patch_norm, 0)
    each(second, jobs_s)
    each(share_wait, jobs_q)
    for b in range(2):
        project(q_t, 128 * b, 128)
        if b == 0:
            each(third, jobs_s)
        attend(True, b, b + 1)
        wait_scatter(drecv.at[b], arecv_sem, 1 + b)
        dout[128 * b:128 * b + 128, :] = drecv[b].reshape(128, HEADS * HP)
        attend_back(b, b + 1)
        project_back(q_t, 128 * b, 128)
        rsend[b] = acc[128 * b:128 * b + 128, :].astype(bf16).reshape(NSEQ, 2, D)
        scatter(rsend.at[b], rrecv.at[b], 3 + b)
        rrecv[b, s] = rsend[b, s]
        if b == 0:
            each(fourth, jobs_s)

    each(fifth, jobs_s)

    def frame_norm(i, carry):
        rows = pl.ds(pl.multiple_of(i * 64, 64), 64)
        normin[rows, :] = (nm_s[rows, :] * (1.0 + mod[1]) + mod[0]).astype(bf16)
        return carry
    lax.fori_loop(0, 4, frame_norm, 0)
    each(share_wait, jobs_s)
    project(q_s, 0, TOK)
    attend(False)

    for cp in pending:
        cp.wait_send()
    o_wait(0)
    wait_scatter(msend, asend_sem, 0)
    for b in range(2):
        wait_scatter(dsend.at[b], asend_sem, 1 + b)

    wait_scatter(rrecv.at[0], arecv_sem, 3)
    acc[...] = dot(back[:, 0:128], rrecv[0].reshape(128, D))
    wait_scatter(rrecv.at[1], arecv_sem, 4)
    acc[...] += dot(back[:, 128:256], rrecv[1].reshape(128, D))

    def mid_grad(i, carry):
        rows = pl.ds(pl.multiple_of(i * 64, 64), 64)
        f, r = i // 2, pl.ds(pl.multiple_of((i % 2) * 64, 64), 64)
        cell = iota((64, 1), 0) * 0 + (2 * s + f)
        masked = jnp.where(cell < frames[0], cot[f, r, :].astype(f32), 0.0)
        grad = masked + norm_back(acc[rows, :], nm_t[rows, :], rs_t[rows, :], 1.0 + mod[4])
        dmid[rows, :] = grad
        normin[rows, :] = (grad * mod[2]).astype(bf16)
        return carry
    lax.fori_loop(0, 4, mid_grad, 0)
    dout[...] = out_back(normin, o_s)
    attend_back(0, 2)
    project_back(q_s, 0, TOK)

    def last_grad(i, carry):
        rows = pl.ds(pl.multiple_of(i * 64, 64), 64)
        f, r = i // 2, pl.ds(pl.multiple_of((i % 2) * 64, 64), 64)
        dnorm = acc[rows, :].astype(bf16).astype(f32)
        grad = norm_back(dnorm, nm_s[rows, :], rs_s[rows, :], 1.0 + mod[1])
        result[f, r, :] = (dmid[rows, :] + grad).astype(bf16)
        return carry
    lax.fori_loop(0, 4, last_grad, 0)

    for b in range(2):
        wait_scatter(rsend.at[b], asend_sem, 3 + b)


def per_device(inputs, mid_inputs, cotangent, modulation, frames, qkv_s, out_s, qkv_t, out_t):
    vmem, hbm = pl.BlockSpec(memory_space=pltpu.VMEM), pl.BlockSpec(memory_space=pltpu.HBM)
    dma = pltpu.SemaphoreType.DMA
    out = pl.pallas_call(
        kernel,
        out_shape=jax.ShapeDtypeStruct((2, 128, D), bf16),
        in_specs=[hbm] * 4 + [pl.BlockSpec(memory_space=pltpu.SMEM)] + [hbm] * 4,
        out_specs=vmem,
        scratch_shapes=[
            pltpu.VMEM((2, 128, D), bf16),
            pltpu.VMEM((2, 128, D), bf16),
            pltpu.VMEM((2, 128, D), bf16),
            pltpu.VMEM((6, 1, D), f32),
            pltpu.VMEM((27, 144), bf16),
            pltpu.VMEM((18, 72), bf16),
            pltpu.VMEM((27, 144), bf16),
            pltpu.VMEM((18, 72), bf16),
            dma((8,)),
            pltpu.VMEM((NZ, 48, 128), bf16),
            pltpu.VMEM((NZ, 64, 128), bf16),
            pltpu.VMEM((NZ, 16, 128), bf16),
            pltpu.VMEM((NZ, 128, QW), bf16),
            pltpu.VMEM((NZ, 128, OW), bf16),
            pltpu.VMEM((NY, 2, NX, 144, QW), bf16),
            pltpu.VMEM((NY, 2, NX, HP, OW), bf16),
            pltpu.VMEM((NY, 2, NX, 144, QW), bf16),
            pltpu.VMEM((NY, 2, NX, HP, OW), bf16),
            pltpu.VMEM((NSEQ, 4, D), bf16),
            pltpu.VMEM((NSEQ, 4, D), bf16),
            pltpu.VMEM((2, NSEQ, 2, HEADS * HP), bf16),
            pltpu.VMEM((2, NSEQ, 2, HEADS * HP), bf16),
            pltpu.VMEM((2, NSEQ, 2, D), bf16),
            pltpu.VMEM((2, NSEQ, 2, D), bf16),
            pltpu.VMEM((TOK, TOK), bf16),
            pltpu.VMEM((TOK, TOK), bf16),
            pltpu.VMEM((TOK, TOK), bf16),
            pltpu.VMEM((TOK, D), bf16),
            pltpu.VMEM((TOK, NY * QW), bf16),
            pltpu.VMEM((TOK, NY * QW), bf16),
            pltpu.VMEM((TOK, HEADS * HP), bf16),
            pltpu.VMEM((2 * HEADS, 128, 128), f32),
            pltpu.VMEM((TOK, D), f32),
            pltpu.VMEM((TOK, D), f32),
            pltpu.VMEM((TOK, 1), f32),
            pltpu.VMEM((TOK, D), f32),
            pltpu.VMEM((TOK, 1), f32),
            pltpu.VMEM((TOK, D), f32),
            dma((2,)), dma((2, 2, 8)), dma((2, 2, 8)), dma((8, 24)), dma((8, 24)), dma((5,)), dma((5,)),
        ],
        compiler_params=pltpu.CompilerParams(
            collective_id=0, has_side_effects=True, vmem_limit_bytes=56 * 1024 * 1024
        ),
        name="blocks_grad",
    )(
        inputs[0], mid_inputs[0], cotangent[0], modulation.reshape(6, 1, D), frames,
        qkv_s.T, out_s.T, qkv_t.T, out_t.T,
    )
    return out[None]


def solution(mesh):
    big = P("dp", "seq", None, None)
    weight = P("dp", "seq")
    return jax.shard_map(
        per_device,
        mesh=mesh,
        in_specs=(big, big, big, P("dp", None, None), P("dp")) + (weight,) * 4,
        out_specs=big,
        check_vma=False,
    )
```

```python
import jax
import jax.numpy as jnp
from jax import lax
from jax.experimental import pallas as pl
from jax.experimental.pallas import tpu as pltpu
from jax.sharding import PartitionSpec as P

HDIM = 72
HEADS = 8
D = 1152
EPS = 1e-06
TOK = 256
NY, NX, NZ = 4, 4, 16
NSEQ = NY * NZ
QW = 512
OW = 384
HP = 80
f32, bf16 = jnp.float32, jnp.bfloat16

NN = (((1,), (0,)), ((), ()))
NT = (((1,), (1,)), ((), ()))
TN = (((0,), (0,)), ((), ()))


def dot(a, b, dims=NN):
    return lax.dot_general(a, b, dims, preferred_element_type=f32)


def iota(shape, axis):
    return lax.broadcasted_iota(jnp.int32, shape, axis)


def head_at(n):
    return (n // 6) * QW + (n % 6) * HDIM


def norm_stats(x):
    center = jnp.mean(x, -1, keepdims=True)
    diff = x - center
    spread = jnp.mean(diff * diff, -1, keepdims=True)
    rstd = lax.rsqrt(spread + EPS)
    return diff * rstd, rstd


def norm_back(dnorm, normed, rstd, gain):
    g = dnorm * gain
    return rstd * (
        g
        - jnp.mean(g, -1, keepdims=True)
        - normed * jnp.mean(g * normed, -1, keepdims=True)
    )


def kernel(
    inp_hbm, mid_hbm, cot_hbm, mod_hbm, frames, qkv_s_hbm, out_s_hbm, qkv_t_hbm, out_t_hbm, result,
    inp, mid, cot, mod, qkv_s, out_s, qkv_t, out_t, load_sem,
    z_t, z_s, eq, eo, q_t, o_t, q_s, o_s,
    msend, mrecv, dsend, drecv, rsend, rrecv,
    pm, pr, back, normin, qkv, dqkv, dout, probs, acc, nm_t, rs_t, nm_s, rs_s, dmid,
    zsend_sem, zrecv_sem, jsend_sem, jrecv_sem, asend_sem, arecv_sem,
):
    dp = lax.axis_index("dp")
    s = lax.axis_index("seq")
    x, c = dp // 2, dp % 2
    y, z = s // NZ, s % NZ
    other = 1 - c
    pending = []

    loads = [
        pltpu.make_async_copy(src, dst, load_sem.at[i])
        for i, (src, dst) in enumerate((
            (qkv_t_hbm, qkv_t), (out_t_hbm, out_t), (qkv_s_hbm, qkv_s), (out_s_hbm, out_s),
            (mid_hbm, mid), (cot_hbm, cot), (mod_hbm, mod), (inp_hbm, inp),
        ))
    ]
    for cp in loads:
        cp.start()

    def seq_dev(yy, zz):
        return {"seq": yy * NZ + zz}

    def x_dev(xx):
        return {"dp": xx * 2 + c}

    far = [(8, dy) for dy in range(NY)]
    near = [(dz, dy) for dy in range(NY) for dz in (0, 1)]
    beside = [(0, dy) for dy in range(1, NY)]

    def peer(dz, dy):
        return lax.rem(y + dy, NY) * NZ + lax.rem(z + dz, NZ)

    def each_peer(f):
        for dz, dy in far:
            f(peer(dz, dy))

        def body(i, carry):
            at = (lax.rem(z + 7 - i, NZ), lax.rem(z + NZ - 7 + i, NZ))
            for way, dy in near:
                f(lax.rem(y + dy, NY) * NZ + at[way])
            return carry
        lax.fori_loop(0, 7, body, 0)
        for dz, dy in beside:
            f(peer(dz, dy))

    barrier = pltpu.get_barrier_semaphore()

    for xx in ((x + 1) % NX, (x + 3) % NX):
        pl.semaphore_signal(barrier, inc=1, device_id=x_dev(xx))
    pl.semaphore_signal(barrier, inc=1, device_id={"dp": x * 2 + other})
    each_peer(lambda to: pl.semaphore_signal(barrier, inc=1, device_id={"seq": to}))

    def pack(ref, group, lanes):
        w = ref[...]
        n, rows = w.shape
        total = None
        for g in range(-(-rows // group)):
            hit = iota((n, 128), 1) == iota((n, 128), 0) + lanes * g
            part = dot(w, jnp.where(hit, 1.0, 0.0).astype(bf16), TN)[group * g:group * (g + 1)]
            if part.shape[0] < group:
                part = jnp.concatenate([part, jnp.zeros((group - part.shape[0], 128), f32)], 0)
            total = part if total is None else total + part
        return total.astype(bf16)

    for cp in loads[:4]:
        cp.wait()
    for ref, q, o in ((z_t, qkv_t, out_t), (z_s, qkv_s, out_s)):
        ref[z, 0:48] = pack(q, 48, 32)
        ref[z, 48:64] = pack(o, 16, 24)

    pl.semaphore_wait(barrier, NSEQ - 1 + 3)

    def zcopy(kind, block, way, step):
        to = lax.rem(z + 1, NZ) if way == 0 else lax.rem(z + NZ - 1, NZ)
        ref = (z_t, z_s)[kind].at[block]
        return pltpu.make_async_remote_copy(
            src_ref=ref, dst_ref=ref,
            send_sem=zsend_sem.at[kind, way, step], recv_sem=zrecv_sem.at[kind, way, step],
            device_id=seq_dev(y, to),
        )

    def ring_step(kind, step):
        for way, block in ((0, lax.rem(z + NZ - step, NZ)), (1, lax.rem(z + step, NZ))):
            if step > 0 and not (way == 1 and step == 8):
                zcopy(kind, block, way, step - 1).wait_recv()
            if step < 8 - way:
                cp = zcopy(kind, block, way, step)
                cp.start()
                pending.append(cp)

    def send_to(src, dst, k, to):
        pltpu.make_async_remote_copy(
            src_ref=src.at[to], dst_ref=dst.at[s],
            send_sem=asend_sem.at[k], recv_sem=arecv_sem.at[k],
            device_id={"seq": to},
        ).start()

    def send_pair(src, dst, k, to):
        pltpu.make_async_remote_copy(
            src_ref=src.at[:, to], dst_ref=dst.at[:, s],
            send_sem=asend_sem.at[k], recv_sem=arecv_sem.at[k],
            device_id={"seq": to},
        ).start()

    def wait_pairs(ref, sem, k):
        part = ref.at[:, pl.ds(0, NSEQ - 1)]
        pltpu.make_async_copy(part, part, sem.at[k]).wait()

    def scatter(src, dst, k):
        each_peer(lambda to: send_to(src, dst, k, to))

    order = far + [(d, dy) for m in range(7, 0, -1) for dy in range(NY) for d in (m, NZ - m)] + beside

    def send_mid(lo, hi):
        for dz, dy in order[lo:hi]:
            send_to(msend, mrecv, 0, peer(dz, dy))

    def wait_scatter(ref, sem, k):
        part = ref.at[pl.ds(0, NSEQ - 1)]
        pltpu.make_async_copy(part, part, sem.at[k]).wait()

    def fill_q(zz, carry):
        lane, col = iota((128, QW), 0), iota((128, QW), 1)
        at = lane & 31
        hit = (at < 27) & (lane < 96) & (col == at + 27 * zz)
        eq[zz] = jnp.where(hit, 1.0, 0.0).astype(bf16)
        return carry

    def fill_o(zz, carry):
        lane, col = iota((128, OW), 0), iota((128, OW), 1)
        at = lane
        for g in range(1, 5):
            at = jnp.where(lane >= 24 * g, lane - 24 * g, at)
        hit = (at < 18) & (col == at + 18 * zz + 32 * y)
        eo[zz] = jnp.where(hit, 1.0, 0.0).astype(bf16)
        return carry

    def own_norms(i, carry):
        rows = pl.ds(pl.multiple_of(i * 64, 64), 64)
        f, r = i // 2, pl.ds(pl.multiple_of((i % 2) * 64, 64), 64)
        nm_t[rows, :], rs_t[rows, :] = norm_stats(mid[f, r, :].astype(f32))
        nm_s[rows, :], rs_s[rows, :] = norm_stats(inp[f, r, :].astype(f32))
        return carry

    def live_cot(f):
        cell = iota((128, 1), 0) * 0 + (2 * s + f)
        return jnp.where(cell < frames[0], cot[f].astype(f32), 0.0)

    def whole_of(ref, lo, hi):
        return jnp.concatenate([ref[i, lo:hi] for i in range(NZ)], 1)

    def unpack(whole, table, group, lanes, count):
        lane = iota(whole.shape, 1) & 127
        parts = []
        for g in range(count):
            live = (lane >= lanes * g) & (lane < lanes * (g + 1))
            parts.append(jnp.where(live, whole, jnp.zeros_like(whole)))
        lhs = jnp.concatenate(parts, 0)
        return dot(lhs, table[...].reshape(NZ * 128, -1)).astype(bf16)

    def unpack_q(whole):
        return unpack(whole, eq, 48, 32, 3)

    def unpack_o(whole):
        return unpack(whole, eo, 16, 24, 5)

    jobs_o = [(0, o_t, "y", 0, 80, 48)]
    jobs_q = [(1, q_t, "x", 0, 144, 80)]
    jobs_s = [(2, o_s, "x", 0, 80, 48), (3, q_s, "y", 0, 144, 80)]

    def view(job, phase, rel, half, core):
        _, ref, first, r, n, m = job
        lo, size = {"all": (r, n), "a": (r, m), "b": (r + m, n - m)}[half]
        rows = pl.ds(lo, size)
        axis = first if phase == 0 else ("x" if first == "y" else "y")
        if axis == "x":
            return ref.at[y if phase == 0 else slice(None), core, (x + rel) % NX, rows]
        return ref.at[(y + rel) % NY, core, x if phase == 0 else slice(None), rows]

    def hop(job, phase, rel, half, way, slot):
        first = job[2]
        axis = first if phase == 0 else ("x" if first == "y" else "y")
        step = 1 if way == 0 else 3
        dev = x_dev((x + step) % NX) if axis == "x" else seq_dev((y + step) % NY, z)
        ref = view(job, phase, rel, half, c)
        return pltpu.make_async_remote_copy(
            src_ref=ref, dst_ref=ref,
            send_sem=jsend_sem.at[job[0], phase * 4 + slot],
            recv_sem=jrecv_sem.at[job[0], phase * 4 + slot],
            device_id=dev,
        )

    def go(cp):
        cp.start()
        pending.append(cp)

    def first_step(job, phase):
        go(hop(job, phase, 0, "all", 0, 0))
        go(hop(job, phase, 0, "all", 1, 1))

    def pass_on(job, phase):
        hop(job, phase, 3, "all", 0, 0).wait_recv()
        go(hop(job, phase, 3, "a", 0, 2))
        hop(job, phase, 1, "all", 1, 1).wait_recv()
        go(hop(job, phase, 1, "b", 1, 3))

    def last_step(job, phase):
        hop(job, phase, 2, "a", 0, 2).wait_recv()
        hop(job, phase, 2, "b", 1, 3).wait_recv()

    def share(job, rel, core):
        ref = view(job, 1, rel, "all", core)
        return pltpu.make_async_remote_copy(
            src_ref=ref, dst_ref=ref,
            send_sem=jsend_sem.at[job[0], 8 + rel], recv_sem=jrecv_sem.at[job[0], 8 + rel],
            device_id={"dp": x * 2 + other},
        )

    def share_wait(job):
        for rel in range(4):
            share(job, rel, other).wait_recv()

    def out_rows(o_ref, yy):
        return jnp.concatenate([o_ref[yy, d % 2, d // 2] for d in range(HEADS)], 0)

    def qkv_rows(q_ref, yy):
        return jnp.concatenate([q_ref[yy, d % 2, d // 2] for d in range(8)], 0)

    def out_back(gated, o_ref):
        total = None
        for yy in range(NY):
            term = dot(gated[:, 256 * yy:256 * yy + OW], out_rows(o_ref, yy), NT)
            total = term if total is None else total + term
        return total.astype(bf16)

    def open_second(job):
        last_step(job, 0)
        first_step(job, 1)
        go(share(job, 0, c))

    def on_second(job):
        pass_on(job, 1)
        go(share(job, 3, c))
        go(share(job, 1, c))

    def end_second(job):
        last_step(job, 1)
        go(share(job, 2, c))

    def each(f, jobs, *args):
        for job in jobs:
            f(job, *args)

    ring_step(0, 0)
    ring_step(1, 0)
    ri, ci = iota((TOK, TOK), 0), iota((TOK, TOK), 1)
    pm[...] = jnp.where(ci == (ri & 1) * 128 + (ri >> 2) * 2 + ((ri >> 1) & 1), 1.0, 0.0).astype(bf16)
    pr[...] = jnp.where(
        ci == ((ri & 127) >> 1) * 4 + (ri >> 7) * 2 + (ri & 1), 1.0, 0.0
    ).astype(bf16)

    back[...] = jnp.where(
        ci == (ri & 1) * 128 + ((ri & 127) >> 1) * 2 + (ri >> 7), 1.0, 0.0
    ).astype(bf16)
    dqkv[...] = jnp.zeros((TOK, NY * QW), bf16)
    loads[4].wait()
    msend[...] = dot(pm[...], mid[...].reshape(TOK, D)).astype(bf16).reshape(NSEQ, 4, D)

    for step in range(8):
        if step > 0:
            ring_step(0, step)
            ring_step(1, step)
        send_mid(2 * step, 2 * step + 2)
        lax.fori_loop(2 * step, 2 * step + 2, fill_o, 0)
        lax.fori_loop(2 * step, 2 * step + 2, fill_q, 0)
        if step == 1:
            for cp in loads[5:]:
                cp.wait()
        if step in (2, 3):
            f = step - 2
            normin[f * 128:(f + 1) * 128, :] = (live_cot(f) * mod[5]).astype(bf16)
        if step > 3:
            lax.fori_loop(step - 4, step - 3, own_norms, 0)
    ring_step(0, 8)
    o_t[y, c, x] = unpack_o(whole_of(z_t, 48, 64))
    each(first_step, jobs_o, 0)
    q_t[y, c, x] = unpack_q(whole_of(z_t, 0, 48))
    each(first_step, jobs_q, 0)
    send_mid(16, 28)
    ring_step(1, 8)
    each(pass_on, jobs_o, 0)
    o_s[y, c, x] = unpack_o(whole_of(z_s, 48, 64))
    q_s[y, c, x] = unpack_q(whole_of(z_s, 0, 48))
    each(open_second, jobs_o)
    each(pass_on, jobs_q, 0)
    each(first_step, jobs_s, 0)
    send_mid(28, 46)
    each(open_second, jobs_q)
    each(on_second, jobs_o)
    send_mid(46, 63)
    each(pass_on, jobs_s, 0)
    each(end_second, jobs_o)

    each(share_wait, jobs_o)
    dout[...] = out_back(normin, o_t)
    for b in range(2):
        part = dot(back[128 * b:128 * b + 128, :], dout[...])
        dsend[b] = part.astype(bf16).reshape(NSEQ, 2, HEADS * HP)
    each_peer(lambda to: send_pair(dsend, drecv, 1, to))
    drecv[:, s] = dsend[:, s]
    mrecv[s] = msend[s]
    each(open_second, jobs_s)
    each(on_second, jobs_q)
    each(end_second, jobs_q)

    def project(q_ref, lo, n):
        def body(yy, carry):
            lanes = pl.ds(pl.multiple_of(yy * QW, QW), QW)
            qkv[lo:lo + n, lanes] = dot(normin[lo:lo + n, :], qkv_rows(q_ref, yy)).astype(bf16)
            return carry
        lax.fori_loop(0, NY, body, 0)

    def project_back(q_ref, lo, n):
        acc[lo:lo + n, :] = jnp.zeros((n, D), f32)

        def body(yy, carry):
            lanes = pl.ds(pl.multiple_of(yy * QW, QW), QW)
            acc[lo:lo + n, :] += dot(dqkv[lo:lo + n, lanes], qkv_rows(q_ref, yy), NT)
            return carry
        lax.fori_loop(0, NY, body, 0)

    def attend(masked, lo=0, hi=2):
        def body(b, carry):
            rows = pl.ds(pl.multiple_of(b * 128, 128), 128)
            for h in range(HEADS):
                q = qkv[rows, head_at(h):head_at(h) + HDIM]
                k = qkv[rows, head_at(8 + h):head_at(8 + h) + HDIM]
                scores = dot(k, q, NT) * HDIM ** -0.5
                if masked:
                    scores = jnp.where(iota((128, 128), 0) < frames[0], scores, -1e30)
                e = jnp.exp(scores - jnp.max(scores, 0, keepdims=True))
                probs[b * HEADS + h] = e / jnp.sum(e, 0, keepdims=True)
            return carry
        lax.fori_loop(lo, hi, body, 0)

    def attend_back(lo, hi):
        def body(b, carry):
            rows = pl.ds(pl.multiple_of(b * 128, 128), 128)
            for h in range(HEADS):
                q = qkv[rows, head_at(h):head_at(h) + HDIM]
                k = qkv[rows, head_at(8 + h):head_at(8 + h) + HDIM]
                v = qkv[rows, head_at(16 + h):head_at(16 + h) + HDIM]
                up = dout[rows, HP * h:HP * h + HDIM]
                p = probs[b * HEADS + h]
                dv = dot(p.astype(bf16), up)
                dp_ = dot(v, up, NT)
                delta = jnp.sum(p * dp_, 0, keepdims=True)
                ds = (p * (dp_ - delta)).astype(bf16)
                dq = dot(ds, k, TN) * HDIM ** -0.5
                dk = dot(ds, q) * HDIM ** -0.5
                dqkv[rows, head_at(h):head_at(h) + HDIM] = dq.astype(bf16)
                dqkv[rows, head_at(8 + h):head_at(8 + h) + HDIM] = dk.astype(bf16)
                dqkv[rows, head_at(16 + h):head_at(16 + h) + HDIM] = dv.astype(bf16)
            return carry
        lax.fori_loop(lo, hi, body, 0)

    wait_scatter(mrecv, arecv_sem, 0)
    acc[...] = dot(pr[...], mrecv[...].reshape(TOK, D))

    def patch_norm(i, carry):
        rows = pl.ds(pl.multiple_of(i * 64, 64), 64)
        normed, _ = norm_stats(acc[rows, :])
        normin[rows, :] = (normed * (1.0 + mod[4]) + mod[3]).astype(bf16)
        return carry
    lax.fori_loop(0, 4, patch_norm, 0)
    each(share_wait, jobs_q)
    project(q_t, 0, TOK)
    attend(True)
    wait_pairs(drecv, arecv_sem, 1)
    dout[...] = drecv[...].reshape(TOK, HEADS * HP)
    for b in range(2):
        attend_back(b, b + 1)
        project_back(q_t, 128 * b, 128)
        rsend[b] = acc[128 * b:128 * b + 128, :].astype(bf16).reshape(NSEQ, 2, D)
        scatter(rsend.at[b], rrecv.at[b], 2 + b)
        rrecv[b, s] = rsend[b, s]
        if b == 0:
            each(on_second, jobs_s)

    each(end_second, jobs_s)

    def frame_norm(i, carry):
        rows = pl.ds(pl.multiple_of(i * 64, 64), 64)
        normin[rows, :] = (nm_s[rows, :] * (1.0 + mod[1]) + mod[0]).astype(bf16)
        return carry
    lax.fori_loop(0, 4, frame_norm, 0)
    each(share_wait, jobs_s)
    project(q_s, 0, TOK)
    attend(False)

    for cp in pending:
        cp.wait_send()
    wait_scatter(msend, asend_sem, 0)
    wait_pairs(dsend, asend_sem, 1)

    wait_scatter(rrecv.at[0], arecv_sem, 2)
    acc[...] = dot(back[:, 0:128], rrecv[0].reshape(128, D))
    wait_scatter(rrecv.at[1], arecv_sem, 3)
    acc[...] += dot(back[:, 128:256], rrecv[1].reshape(128, D))

    def mid_grad(i, carry):
        rows = pl.ds(pl.multiple_of(i * 64, 64), 64)
        f, r = i // 2, pl.ds(pl.multiple_of((i % 2) * 64, 64), 64)
        cell = iota((64, 1), 0) * 0 + (2 * s + f)
        masked = jnp.where(cell < frames[0], cot[f, r, :].astype(f32), 0.0)
        grad = masked + norm_back(acc[rows, :], nm_t[rows, :], rs_t[rows, :], 1.0 + mod[4])
        dmid[rows, :] = grad
        normin[rows, :] = (grad * mod[2]).astype(bf16)
        return carry
    lax.fori_loop(0, 4, mid_grad, 0)
    dout[...] = out_back(normin, o_s)
    attend_back(0, 2)
    project_back(q_s, 0, TOK)

    def last_grad(i, carry):
        rows = pl.ds(pl.multiple_of(i * 64, 64), 64)
        f, r = i // 2, pl.ds(pl.multiple_of((i % 2) * 64, 64), 64)
        dnorm = acc[rows, :].astype(bf16).astype(f32)
        grad = norm_back(dnorm, nm_s[rows, :], rs_s[rows, :], 1.0 + mod[1])
        result[f, r, :] = (dmid[rows, :] + grad).astype(bf16)
        return carry
    lax.fori_loop(0, 4, last_grad, 0)

    for b in range(2):
        wait_scatter(rsend.at[b], asend_sem, 2 + b)


def per_device(inputs, mid_inputs, cotangent, modulation, frames, qkv_s, out_s, qkv_t, out_t):
    vmem, hbm = pl.BlockSpec(memory_space=pltpu.VMEM), pl.BlockSpec(memory_space=pltpu.HBM)
    dma = pltpu.SemaphoreType.DMA
    out = pl.pallas_call(
        kernel,
        out_shape=jax.ShapeDtypeStruct((2, 128, D), bf16),
        in_specs=[hbm] * 4 + [pl.BlockSpec(memory_space=pltpu.SMEM)] + [hbm] * 4,
        out_specs=vmem,
        scratch_shapes=[
            pltpu.VMEM((2, 128, D), bf16),
            pltpu.VMEM((2, 128, D), bf16),
            pltpu.VMEM((2, 128, D), bf16),
            pltpu.VMEM((6, 1, D), f32),
            pltpu.VMEM((27, 144), bf16),
            pltpu.VMEM((18, 72), bf16),
            pltpu.VMEM((27, 144), bf16),
            pltpu.VMEM((18, 72), bf16),
            dma((8,)),
            pltpu.VMEM((NZ, 64, 128), bf16),
            pltpu.VMEM((NZ, 64, 128), bf16),
            pltpu.VMEM((NZ, 128, QW), bf16),
            pltpu.VMEM((NZ, 128, OW), bf16),
            pltpu.VMEM((NY, 2, NX, 144, QW), bf16),
            pltpu.VMEM((NY, 2, NX, HP, OW), bf16),
            pltpu.VMEM((NY, 2, NX, 144, QW), bf16),
            pltpu.VMEM((NY, 2, NX, HP, OW), bf16),
            pltpu.VMEM((NSEQ, 4, D), bf16),
            pltpu.VMEM((NSEQ, 4, D), bf16),
            pltpu.VMEM((2, NSEQ, 2, HEADS * HP), bf16),
            pltpu.VMEM((2, NSEQ, 2, HEADS * HP), bf16),
            pltpu.VMEM((2, NSEQ, 2, D), bf16),
            pltpu.VMEM((2, NSEQ, 2, D), bf16),
            pltpu.VMEM((TOK, TOK), bf16),
            pltpu.VMEM((TOK, TOK), bf16),
            pltpu.VMEM((TOK, TOK), bf16),
            pltpu.VMEM((TOK, D), bf16),
            pltpu.VMEM((TOK, NY * QW), bf16),
            pltpu.VMEM((TOK, NY * QW), bf16),
            pltpu.VMEM((TOK, HEADS * HP), bf16),
            pltpu.VMEM((2 * HEADS, 128, 128), f32),
            pltpu.VMEM((TOK, D), f32),
            pltpu.VMEM((TOK, D), f32),
            pltpu.VMEM((TOK, 1), f32),
            pltpu.VMEM((TOK, D), f32),
            pltpu.VMEM((TOK, 1), f32),
            pltpu.VMEM((TOK, D), f32),
            dma((2, 2, 8)), dma((2, 2, 8)), dma((4, 12)), dma((4, 12)), dma((4,)), dma((4,)),
        ],
        compiler_params=pltpu.CompilerParams(
            collective_id=0, has_side_effects=True, vmem_limit_bytes=56 * 1024 * 1024
        ),
        name="blocks_grad",
    )(
        inputs[0], mid_inputs[0], cotangent[0], modulation.reshape(6, 1, D), frames,
        qkv_s.T, out_s.T, qkv_t.T, out_t.T,
    )
    return out[None]


def solution(mesh):
    big = P("dp", "seq", None, None)
    weight = P("dp", "seq")
    return jax.shard_map(
        per_device,
        mesh=mesh,
        in_specs=(big, big, big, P("dp", None, None), P("dp")) + (weight,) * 4,
        out_specs=big,
        check_vma=False,
    )
```

```python
import jax
import jax.numpy as jnp
from jax import lax
from jax.experimental import pallas as pl
from jax.experimental.pallas import tpu as pltpu
from jax.sharding import PartitionSpec as P

HDIM = 72
HEADS = 8
D = 1152
EPS = 1e-06
TOK = 256
NY, NX, NZ = 4, 4, 16
NSEQ = NY * NZ
QW = 512
OW = 384
HP = 80
f32, bf16 = jnp.float32, jnp.bfloat16

NN = (((1,), (0,)), ((), ()))
NT = (((1,), (1,)), ((), ()))
TN = (((0,), (0,)), ((), ()))


def dot(a, b, dims=NN):
    return lax.dot_general(a, b, dims, preferred_element_type=f32)


def iota(shape, axis):
    return lax.broadcasted_iota(jnp.int32, shape, axis)


def head_at(n):
    return (n // 6) * QW + (n % 6) * HDIM


def norm_stats(x):
    center = jnp.mean(x, -1, keepdims=True)
    diff = x - center
    spread = jnp.mean(diff * diff, -1, keepdims=True)
    rstd = lax.rsqrt(spread + EPS)
    return diff * rstd, rstd


def norm_back(dnorm, normed, rstd, gain):
    g = dnorm * gain
    return rstd * (
        g
        - jnp.mean(g, -1, keepdims=True)
        - normed * jnp.mean(g * normed, -1, keepdims=True)
    )


def kernel(
    inp_hbm, mid_hbm, cot_hbm, mod_hbm, frames, qkv_s_hbm, out_s_hbm, qkv_t_hbm, out_t_hbm, result,
    inp, mid, cot, mod, qkv_s, out_s, qkv_t, out_t, load_sem,
    z_t, z_s, eq, eo, q_t, o_t, q_s, o_s,
    msend, mrecv, dsend, drecv, rsend, rrecv,
    pm, pr, back, normin, qkv, dqkv, dout, probs, acc, nm_t, rs_t, nm_s, rs_s, dmid,
    zsend_sem, zrecv_sem, jsend_sem, jrecv_sem, asend_sem, arecv_sem,
):
    dp = lax.axis_index("dp")
    s = lax.axis_index("seq")
    x, c = dp // 2, dp % 2
    y, z = s // NZ, s % NZ
    other = 1 - c
    pending = []

    loads = [
        pltpu.make_async_copy(src, dst, load_sem.at[i])
        for i, (src, dst) in enumerate((
            (qkv_t_hbm, qkv_t), (out_t_hbm, out_t), (qkv_s_hbm, qkv_s), (out_s_hbm, out_s),
            (mid_hbm, mid), (cot_hbm, cot), (mod_hbm, mod), (inp_hbm, inp),
        ))
    ]
    for cp in loads:
        cp.start()

    def seq_dev(yy, zz):
        return {"seq": yy * NZ + zz}

    def x_dev(xx):
        return {"dp": xx * 2 + c}

    far = [(8, dy) for dy in range(NY)]
    near = [(dz, dy) for dy in range(NY) for dz in (0, 1)]
    beside = [(0, dy) for dy in range(1, NY)]

    def peer(dz, dy):
        return lax.rem(y + dy, NY) * NZ + lax.rem(z + dz, NZ)

    def each_peer(f):
        for dz, dy in far:
            f(peer(dz, dy))

        def body(i, carry):
            at = (lax.rem(z + 7 - i, NZ), lax.rem(z + NZ - 7 + i, NZ))
            for way, dy in near:
                f(lax.rem(y + dy, NY) * NZ + at[way])
            return carry
        lax.fori_loop(0, 7, body, 0)
        for dz, dy in beside:
            f(peer(dz, dy))

    barrier = pltpu.get_barrier_semaphore()

    for xx in ((x + 1) % NX, (x + 3) % NX):
        pl.semaphore_signal(barrier, inc=1, device_id=x_dev(xx))
    pl.semaphore_signal(barrier, inc=1, device_id={"dp": x * 2 + other})
    each_peer(lambda to: pl.semaphore_signal(barrier, inc=1, device_id={"seq": to}))

    def pack(ref, group, lanes):
        w = ref[...]
        n, rows = w.shape
        total = None
        for g in range(-(-rows // group)):
            hit = iota((n, 128), 1) == iota((n, 128), 0) + lanes * g
            part = dot(w, jnp.where(hit, 1.0, 0.0).astype(bf16), TN)[group * g:group * (g + 1)]
            if part.shape[0] < group:
                part = jnp.concatenate([part, jnp.zeros((group - part.shape[0], 128), f32)], 0)
            total = part if total is None else total + part
        return total.astype(bf16)

    for cp in loads[:4]:
        cp.wait()
    for ref, q, o in ((z_t, qkv_t, out_t), (z_s, qkv_s, out_s)):
        ref[z, 0:48] = pack(q, 48, 32)
        ref[z, 48:64] = pack(o, 16, 24)

    pl.semaphore_wait(barrier, NSEQ - 1 + 3)

    def zcopy(kind, block, way, step):
        to = lax.rem(z + 1, NZ) if way == 0 else lax.rem(z + NZ - 1, NZ)
        ref = (z_t, z_s)[kind].at[block]
        return pltpu.make_async_remote_copy(
            src_ref=ref, dst_ref=ref,
            send_sem=zsend_sem.at[kind, way, step], recv_sem=zrecv_sem.at[kind, way, step],
            device_id=seq_dev(y, to),
        )

    def ring_step(kind, step):
        for way, block in ((0, lax.rem(z + NZ - step, NZ)), (1, lax.rem(z + step, NZ))):
            if step > 0 and not (way == 1 and step == 8):
                zcopy(kind, block, way, step - 1).wait_recv()
            if step < 8 - way:
                cp = zcopy(kind, block, way, step)
                cp.start()
                pending.append(cp)

    def send_to(src, dst, k, to):
        pltpu.make_async_remote_copy(
            src_ref=src.at[to], dst_ref=dst.at[s],
            send_sem=asend_sem.at[k], recv_sem=arecv_sem.at[k],
            device_id={"seq": to},
        ).start()

    def scatter(src, dst, k):
        each_peer(lambda to: send_to(src, dst, k, to))

    order = far + [(d, dy) for m in range(7, 0, -1) for dy in range(NY) for d in (m, NZ - m)] + beside

    def send_mid(lo, hi):
        for dz, dy in order[lo:hi]:
            send_to(msend, mrecv, 0, peer(dz, dy))

    def wait_scatter(ref, sem, k):
        part = ref.at[pl.ds(0, NSEQ - 1)]
        pltpu.make_async_copy(part, part, sem.at[k]).wait()

    def fill_q(zz, carry):
        lane, col = iota((128, QW), 0), iota((128, QW), 1)
        at = lane & 31
        hit = (at < 27) & (lane < 96) & (col == at + 27 * zz)
        eq[zz] = jnp.where(hit, 1.0, 0.0).astype(bf16)
        return carry

    def fill_o(zz, carry):
        lane, col = iota((128, OW), 0), iota((128, OW), 1)
        at = lane
        for g in range(1, 5):
            at = jnp.where(lane >= 24 * g, lane - 24 * g, at)
        hit = (at < 18) & (col == at + 18 * zz + 32 * y)
        eo[zz] = jnp.where(hit, 1.0, 0.0).astype(bf16)
        return carry

    def own_norms(i, carry):
        rows = pl.ds(pl.multiple_of(i * 64, 64), 64)
        f, r = i // 2, pl.ds(pl.multiple_of((i % 2) * 64, 64), 64)
        nm_t[rows, :], rs_t[rows, :] = norm_stats(mid[f, r, :].astype(f32))
        nm_s[rows, :], rs_s[rows, :] = norm_stats(inp[f, r, :].astype(f32))
        return carry

    def live_cot(f):
        cell = iota((128, 1), 0) * 0 + (2 * s + f)
        return jnp.where(cell < frames[0], cot[f].astype(f32), 0.0)

    def whole_of(ref, lo, hi):
        return jnp.concatenate([ref[i, lo:hi] for i in range(NZ)], 1)

    def unpack(whole, table, group, lanes, count):
        lane = iota(whole.shape, 1) & 127
        parts = []
        for g in range(count):
            live = (lane >= lanes * g) & (lane < lanes * (g + 1))
            parts.append(jnp.where(live, whole, jnp.zeros_like(whole)))
        lhs = jnp.concatenate(parts, 0)
        return dot(lhs, table[...].reshape(NZ * 128, -1)).astype(bf16)

    def unpack_q(whole):
        return unpack(whole, eq, 48, 32, 3)

    def unpack_o(whole):
        return unpack(whole, eo, 16, 24, 5)

    jobs_o = [(0, o_t, "y", 0, 48, 32), (1, o_t, "x", 48, 32, 16)]
    jobs_q = [(2, q_t, "y", 0, 112, 64), (3, q_t, "x", 112, 32, 16)]
    jobs_s = [
        (4, o_s, "y", 0, 48, 32), (5, o_s, "x", 48, 32, 16),
        (6, q_s, "y", 0, 112, 64), (7, q_s, "x", 112, 32, 16),
    ]

    def view(job, phase, rel, half, core):
        _, ref, first, r, n, m = job
        lo, size = {"all": (r, n), "a": (r, m), "b": (r + m, n - m)}[half]
        rows = pl.ds(lo, size)
        axis = first if phase == 0 else ("x" if first == "y" else "y")
        if axis == "x":
            return ref.at[y if phase == 0 else slice(None), core, (x + rel) % NX, rows]
        return ref.at[(y + rel) % NY, core, x if phase == 0 else slice(None), rows]

    def hop(job, phase, rel, half, way, slot):
        first = job[2]
        axis = first if phase == 0 else ("x" if first == "y" else "y")
        step = 1 if way == 0 else 3
        dev = x_dev((x + step) % NX) if axis == "x" else seq_dev((y + step) % NY, z)
        ref = view(job, phase, rel, half, c)
        return pltpu.make_async_remote_copy(
            src_ref=ref, dst_ref=ref,
            send_sem=jsend_sem.at[job[0], phase * 4 + slot],
            recv_sem=jrecv_sem.at[job[0], phase * 4 + slot],
            device_id=dev,
        )

    def go(cp):
        cp.start()
        pending.append(cp)

    def first_step(job, phase):
        go(hop(job, phase, 0, "all", 0, 0))
        go(hop(job, phase, 0, "all", 1, 1))

    def pass_on(job, phase):
        hop(job, phase, 3, "all", 0, 0).wait_recv()
        go(hop(job, phase, 3, "a", 0, 2))
        hop(job, phase, 1, "all", 1, 1).wait_recv()
        go(hop(job, phase, 1, "b", 1, 3))

    def last_step(job, phase):
        hop(job, phase, 2, "a", 0, 2).wait_recv()
        hop(job, phase, 2, "b", 1, 3).wait_recv()

    def share(job, rel, core):
        ref = view(job, 1, rel, "all", core)
        return pltpu.make_async_remote_copy(
            src_ref=ref, dst_ref=ref,
            send_sem=jsend_sem.at[job[0], 8 + rel], recv_sem=jrecv_sem.at[job[0], 8 + rel],
            device_id={"dp": x * 2 + other},
        )

    def share_wait(job):
        for rel in range(4):
            share(job, rel, other).wait_recv()

    def out_rows(o_ref, yy):
        return jnp.concatenate([o_ref[yy, d % 2, d // 2] for d in range(HEADS)], 0)

    def qkv_rows(q_ref, yy):
        return jnp.concatenate([q_ref[yy, d % 2, d // 2] for d in range(8)], 0)

    def out_back(gated, o_ref):
        total = None
        for yy in range(NY):
            term = dot(gated[:, 256 * yy:256 * yy + OW], out_rows(o_ref, yy), NT)
            total = term if total is None else total + term
        return total.astype(bf16)

    def open_second(job):
        last_step(job, 0)
        first_step(job, 1)
        go(share(job, 0, c))

    def on_second(job):
        pass_on(job, 1)
        go(share(job, 3, c))
        go(share(job, 1, c))

    def end_second(job):
        last_step(job, 1)
        go(share(job, 2, c))

    def each(f, jobs, *args):
        for job in jobs:
            f(job, *args)

    ring_step(0, 0)
    ring_step(1, 0)
    ri, ci = iota((TOK, TOK), 0), iota((TOK, TOK), 1)
    pm[...] = jnp.where(ci == (ri & 1) * 128 + (ri >> 2) * 2 + ((ri >> 1) & 1), 1.0, 0.0).astype(bf16)
    pr[...] = jnp.where(
        ci == ((ri & 127) >> 1) * 4 + (ri >> 7) * 2 + (ri & 1), 1.0, 0.0
    ).astype(bf16)

    back[...] = jnp.where(
        ci == (ri & 1) * 128 + ((ri & 127) >> 1) * 2 + (ri >> 7), 1.0, 0.0
    ).astype(bf16)
    dqkv[...] = jnp.zeros((TOK, NY * QW), bf16)
    loads[4].wait()
    msend[...] = dot(pm[...], mid[...].reshape(TOK, D)).astype(bf16).reshape(NSEQ, 4, D)

    for step in range(8):
        if step > 0:
            ring_step(0, step)
            ring_step(1, step)
        send_mid(step, step + 1)
        lax.fori_loop(2 * step, 2 * step + 2, fill_o, 0)
        lax.fori_loop(2 * step, 2 * step + 2, fill_q, 0)
        if step == 1:
            for cp in loads[5:]:
                cp.wait()
        if step in (2, 3):
            f = step - 2
            normin[f * 128:(f + 1) * 128, :] = (live_cot(f) * mod[5]).astype(bf16)
        if step > 3:
            lax.fori_loop(step - 4, step - 3, own_norms, 0)
    ring_step(0, 8)
    o_t[y, c, x] = unpack_o(whole_of(z_t, 48, 64))
    each(first_step, jobs_o, 0)
    q_t[y, c, x] = unpack_q(whole_of(z_t, 0, 48))
    each(first_step, jobs_q, 0)
    send_mid(8, 20)
    ring_step(1, 8)
    o_s[y, c, x] = unpack_o(whole_of(z_s, 48, 64))
    q_s[y, c, x] = unpack_q(whole_of(z_s, 0, 48))
    each(pass_on, jobs_o, 0)
    each(open_second, jobs_o)
    send_mid(20, 32)
    each(pass_on, jobs_q, 0)
    send_mid(32, 44)
    each(on_second, jobs_o)
    each(open_second, jobs_q)
    send_mid(44, 63)
    each(end_second, jobs_o)
    each(first_step, jobs_s, 0)

    each(share_wait, jobs_o)
    dout[...] = out_back(normin, o_t)
    for b in range(2):
        part = dot(back[128 * b:128 * b + 128, :], dout[...])
        dsend[b] = part.astype(bf16).reshape(NSEQ, 2, HEADS * HP)
        scatter(dsend.at[b], drecv.at[b], 1 + b)
        drecv[b, s] = dsend[b, s]
    mrecv[s] = msend[s]
    each(on_second, jobs_q)
    each(end_second, jobs_q)

    def project(q_ref, lo, n):
        def body(yy, carry):
            lanes = pl.ds(pl.multiple_of(yy * QW, QW), QW)
            qkv[lo:lo + n, lanes] = dot(normin[lo:lo + n, :], qkv_rows(q_ref, yy)).astype(bf16)
            return carry
        lax.fori_loop(0, NY, body, 0)

    def project_back(q_ref, lo, n):
        acc[lo:lo + n, :] = jnp.zeros((n, D), f32)

        def body(yy, carry):
            lanes = pl.ds(pl.multiple_of(yy * QW, QW), QW)
            acc[lo:lo + n, :] += dot(dqkv[lo:lo + n, lanes], qkv_rows(q_ref, yy), NT)
            return carry
        lax.fori_loop(0, NY, body, 0)

    def attend(masked, lo=0, hi=2):
        def body(b, carry):
            rows = pl.ds(pl.multiple_of(b * 128, 128), 128)
            for h in range(HEADS):
                q = qkv[rows, head_at(h):head_at(h) + HDIM]
                k = qkv[rows, head_at(8 + h):head_at(8 + h) + HDIM]
                scores = dot(k, q, NT) * HDIM ** -0.5
                if masked:
                    scores = jnp.where(iota((128, 128), 0) < frames[0], scores, -1e30)
                e = jnp.exp(scores - jnp.max(scores, 0, keepdims=True))
                probs[b * HEADS + h] = e / jnp.sum(e, 0, keepdims=True)
            return carry
        lax.fori_loop(lo, hi, body, 0)

    def attend_back(lo, hi):
        def body(b, carry):
            rows = pl.ds(pl.multiple_of(b * 128, 128), 128)
            for h in range(HEADS):
                q = qkv[rows, head_at(h):head_at(h) + HDIM]
                k = qkv[rows, head_at(8 + h):head_at(8 + h) + HDIM]
                v = qkv[rows, head_at(16 + h):head_at(16 + h) + HDIM]
                up = dout[rows, HP * h:HP * h + HDIM]
                p = probs[b * HEADS + h]
                dv = dot(p.astype(bf16), up)
                dp_ = dot(v, up, NT)
                delta = jnp.sum(p * dp_, 0, keepdims=True)
                ds = (p * (dp_ - delta)).astype(bf16)
                dq = dot(ds, k, TN) * HDIM ** -0.5
                dk = dot(ds, q) * HDIM ** -0.5
                dqkv[rows, head_at(h):head_at(h) + HDIM] = dq.astype(bf16)
                dqkv[rows, head_at(8 + h):head_at(8 + h) + HDIM] = dk.astype(bf16)
                dqkv[rows, head_at(16 + h):head_at(16 + h) + HDIM] = dv.astype(bf16)
            return carry
        lax.fori_loop(lo, hi, body, 0)

    wait_scatter(mrecv, arecv_sem, 0)
    acc[...] = dot(pr[...], mrecv[...].reshape(TOK, D))

    def patch_norm(i, carry):
        rows = pl.ds(pl.multiple_of(i * 64, 64), 64)
        normed, _ = norm_stats(acc[rows, :])
        normin[rows, :] = (normed * (1.0 + mod[4]) + mod[3]).astype(bf16)
        return carry
    lax.fori_loop(0, 4, patch_norm, 0)
    each(pass_on, jobs_s, 0)
    each(open_second, jobs_s)
    each(share_wait, jobs_q)
    for b in range(2):
        project(q_t, 128 * b, 128)
        attend(True, b, b + 1)
        wait_scatter(drecv.at[b], arecv_sem, 1 + b)
        dout[128 * b:128 * b + 128, :] = drecv[b].reshape(128, HEADS * HP)
        attend_back(b, b + 1)
        project_back(q_t, 128 * b, 128)
        rsend[b] = acc[128 * b:128 * b + 128, :].astype(bf16).reshape(NSEQ, 2, D)
        scatter(rsend.at[b], rrecv.at[b], 3 + b)
        rrecv[b, s] = rsend[b, s]
        if b == 0:
            each(on_second, jobs_s)

    each(end_second, jobs_s)

    def frame_norm(i, carry):
        rows = pl.ds(pl.multiple_of(i * 64, 64), 64)
        normin[rows, :] = (nm_s[rows, :] * (1.0 + mod[1]) + mod[0]).astype(bf16)
        return carry
    lax.fori_loop(0, 4, frame_norm, 0)
    each(share_wait, jobs_s)
    project(q_s, 0, TOK)
    attend(False)

    for cp in pending:
        cp.wait_send()
    wait_scatter(msend, asend_sem, 0)
    for b in range(2):
        wait_scatter(dsend.at[b], asend_sem, 1 + b)

    wait_scatter(rrecv.at[0], arecv_sem, 3)
    acc[...] = dot(back[:, 0:128], rrecv[0].reshape(128, D))
    wait_scatter(rrecv.at[1], arecv_sem, 4)
    acc[...] += dot(back[:, 128:256], rrecv[1].reshape(128, D))

    def mid_grad(i, carry):
        rows = pl.ds(pl.multiple_of(i * 64, 64), 64)
        f, r = i // 2, pl.ds(pl.multiple_of((i % 2) * 64, 64), 64)
        cell = iota((64, 1), 0) * 0 + (2 * s + f)
        masked = jnp.where(cell < frames[0], cot[f, r, :].astype(f32), 0.0)
        grad = masked + norm_back(acc[rows, :], nm_t[rows, :], rs_t[rows, :], 1.0 + mod[4])
        dmid[rows, :] = grad
        normin[rows, :] = (grad * mod[2]).astype(bf16)
        return carry
    lax.fori_loop(0, 4, mid_grad, 0)
    dout[...] = out_back(normin, o_s)
    attend_back(0, 2)
    project_back(q_s, 0, TOK)

    def last_grad(i, carry):
        rows = pl.ds(pl.multiple_of(i * 64, 64), 64)
        f, r = i // 2, pl.ds(pl.multiple_of((i % 2) * 64, 64), 64)
        dnorm = acc[rows, :].astype(bf16).astype(f32)
        grad = norm_back(dnorm, nm_s[rows, :], rs_s[rows, :], 1.0 + mod[1])
        result[f, r, :] = (dmid[rows, :] + grad).astype(bf16)
        return carry
    lax.fori_loop(0, 4, last_grad, 0)

    for b in range(2):
        wait_scatter(rsend.at[b], asend_sem, 3 + b)


def per_device(inputs, mid_inputs, cotangent, modulation, frames, qkv_s, out_s, qkv_t, out_t):
    vmem, hbm = pl.BlockSpec(memory_space=pltpu.VMEM), pl.BlockSpec(memory_space=pltpu.HBM)
    dma = pltpu.SemaphoreType.DMA
    out = pl.pallas_call(
        kernel,
        out_shape=jax.ShapeDtypeStruct((2, 128, D), bf16),
        in_specs=[hbm] * 4 + [pl.BlockSpec(memory_space=pltpu.SMEM)] + [hbm] * 4,
        out_specs=vmem,
        scratch_shapes=[
            pltpu.VMEM((2, 128, D), bf16),
            pltpu.VMEM((2, 128, D), bf16),
            pltpu.VMEM((2, 128, D), bf16),
            pltpu.VMEM((6, 1, D), f32),
            pltpu.VMEM((27, 144), bf16),
            pltpu.VMEM((18, 72), bf16),
            pltpu.VMEM((27, 144), bf16),
            pltpu.VMEM((18, 72), bf16),
            dma((8,)),
            pltpu.VMEM((NZ, 64, 128), bf16),
            pltpu.VMEM((NZ, 64, 128), bf16),
            pltpu.VMEM((NZ, 128, QW), bf16),
            pltpu.VMEM((NZ, 128, OW), bf16),
            pltpu.VMEM((NY, 2, NX, 144, QW), bf16),
            pltpu.VMEM((NY, 2, NX, HP, OW), bf16),
            pltpu.VMEM((NY, 2, NX, 144, QW), bf16),
            pltpu.VMEM((NY, 2, NX, HP, OW), bf16),
            pltpu.VMEM((NSEQ, 4, D), bf16),
            pltpu.VMEM((NSEQ, 4, D), bf16),
            pltpu.VMEM((2, NSEQ, 2, HEADS * HP), bf16),
            pltpu.VMEM((2, NSEQ, 2, HEADS * HP), bf16),
            pltpu.VMEM((2, NSEQ, 2, D), bf16),
            pltpu.VMEM((2, NSEQ, 2, D), bf16),
            pltpu.VMEM((TOK, TOK), bf16),
            pltpu.VMEM((TOK, TOK), bf16),
            pltpu.VMEM((TOK, TOK), bf16),
            pltpu.VMEM((TOK, D), bf16),
            pltpu.VMEM((TOK, NY * QW), bf16),
            pltpu.VMEM((TOK, NY * QW), bf16),
            pltpu.VMEM((TOK, HEADS * HP), bf16),
            pltpu.VMEM((2 * HEADS, 128, 128), f32),
            pltpu.VMEM((TOK, D), f32),
            pltpu.VMEM((TOK, D), f32),
            pltpu.VMEM((TOK, 1), f32),
            pltpu.VMEM((TOK, D), f32),
            pltpu.VMEM((TOK, 1), f32),
            pltpu.VMEM((TOK, D), f32),
            dma((2, 2, 8)), dma((2, 2, 8)), dma((8, 12)), dma((8, 12)), dma((5,)), dma((5,)),
        ],
        compiler_params=pltpu.CompilerParams(
            collective_id=0, has_side_effects=True, vmem_limit_bytes=56 * 1024 * 1024
        ),
        name="blocks_grad",
    )(
        inputs[0], mid_inputs[0], cotangent[0], modulation.reshape(6, 1, D), frames,
        qkv_s.T, out_s.T, qkv_t.T, out_t.T,
    )
    return out[None]


def solution(mesh):
    big = P("dp", "seq", None, None)
    weight = P("dp", "seq")
    return jax.shard_map(
        per_device,
        mesh=mesh,
        in_specs=(big, big, big, P("dp", None, None), P("dp")) + (weight,) * 4,
        out_specs=big,
        check_vma=False,
    )
```

```python
import jax
import jax.numpy as jnp
from jax import lax
from jax.experimental import pallas as pl
from jax.experimental.pallas import tpu as pltpu
from jax.sharding import PartitionSpec as P

HDIM = 72
HEADS = 8
D = 1152
EPS = 1e-06
TOK = 256
NY, NX, NZ = 4, 4, 16
NSEQ = NY * NZ
QW = 512
OW = 384
HP = 80
f32, bf16 = jnp.float32, jnp.bfloat16

NN = (((1,), (0,)), ((), ()))
NT = (((1,), (1,)), ((), ()))
TN = (((0,), (0,)), ((), ()))


def dot(a, b, dims=NN):
    return lax.dot_general(a, b, dims, preferred_element_type=f32)


def iota(shape, axis):
    return lax.broadcasted_iota(jnp.int32, shape, axis)


def head_at(n):
    return (n // 6) * QW + (n % 6) * HDIM


def norm_stats(x):
    center = jnp.mean(x, -1, keepdims=True)
    diff = x - center
    spread = jnp.mean(diff * diff, -1, keepdims=True)
    rstd = lax.rsqrt(spread + EPS)
    return diff * rstd, rstd


def norm_back(dnorm, normed, rstd, gain):
    g = dnorm * gain
    return rstd * (
        g
        - jnp.mean(g, -1, keepdims=True)
        - normed * jnp.mean(g * normed, -1, keepdims=True)
    )


def kernel(
    inp_hbm, mid_hbm, cot_hbm, mod_hbm, frames, qkv_s_hbm, out_s_hbm, qkv_t_hbm, out_t_hbm, result,
    inp, mid, cot, mod, qkv_s, out_s, qkv_t, out_t, load_sem,
    z_t, z_s, eq, eo, q_t, o_t, q_s, o_s,
    msend, mrecv, dsend, drecv, rsend, rrecv,
    pm, pr, back, normin, qkv, dqkv, dout, probs, acc, nm_t, rs_t, nm_s, rs_s, dmid,
    zsend_sem, zrecv_sem, jsend_sem, jrecv_sem, asend_sem, arecv_sem,
):
    dp = lax.axis_index("dp")
    s = lax.axis_index("seq")
    x, c = dp // 2, dp % 2
    y, z = s // NZ, s % NZ
    other = 1 - c
    pending = []

    loads = [
        pltpu.make_async_copy(src, dst, load_sem.at[i])
        for i, (src, dst) in enumerate((
            (qkv_t_hbm, qkv_t), (out_t_hbm, out_t), (qkv_s_hbm, qkv_s), (out_s_hbm, out_s),
            (mid_hbm, mid), (cot_hbm, cot), (mod_hbm, mod), (inp_hbm, inp),
        ))
    ]
    for cp in loads:
        cp.start()

    def seq_dev(yy, zz):
        return {"seq": yy * NZ + zz}

    def x_dev(xx):
        return {"dp": xx * 2 + c}

    far = [(8, dy) for dy in range(NY)]
    near = [(dz, dy) for dy in range(NY) for dz in (0, 1)]
    beside = [(0, dy) for dy in range(1, NY)]

    def peer(dz, dy):
        return lax.rem(y + dy, NY) * NZ + lax.rem(z + dz, NZ)

    def each_peer(f):
        for dz, dy in far:
            f(peer(dz, dy))

        def body(i, carry):
            at = (lax.rem(z + 7 - i, NZ), lax.rem(z + NZ - 7 + i, NZ))
            for way, dy in near:
                f(lax.rem(y + dy, NY) * NZ + at[way])
            return carry
        lax.fori_loop(0, 7, body, 0)
        for dz, dy in beside:
            f(peer(dz, dy))

    barrier = pltpu.get_barrier_semaphore()

    for xx in ((x + 1) % NX, (x + 3) % NX):
        pl.semaphore_signal(barrier, inc=1, device_id=x_dev(xx))
    pl.semaphore_signal(barrier, inc=1, device_id={"dp": x * 2 + other})
    each_peer(lambda to: pl.semaphore_signal(barrier, inc=1, device_id={"seq": to}))

    def pack(ref, group, lanes):
        w = ref[...]
        n, rows = w.shape
        total = None
        for g in range(-(-rows // group)):
            hit = iota((n, 128), 1) == iota((n, 128), 0) + lanes * g
            part = dot(w, jnp.where(hit, 1.0, 0.0).astype(bf16), TN)[group * g:group * (g + 1)]
            if part.shape[0] < group:
                part = jnp.concatenate([part, jnp.zeros((group - part.shape[0], 128), f32)], 0)
            total = part if total is None else total + part
        return total.astype(bf16)

    for cp in loads[:4]:
        cp.wait()
    for ref, q, o in ((z_t, qkv_t, out_t), (z_s, qkv_s, out_s)):
        ref[z, 0:48] = pack(q, 48, 32)
        ref[z, 48:64] = pack(o, 16, 24)

    pl.semaphore_wait(barrier, NSEQ - 1 + 3)

    def zcopy(kind, block, way, step):
        to = lax.rem(z + 1, NZ) if way == 0 else lax.rem(z + NZ - 1, NZ)
        ref = (z_t, z_s)[kind].at[block]
        return pltpu.make_async_remote_copy(
            src_ref=ref, dst_ref=ref,
            send_sem=zsend_sem.at[kind, way, step], recv_sem=zrecv_sem.at[kind, way, step],
            device_id=seq_dev(y, to),
        )

    def ring_step(kind, step):
        for way, block in ((0, lax.rem(z + NZ - step, NZ)), (1, lax.rem(z + step, NZ))):
            if step > 0 and not (way == 1 and step == 8):
                zcopy(kind, block, way, step - 1).wait_recv()
            if step < 8 - way:
                cp = zcopy(kind, block, way, step)
                cp.start()
                pending.append(cp)

    def send_to(src, dst, k, to):
        pltpu.make_async_remote_copy(
            src_ref=src.at[to], dst_ref=dst.at[s],
            send_sem=asend_sem.at[k], recv_sem=arecv_sem.at[k],
            device_id={"seq": to},
        ).start()

    def scatter(src, dst, k):
        each_peer(lambda to: send_to(src, dst, k, to))

    order = far + [(d, dy) for m in range(7, 0, -1) for dy in range(NY) for d in (m, NZ - m)] + beside

    def send_mid(lo, hi):
        for dz, dy in order[lo:hi]:
            send_to(msend, mrecv, 0, peer(dz, dy))

    def wait_scatter(ref, sem, k):
        part = ref.at[pl.ds(0, NSEQ - 1)]
        pltpu.make_async_copy(part, part, sem.at[k]).wait()

    def fill_q(zz, carry):
        lane, col = iota((128, QW), 0), iota((128, QW), 1)
        at = lane & 31
        hit = (at < 27) & (lane < 96) & (col == at + 27 * zz)
        eq[zz] = jnp.where(hit, 1.0, 0.0).astype(bf16)
        return carry

    def fill_o(zz, carry):
        lane, col = iota((128, OW), 0), iota((128, OW), 1)
        at = lane
        for g in range(1, 5):
            at = jnp.where(lane >= 24 * g, lane - 24 * g, at)
        hit = (at < 18) & (col == at + 18 * zz + 32 * y)
        eo[zz] = jnp.where(hit, 1.0, 0.0).astype(bf16)
        return carry

    def own_norms(i, carry):
        rows = pl.ds(pl.multiple_of(i * 64, 64), 64)
        f, r = i // 2, pl.ds(pl.multiple_of((i % 2) * 64, 64), 64)
        nm_t[rows, :], rs_t[rows, :] = norm_stats(mid[f, r, :].astype(f32))
        nm_s[rows, :], rs_s[rows, :] = norm_stats(inp[f, r, :].astype(f32))
        return carry

    def live_cot(f):
        cell = iota((128, 1), 0) * 0 + (2 * s + f)
        return jnp.where(cell < frames[0], cot[f].astype(f32), 0.0)

    def whole_of(ref, lo, hi):
        return jnp.concatenate([ref[i, lo:hi] for i in range(NZ)], 1)

    def unpack(whole, table, group, lanes, count):
        lane = iota(whole.shape, 1) & 127
        parts = []
        for g in range(count):
            live = (lane >= lanes * g) & (lane < lanes * (g + 1))
            parts.append(jnp.where(live, whole, jnp.zeros_like(whole)))
        lhs = jnp.concatenate(parts, 0)
        return dot(lhs, table[...].reshape(NZ * 128, -1)).astype(bf16)

    def unpack_q(whole):
        return unpack(whole, eq, 48, 32, 3)

    def unpack_o(whole):
        return unpack(whole, eo, 16, 24, 5)

    jobs_o = [(0, o_t, "y", 0, 48, 32), (1, o_t, "x", 48, 32, 16)]
    jobs_q = [(2, q_t, "y", 0, 112, 64), (3, q_t, "x", 112, 32, 16)]
    jobs_s = [
        (4, o_s, "y", 0, 48, 32), (5, o_s, "x", 48, 32, 16),
        (6, q_s, "y", 0, 112, 64), (7, q_s, "x", 112, 32, 16),
    ]

    def view(job, phase, rel, half, core):
        _, ref, first, r, n, m = job
        lo, size = {"all": (r, n), "a": (r, m), "b": (r + m, n - m)}[half]
        rows = pl.ds(lo, size)
        axis = first if phase == 0 else ("x" if first == "y" else "y")
        if axis == "x":
            return ref.at[y if phase == 0 else slice(None), core, (x + rel) % NX, rows]
        return ref.at[(y + rel) % NY, core, x if phase == 0 else slice(None), rows]

    def hop(job, phase, rel, half, way, slot):
        first = job[2]
        axis = first if phase == 0 else ("x" if first == "y" else "y")
        step = 1 if way == 0 else 3
        dev = x_dev((x + step) % NX) if axis == "x" else seq_dev((y + step) % NY, z)
        ref = view(job, phase, rel, half, c)
        return pltpu.make_async_remote_copy(
            src_ref=ref, dst_ref=ref,
            send_sem=jsend_sem.at[job[0], phase * 4 + slot],
            recv_sem=jrecv_sem.at[job[0], phase * 4 + slot],
            device_id=dev,
        )

    def go(cp):
        cp.start()
        pending.append(cp)

    def first_step(job, phase):
        go(hop(job, phase, 0, "all", 0, 0))
        go(hop(job, phase, 0, "all", 1, 1))

    def pass_on(job, phase):
        hop(job, phase, 3, "all", 0, 0).wait_recv()
        go(hop(job, phase, 3, "a", 0, 2))
        hop(job, phase, 1, "all", 1, 1).wait_recv()
        go(hop(job, phase, 1, "b", 1, 3))

    def last_step(job, phase):
        hop(job, phase, 2, "a", 0, 2).wait_recv()
        hop(job, phase, 2, "b", 1, 3).wait_recv()

    def share(job, rel, core):
        ref = view(job, 1, rel, "all", core)
        return pltpu.make_async_remote_copy(
            src_ref=ref, dst_ref=ref,
            send_sem=jsend_sem.at[job[0], 8 + rel], recv_sem=jrecv_sem.at[job[0], 8 + rel],
            device_id={"dp": x * 2 + other},
        )

    def share_wait(job):
        for rel in range(4):
            share(job, rel, other).wait_recv()

    def out_rows(o_ref, yy):
        return jnp.concatenate([o_ref[yy, d % 2, d // 2] for d in range(HEADS)], 0)

    def qkv_rows(q_ref, yy):
        return jnp.concatenate([q_ref[yy, d % 2, d // 2] for d in range(8)], 0)

    def out_back(gated, o_ref):
        total = None
        for yy in range(NY):
            term = dot(gated[:, 256 * yy:256 * yy + OW], out_rows(o_ref, yy), NT)
            total = term if total is None else total + term
        return total.astype(bf16)

    def open_second(job):
        last_step(job, 0)
        first_step(job, 1)
        go(share(job, 0, c))

    def on_second(job):
        pass_on(job, 1)
        go(share(job, 3, c))
        go(share(job, 1, c))

    def end_second(job):
        last_step(job, 1)
        go(share(job, 2, c))

    def each(f, jobs, *args):
        for job in jobs:
            f(job, *args)

    ring_step(0, 0)
    ring_step(1, 0)
    ri, ci = iota((TOK, TOK), 0), iota((TOK, TOK), 1)
    pm[...] = jnp.where(ci == (ri & 1) * 128 + (ri >> 2) * 2 + ((ri >> 1) & 1), 1.0, 0.0).astype(bf16)
    pr[...] = jnp.where(
        ci == ((ri & 127) >> 1) * 4 + (ri >> 7) * 2 + (ri & 1), 1.0, 0.0
    ).astype(bf16)

    back[...] = jnp.where(
        ci == (ri & 1) * 128 + ((ri & 127) >> 1) * 2 + (ri >> 7), 1.0, 0.0
    ).astype(bf16)
    dqkv[...] = jnp.zeros((TOK, NY * QW), bf16)
    loads[4].wait()
    msend[...] = dot(pm[...], mid[...].reshape(TOK, D)).astype(bf16).reshape(NSEQ, 4, D)

    for step in range(8):
        if step > 0:
            ring_step(0, step)
            ring_step(1, step)
        send_mid(step, step + 1)
        lax.fori_loop(2 * step, 2 * step + 2, fill_o, 0)
        lax.fori_loop(2 * step, 2 * step + 2, fill_q, 0)
        if step == 1:
            for cp in loads[5:]:
                cp.wait()
        if step in (2, 3):
            f = step - 2
            normin[f * 128:(f + 1) * 128, :] = (live_cot(f) * mod[5]).astype(bf16)
        if step > 3:
            lax.fori_loop(step - 4, step - 3, own_norms, 0)
    ring_step(0, 8)
    o_t[y, c, x] = unpack_o(whole_of(z_t, 48, 64))
    each(first_step, jobs_o, 0)
    q_t[y, c, x] = unpack_q(whole_of(z_t, 0, 48))
    each(first_step, jobs_q, 0)
    send_mid(8, 20)
    ring_step(1, 8)
    o_s[y, c, x] = unpack_o(whole_of(z_s, 48, 64))
    q_s[y, c, x] = unpack_q(whole_of(z_s, 0, 48))
    each(pass_on, jobs_o, 0)
    each(open_second, jobs_o)
    send_mid(20, 32)
    each(pass_on, jobs_q, 0)
    send_mid(32, 44)
    each(on_second, jobs_o)
    each(open_second, jobs_q)
    send_mid(44, 63)
    each(end_second, jobs_o)
    each(first_step, jobs_s, 0)

    each(share_wait, jobs_o)
    dout[...] = out_back(normin, o_t)
    for b in range(2):
        part = dot(back[128 * b:128 * b + 128, :], dout[...])
        dsend[b] = part.astype(bf16).reshape(NSEQ, 2, HEADS * HP)
        scatter(dsend.at[b], drecv.at[b], 1 + b)
        drecv[b, s] = dsend[b, s]
        if b == 0:
            each(on_second, jobs_q)
    mrecv[s] = msend[s]
    each(end_second, jobs_q)

    def project(q_ref, lo, n):
        def body(yy, carry):
            lanes = pl.ds(pl.multiple_of(yy * QW, QW), QW)
            qkv[lo:lo + n, lanes] = dot(normin[lo:lo + n, :], qkv_rows(q_ref, yy)).astype(bf16)
            return carry
        lax.fori_loop(0, NY, body, 0)

    def project_back(q_ref, lo, n):
        acc[lo:lo + n, :] = jnp.zeros((n, D), f32)

        def body(yy, carry):
            lanes = pl.ds(pl.multiple_of(yy * QW, QW), QW)
            acc[lo:lo + n, :] += dot(dqkv[lo:lo + n, lanes], qkv_rows(q_ref, yy), NT)
            return carry
        lax.fori_loop(0, NY, body, 0)

    def attend(masked, lo=0, hi=2):
        def body(b, carry):
            rows = pl.ds(pl.multiple_of(b * 128, 128), 128)
            for h in range(HEADS):
                q = qkv[rows, head_at(h):head_at(h) + HDIM]
                k = qkv[rows, head_at(8 + h):head_at(8 + h) + HDIM]
                scores = dot(k, q, NT) * HDIM ** -0.5
                if masked:
                    scores = jnp.where(iota((128, 128), 0) < frames[0], scores, -1e30)
                e = jnp.exp(scores - jnp.max(scores, 0, keepdims=True))
                probs[b * HEADS + h] = e / jnp.sum(e, 0, keepdims=True)
            return carry
        lax.fori_loop(lo, hi, body, 0)

    def attend_back(lo, hi):
        def body(b, carry):
            rows = pl.ds(pl.multiple_of(b * 128, 128), 128)
            for h in range(HEADS):
                q = qkv[rows, head_at(h):head_at(h) + HDIM]
                k = qkv[rows, head_at(8 + h):head_at(8 + h) + HDIM]
                v = qkv[rows, head_at(16 + h):head_at(16 + h) + HDIM]
                up = dout[rows, HP * h:HP * h + HDIM]
                p = probs[b * HEADS + h]
                dv = dot(p.astype(bf16), up)
                dp_ = dot(v, up, NT)
                delta = jnp.sum(p * dp_, 0, keepdims=True)
                ds = (p * (dp_ - delta)).astype(bf16)
                dq = dot(ds, k, TN) * HDIM ** -0.5
                dk = dot(ds, q) * HDIM ** -0.5
                dqkv[rows, head_at(h):head_at(h) + HDIM] = dq.astype(bf16)
                dqkv[rows, head_at(8 + h):head_at(8 + h) + HDIM] = dk.astype(bf16)
                dqkv[rows, head_at(16 + h):head_at(16 + h) + HDIM] = dv.astype(bf16)
            return carry
        lax.fori_loop(lo, hi, body, 0)

    wait_scatter(mrecv, arecv_sem, 0)
    acc[...] = dot(pr[...], mrecv[...].reshape(TOK, D))

    def patch_norm(i, carry):
        rows = pl.ds(pl.multiple_of(i * 64, 64), 64)
        normed, _ = norm_stats(acc[rows, :])
        normin[rows, :] = (normed * (1.0 + mod[4]) + mod[3]).astype(bf16)
        return carry
    lax.fori_loop(0, 4, patch_norm, 0)
    each(pass_on, jobs_s, 0)
    each(open_second, jobs_s)
    each(share_wait, jobs_q)
    for b in range(2):
        project(q_t, 128 * b, 128)
        attend(True, b, b + 1)
        if b == 1:
            each(on_second, jobs_s)
        wait_scatter(drecv.at[b], arecv_sem, 1 + b)
        dout[128 * b:128 * b + 128, :] = drecv[b].reshape(128, HEADS * HP)
        attend_back(b, b + 1)
        project_back(q_t, 128 * b, 128)
        rsend[b] = acc[128 * b:128 * b + 128, :].astype(bf16).reshape(NSEQ, 2, D)
        scatter(rsend.at[b], rrecv.at[b], 3 + b)
        rrecv[b, s] = rsend[b, s]

    each(end_second, jobs_s)

    def frame_norm(i, carry):
        rows = pl.ds(pl.multiple_of(i * 64, 64), 64)
        normin[rows, :] = (nm_s[rows, :] * (1.0 + mod[1]) + mod[0]).astype(bf16)
        return carry
    lax.fori_loop(0, 4, frame_norm, 0)
    each(share_wait, jobs_s)
    project(q_s, 0, TOK)
    attend(False)

    for cp in pending:
        cp.wait_send()
    wait_scatter(msend, asend_sem, 0)
    for b in range(2):
        wait_scatter(dsend.at[b], asend_sem, 1 + b)

    wait_scatter(rrecv.at[0], arecv_sem, 3)
    acc[...] = dot(back[:, 0:128], rrecv[0].reshape(128, D))
    wait_scatter(rrecv.at[1], arecv_sem, 4)
    acc[...] += dot(back[:, 128:256], rrecv[1].reshape(128, D))

    def mid_grad(i, carry):
        rows = pl.ds(pl.multiple_of(i * 64, 64), 64)
        f, r = i // 2, pl.ds(pl.multiple_of((i % 2) * 64, 64), 64)
        cell = iota((64, 1), 0) * 0 + (2 * s + f)
        masked = jnp.where(cell < frames[0], cot[f, r, :].astype(f32), 0.0)
        grad = masked + norm_back(acc[rows, :], nm_t[rows, :], rs_t[rows, :], 1.0 + mod[4])
        dmid[rows, :] = grad
        normin[rows, :] = (grad * mod[2]).astype(bf16)
        return carry
    lax.fori_loop(0, 4, mid_grad, 0)
    dout[...] = out_back(normin, o_s)
    attend_back(0, 2)
    project_back(q_s, 0, TOK)

    def last_grad(i, carry):
        rows = pl.ds(pl.multiple_of(i * 64, 64), 64)
        f, r = i // 2, pl.ds(pl.multiple_of((i % 2) * 64, 64), 64)
        dnorm = acc[rows, :].astype(bf16).astype(f32)
        grad = norm_back(dnorm, nm_s[rows, :], rs_s[rows, :], 1.0 + mod[1])
        result[f, r, :] = (dmid[rows, :] + grad).astype(bf16)
        return carry
    lax.fori_loop(0, 4, last_grad, 0)

    for b in range(2):
        wait_scatter(rsend.at[b], asend_sem, 3 + b)


def per_device(inputs, mid_inputs, cotangent, modulation, frames, qkv_s, out_s, qkv_t, out_t):
    vmem, hbm = pl.BlockSpec(memory_space=pltpu.VMEM), pl.BlockSpec(memory_space=pltpu.HBM)
    dma = pltpu.SemaphoreType.DMA
    out = pl.pallas_call(
        kernel,
        out_shape=jax.ShapeDtypeStruct((2, 128, D), bf16),
        in_specs=[hbm] * 4 + [pl.BlockSpec(memory_space=pltpu.SMEM)] + [hbm] * 4,
        out_specs=vmem,
        scratch_shapes=[
            pltpu.VMEM((2, 128, D), bf16),
            pltpu.VMEM((2, 128, D), bf16),
            pltpu.VMEM((2, 128, D), bf16),
            pltpu.VMEM((6, 1, D), f32),
            pltpu.VMEM((27, 144), bf16),
            pltpu.VMEM((18, 72), bf16),
            pltpu.VMEM((27, 144), bf16),
            pltpu.VMEM((18, 72), bf16),
            dma((8,)),
            pltpu.VMEM((NZ, 64, 128), bf16),
            pltpu.VMEM((NZ, 64, 128), bf16),
            pltpu.VMEM((NZ, 128, QW), bf16),
            pltpu.VMEM((NZ, 128, OW), bf16),
            pltpu.VMEM((NY, 2, NX, 144, QW), bf16),
            pltpu.VMEM((NY, 2, NX, HP, OW), bf16),
            pltpu.VMEM((NY, 2, NX, 144, QW), bf16),
            pltpu.VMEM((NY, 2, NX, HP, OW), bf16),
            pltpu.VMEM((NSEQ, 4, D), bf16),
            pltpu.VMEM((NSEQ, 4, D), bf16),
            pltpu.VMEM((2, NSEQ, 2, HEADS * HP), bf16),
            pltpu.VMEM((2, NSEQ, 2, HEADS * HP), bf16),
            pltpu.VMEM((2, NSEQ, 2, D), bf16),
            pltpu.VMEM((2, NSEQ, 2, D), bf16),
            pltpu.VMEM((TOK, TOK), bf16),
            pltpu.VMEM((TOK, TOK), bf16),
            pltpu.VMEM((TOK, TOK), bf16),
            pltpu.VMEM((TOK, D), bf16),
            pltpu.VMEM((TOK, NY * QW), bf16),
            pltpu.VMEM((TOK, NY * QW), bf16),
            pltpu.VMEM((TOK, HEADS * HP), bf16),
            pltpu.VMEM((2 * HEADS, 128, 128), f32),
            pltpu.VMEM((TOK, D), f32),
            pltpu.VMEM((TOK, D), f32),
            pltpu.VMEM((TOK, 1), f32),
            pltpu.VMEM((TOK, D), f32),
            pltpu.VMEM((TOK, 1), f32),
            pltpu.VMEM((TOK, D), f32),
            dma((2, 2, 8)), dma((2, 2, 8)), dma((8, 12)), dma((8, 12)), dma((5,)), dma((5,)),
        ],
        compiler_params=pltpu.CompilerParams(
            collective_id=0, has_side_effects=True, vmem_limit_bytes=56 * 1024 * 1024
        ),
        name="blocks_grad",
    )(
        inputs[0], mid_inputs[0], cotangent[0], modulation.reshape(6, 1, D), frames,
        qkv_s.T, out_s.T, qkv_t.T, out_t.T,
    )
    return out[None]


def solution(mesh):
    big = P("dp", "seq", None, None)
    weight = P("dp", "seq")
    return jax.shard_map(
        per_device,
        mesh=mesh,
        in_specs=(big, big, big, P("dp", None, None), P("dp")) + (weight,) * 4,
        out_specs=big,
        check_vma=False,
    )
```

```python
import jax
import jax.numpy as jnp
from jax import lax
from jax.experimental import pallas as pl
from jax.experimental.pallas import tpu as pltpu
from jax.sharding import PartitionSpec as P

HDIM = 72
HEADS = 8
D = 1152
EPS = 1e-06
TOK = 256
NY, NX, NZ = 4, 4, 16
NSEQ = NY * NZ
QW = 512
OW = 384
HP = 80
f32, bf16 = jnp.float32, jnp.bfloat16

NN = (((1,), (0,)), ((), ()))
NT = (((1,), (1,)), ((), ()))
TN = (((0,), (0,)), ((), ()))


def dot(a, b, dims=NN):
    return lax.dot_general(a, b, dims, preferred_element_type=f32)


def iota(shape, axis):
    return lax.broadcasted_iota(jnp.int32, shape, axis)


def head_at(n):
    return (n // 6) * QW + (n % 6) * HDIM


def norm_stats(x):
    center = jnp.mean(x, -1, keepdims=True)
    diff = x - center
    spread = jnp.mean(diff * diff, -1, keepdims=True)
    rstd = lax.rsqrt(spread + EPS)
    return diff * rstd, rstd


def norm_back(dnorm, normed, rstd, gain):
    g = dnorm * gain
    return rstd * (
        g
        - jnp.mean(g, -1, keepdims=True)
        - normed * jnp.mean(g * normed, -1, keepdims=True)
    )


def kernel(
    inp_hbm, mid_hbm, cot_hbm, mod_hbm, frames, qkv_s_hbm, out_s_hbm, qkv_t_hbm, out_t_hbm, result,
    inp, mid, cot, mod, qkv_s, out_s, qkv_t, out_t, load_sem,
    z_t, z_s, eq, eo, q_t, o_t, q_s, o_s,
    msend, mrecv, dsend, drecv, rsend, rrecv,
    pm, pr, back, normin, qkv, dqkv, dout, probs, acc, nm_t, rs_t, nm_s, rs_s, dmid,
    zsend_sem, zrecv_sem, jsend_sem, jrecv_sem, asend_sem, arecv_sem,
):
    dp = lax.axis_index("dp")
    s = lax.axis_index("seq")
    x, c = dp // 2, dp % 2
    y, z = s // NZ, s % NZ
    other = 1 - c
    pending = []

    loads = [
        pltpu.make_async_copy(src, dst, load_sem.at[i])
        for i, (src, dst) in enumerate((
            (qkv_t_hbm, qkv_t), (out_t_hbm, out_t), (qkv_s_hbm, qkv_s), (out_s_hbm, out_s),
            (mid_hbm, mid), (cot_hbm, cot), (mod_hbm, mod), (inp_hbm, inp),
        ))
    ]
    for cp in loads:
        cp.start()

    def seq_dev(yy, zz):
        return {"seq": yy * NZ + zz}

    def x_dev(xx):
        return {"dp": xx * 2 + c}

    far = [(8, dy) for dy in range(NY)]
    near = [(dz, dy) for dy in range(NY) for dz in (0, 1)]
    beside = [(0, dy) for dy in range(1, NY)]

    def peer(dz, dy):
        return lax.rem(y + dy, NY) * NZ + lax.rem(z + dz, NZ)

    def each_peer(f):
        for dz, dy in far:
            f(peer(dz, dy))

        def body(i, carry):
            at = (lax.rem(z + 7 - i, NZ), lax.rem(z + NZ - 7 + i, NZ))
            for way, dy in near:
                f(lax.rem(y + dy, NY) * NZ + at[way])
            return carry
        lax.fori_loop(0, 7, body, 0)
        for dz, dy in beside:
            f(peer(dz, dy))

    barrier = pltpu.get_barrier_semaphore()

    for xx in ((x + 1) % NX, (x + 3) % NX):
        pl.semaphore_signal(barrier, inc=1, device_id=x_dev(xx))
    pl.semaphore_signal(barrier, inc=1, device_id={"dp": x * 2 + other})
    each_peer(lambda to: pl.semaphore_signal(barrier, inc=1, device_id={"seq": to}))

    def pack(ref, group, lanes):
        w = ref[...]
        n, rows = w.shape
        total = None
        for g in range(-(-rows // group)):
            hit = iota((n, 128), 1) == iota((n, 128), 0) + lanes * g
            part = dot(w, jnp.where(hit, 1.0, 0.0).astype(bf16), TN)[group * g:group * (g + 1)]
            if part.shape[0] < group:
                part = jnp.concatenate([part, jnp.zeros((group - part.shape[0], 128), f32)], 0)
            total = part if total is None else total + part
        return total.astype(bf16)

    for cp in loads[:4]:
        cp.wait()
    for ref, q, o in ((z_t, qkv_t, out_t), (z_s, qkv_s, out_s)):
        ref[z, 0:48] = pack(q, 48, 32)
        ref[z, 48:64] = pack(o, 16, 24)

    pl.semaphore_wait(barrier, NSEQ - 1 + 3)

    def zcopy(kind, block, way, step):
        to = lax.rem(z + 1, NZ) if way == 0 else lax.rem(z + NZ - 1, NZ)
        ref = (z_t, z_s)[kind].at[block]
        return pltpu.make_async_remote_copy(
            src_ref=ref, dst_ref=ref,
            send_sem=zsend_sem.at[kind, way, step], recv_sem=zrecv_sem.at[kind, way, step],
            device_id=seq_dev(y, to),
        )

    def ring_step(kind, step):
        for way, block in ((0, lax.rem(z + NZ - step, NZ)), (1, lax.rem(z + step, NZ))):
            if step > 0 and not (way == 1 and step == 8):
                zcopy(kind, block, way, step - 1).wait_recv()
            if step < 8 - way:
                cp = zcopy(kind, block, way, step)
                cp.start()
                pending.append(cp)

    def send_to(src, dst, k, to):
        pltpu.make_async_remote_copy(
            src_ref=src.at[to], dst_ref=dst.at[s],
            send_sem=asend_sem.at[k], recv_sem=arecv_sem.at[k],
            device_id={"seq": to},
        ).start()

    def scatter(src, dst, k):
        each_peer(lambda to: send_to(src, dst, k, to))

    order = far + [(d, dy) for m in range(7, 0, -1) for dy in range(NY) for d in (m, NZ - m)] + beside

    def send_mid(lo, hi):
        for dz, dy in order[lo:hi]:
            send_to(msend, mrecv, 0, peer(dz, dy))

    def wait_scatter(ref, sem, k):
        part = ref.at[pl.ds(0, NSEQ - 1)]
        pltpu.make_async_copy(part, part, sem.at[k]).wait()

    def fill_q(zz, carry):
        lane, col = iota((128, QW), 0), iota((128, QW), 1)
        at = lane & 31
        hit = (at < 27) & (lane < 96) & (col == at + 27 * zz)
        eq[zz] = jnp.where(hit, 1.0, 0.0).astype(bf16)
        return carry

    def fill_o(zz, carry):
        lane, col = iota((128, OW), 0), iota((128, OW), 1)
        at = lane
        for g in range(1, 5):
            at = jnp.where(lane >= 24 * g, lane - 24 * g, at)
        hit = (at < 18) & (col == at + 18 * zz + 32 * y)
        eo[zz] = jnp.where(hit, 1.0, 0.0).astype(bf16)
        return carry

    def own_norms(i, carry):
        rows = pl.ds(pl.multiple_of(i * 64, 64), 64)
        f, r = i // 2, pl.ds(pl.multiple_of((i % 2) * 64, 64), 64)
        nm_t[rows, :], rs_t[rows, :] = norm_stats(mid[f, r, :].astype(f32))
        nm_s[rows, :], rs_s[rows, :] = norm_stats(inp[f, r, :].astype(f32))
        return carry

    def live_cot(f):
        cell = iota((128, 1), 0) * 0 + (2 * s + f)
        return jnp.where(cell < frames[0], cot[f].astype(f32), 0.0)

    def whole_of(ref, lo, hi):
        return jnp.concatenate([ref[i, lo:hi] for i in range(NZ)], 1)

    def unpack(whole, table, group, lanes, count):
        lane = iota(whole.shape, 1) & 127
        parts = []
        for g in range(count):
            live = (lane >= lanes * g) & (lane < lanes * (g + 1))
            parts.append(jnp.where(live, whole, jnp.zeros_like(whole)))
        lhs = jnp.concatenate(parts, 0)
        return dot(lhs, table[...].reshape(NZ * 128, -1)).astype(bf16)

    def unpack_q(whole):
        return unpack(whole, eq, 48, 32, 3)

    def unpack_o(whole):
        return unpack(whole, eo, 16, 24, 5)

    jobs_o = [(0, o_t, "y", 0, 48, 32), (1, o_t, "x", 48, 32, 16)]
    jobs_q = [(2, q_t, "y", 0, 112, 64), (3, q_t, "x", 112, 32, 16)]
    jobs_s = [
        (4, o_s, "y", 0, 48, 32), (5, o_s, "x", 48, 32, 16),
        (6, q_s, "y", 0, 112, 64), (7, q_s, "x", 112, 32, 16),
    ]

    def view(job, phase, rel, half, core):
        _, ref, first, r, n, m = job
        lo, size = {"all": (r, n), "a": (r, m), "b": (r + m, n - m)}[half]
        rows = pl.ds(lo, size)
        axis = first if phase == 0 else ("x" if first == "y" else "y")
        if axis == "x":
            return ref.at[y if phase == 0 else slice(None), core, (x + rel) % NX, rows]
        return ref.at[(y + rel) % NY, core, x if phase == 0 else slice(None), rows]

    def hop(job, phase, rel, half, way, slot):
        first = job[2]
        axis = first if phase == 0 else ("x" if first == "y" else "y")
        step = 1 if way == 0 else 3
        dev = x_dev((x + step) % NX) if axis == "x" else seq_dev((y + step) % NY, z)
        ref = view(job, phase, rel, half, c)
        return pltpu.make_async_remote_copy(
            src_ref=ref, dst_ref=ref,
            send_sem=jsend_sem.at[job[0], phase * 4 + slot],
            recv_sem=jrecv_sem.at[job[0], phase * 4 + slot],
            device_id=dev,
        )

    def go(cp):
        cp.start()
        pending.append(cp)

    def first_step(job, phase):
        go(hop(job, phase, 0, "all", 0, 0))
        go(hop(job, phase, 0, "all", 1, 1))

    def pass_on(job, phase):
        hop(job, phase, 3, "all", 0, 0).wait_recv()
        go(hop(job, phase, 3, "a", 0, 2))
        hop(job, phase, 1, "all", 1, 1).wait_recv()
        go(hop(job, phase, 1, "b", 1, 3))

    def last_step(job, phase):
        hop(job, phase, 2, "a", 0, 2).wait_recv()
        hop(job, phase, 2, "b", 1, 3).wait_recv()

    def share(job, rel, core):
        ref = view(job, 1, rel, "all", core)
        return pltpu.make_async_remote_copy(
            src_ref=ref, dst_ref=ref,
            send_sem=jsend_sem.at[job[0], 8 + rel], recv_sem=jrecv_sem.at[job[0], 8 + rel],
            device_id={"dp": x * 2 + other},
        )

    def share_wait(job):
        for rel in range(4):
            share(job, rel, other).wait_recv()

    def out_rows(o_ref, yy):
        return jnp.concatenate([o_ref[yy, d % 2, d // 2] for d in range(HEADS)], 0)

    def qkv_rows(q_ref, yy):
        return jnp.concatenate([q_ref[yy, d % 2, d // 2] for d in range(8)], 0)

    def out_back(gated, o_ref):
        total = None
        for yy in range(NY):
            term = dot(gated[:, 256 * yy:256 * yy + OW], out_rows(o_ref, yy), NT)
            total = term if total is None else total + term
        return total.astype(bf16)

    def open_second(job):
        last_step(job, 0)
        first_step(job, 1)
        go(share(job, 0, c))

    def on_second(job):
        pass_on(job, 1)
        go(share(job, 3, c))
        go(share(job, 1, c))

    def end_second(job):
        last_step(job, 1)
        go(share(job, 2, c))

    def each(f, jobs, *args):
        for job in jobs:
            f(job, *args)

    ring_step(0, 0)
    ring_step(1, 0)
    ri, ci = iota((TOK, TOK), 0), iota((TOK, TOK), 1)
    pm[...] = jnp.where(ci == (ri & 1) * 128 + (ri >> 2) * 2 + ((ri >> 1) & 1), 1.0, 0.0).astype(bf16)
    pr[...] = jnp.where(
        ci == ((ri & 127) >> 1) * 4 + (ri >> 7) * 2 + (ri & 1), 1.0, 0.0
    ).astype(bf16)

    back[...] = jnp.where(
        ci == (ri & 1) * 128 + ((ri & 127) >> 1) * 2 + (ri >> 7), 1.0, 0.0
    ).astype(bf16)
    dqkv[...] = jnp.zeros((TOK, NY * QW), bf16)
    loads[4].wait()
    msend[...] = dot(pm[...], mid[...].reshape(TOK, D)).astype(bf16).reshape(NSEQ, 4, D)

    for step in range(8):
        if step > 0:
            ring_step(0, step)
            ring_step(1, step)
        send_mid(step, step + 1)
        lax.fori_loop(2 * step, 2 * step + 2, fill_o, 0)
        lax.fori_loop(2 * step, 2 * step + 2, fill_q, 0)
        if step == 1:
            for cp in loads[5:]:
                cp.wait()
        if step in (2, 3):
            f = step - 2
            normin[f * 128:(f + 1) * 128, :] = (live_cot(f) * mod[5]).astype(bf16)
        if step > 3:
            lax.fori_loop(step - 4, step - 3, own_norms, 0)
    ring_step(0, 8)
    o_t[y, c, x] = unpack_o(whole_of(z_t, 48, 64))
    each(first_step, jobs_o, 0)
    q_t[y, c, x] = unpack_q(whole_of(z_t, 0, 48))
    each(first_step, jobs_q, 0)
    send_mid(8, 20)
    ring_step(1, 8)
    o_s[y, c, x] = unpack_o(whole_of(z_s, 48, 64))
    q_s[y, c, x] = unpack_q(whole_of(z_s, 0, 48))
    each(pass_on, jobs_o, 0)
    each(open_second, jobs_o)
    send_mid(20, 32)
    each(pass_on, jobs_q, 0)
    send_mid(32, 44)
    each(on_second, jobs_o)
    each(open_second, jobs_q)
    send_mid(44, 63)
    each(end_second, jobs_o)
    each(first_step, jobs_s, 0)

    each(share_wait, jobs_o)
    dout[...] = out_back(normin, o_t)
    for b in range(2):
        part = dot(back[128 * b:128 * b + 128, :], dout[...])
        dsend[b] = part.astype(bf16).reshape(NSEQ, 2, HEADS * HP)
        scatter(dsend.at[b], drecv.at[b], 1 + b)
        drecv[b, s] = dsend[b, s]
        if b == 0:
            each(on_second, jobs_q)
    mrecv[s] = msend[s]
    each(end_second, jobs_q)

    def project(q_ref, lo, n):
        def body(yy, carry):
            lanes = pl.ds(pl.multiple_of(yy * QW, QW), QW)
            qkv[lo:lo + n, lanes] = dot(normin[lo:lo + n, :], qkv_rows(q_ref, yy)).astype(bf16)
            return carry
        lax.fori_loop(0, NY, body, 0)

    def project_back(q_ref, lo, n):
        for at in range(0, D, 384):
            total = None
            for yy in range(NY):
                part = dqkv[lo:lo + n, yy * QW:(yy + 1) * QW]
                term = dot(part, qkv_rows(q_ref, yy)[at:at + 384], NT)
                total = term if total is None else total + term
            acc[lo:lo + n, at:at + 384] = total

    def attend(masked, lo=0, hi=2):
        def body(b, carry):
            rows = pl.ds(pl.multiple_of(b * 128, 128), 128)
            for h in range(HEADS):
                q = qkv[rows, head_at(h):head_at(h) + HDIM]
                k = qkv[rows, head_at(8 + h):head_at(8 + h) + HDIM]
                scores = dot(k, q, NT) * HDIM ** -0.5
                if masked:
                    scores = jnp.where(iota((128, 128), 0) < frames[0], scores, -1e30)
                e = jnp.exp(scores - jnp.max(scores, 0, keepdims=True))
                probs[b * HEADS + h] = e / jnp.sum(e, 0, keepdims=True)
            return carry
        lax.fori_loop(lo, hi, body, 0)

    def attend_back(lo, hi):
        def body(b, carry):
            rows = pl.ds(pl.multiple_of(b * 128, 128), 128)
            for h in range(HEADS):
                q = qkv[rows, head_at(h):head_at(h) + HDIM]
                k = qkv[rows, head_at(8 + h):head_at(8 + h) + HDIM]
                v = qkv[rows, head_at(16 + h):head_at(16 + h) + HDIM]
                up = dout[rows, HP * h:HP * h + HDIM]
                p = probs[b * HEADS + h]
                dv = dot(p.astype(bf16), up)
                dp_ = dot(v, up, NT)
                delta = jnp.sum(p * dp_, 0, keepdims=True)
                ds = (p * (dp_ - delta)).astype(bf16)
                dq = dot(ds, k, TN) * HDIM ** -0.5
                dk = dot(ds, q) * HDIM ** -0.5
                dqkv[rows, head_at(h):head_at(h) + HDIM] = dq.astype(bf16)
                dqkv[rows, head_at(8 + h):head_at(8 + h) + HDIM] = dk.astype(bf16)
                dqkv[rows, head_at(16 + h):head_at(16 + h) + HDIM] = dv.astype(bf16)
            return carry
        lax.fori_loop(lo, hi, body, 0)

    wait_scatter(mrecv, arecv_sem, 0)
    acc[...] = dot(pr[...], mrecv[...].reshape(TOK, D))

    def patch_norm(i, carry):
        rows = pl.ds(pl.multiple_of(i * 64, 64), 64)
        normed, _ = norm_stats(acc[rows, :])
        normin[rows, :] = (normed * (1.0 + mod[4]) + mod[3]).astype(bf16)
        return carry
    lax.fori_loop(0, 4, patch_norm, 0)
    each(pass_on, jobs_s, 0)
    each(open_second, jobs_s)
    each(share_wait, jobs_q)
    for b in range(2):
        project(q_t, 128 * b, 128)
        attend(True, b, b + 1)
        if b == 1:
            each(on_second, jobs_s)
        wait_scatter(drecv.at[b], arecv_sem, 1 + b)
        dout[128 * b:128 * b + 128, :] = drecv[b].reshape(128, HEADS * HP)
        attend_back(b, b + 1)
        project_back(q_t, 128 * b, 128)
        rsend[b] = acc[128 * b:128 * b + 128, :].astype(bf16).reshape(NSEQ, 2, D)
        scatter(rsend.at[b], rrecv.at[b], 3 + b)
        rrecv[b, s] = rsend[b, s]

    each(end_second, jobs_s)

    def frame_norm(i, carry):
        rows = pl.ds(pl.multiple_of(i * 64, 64), 64)
        normin[rows, :] = (nm_s[rows, :] * (1.0 + mod[1]) + mod[0]).astype(bf16)
        return carry
    lax.fori_loop(0, 4, frame_norm, 0)
    each(share_wait, jobs_s)
    project(q_s, 0, TOK)
    attend(False)

    for cp in pending:
        cp.wait_send()
    wait_scatter(msend, asend_sem, 0)
    for b in range(2):
        wait_scatter(dsend.at[b], asend_sem, 1 + b)

    wait_scatter(rrecv.at[0], arecv_sem, 3)
    acc[...] = dot(back[:, 0:128], rrecv[0].reshape(128, D))
    wait_scatter(rrecv.at[1], arecv_sem, 4)
    acc[...] += dot(back[:, 128:256], rrecv[1].reshape(128, D))

    def mid_grad(i, carry):
        rows = pl.ds(pl.multiple_of(i * 64, 64), 64)
        f, r = i // 2, pl.ds(pl.multiple_of((i % 2) * 64, 64), 64)
        cell = iota((64, 1), 0) * 0 + (2 * s + f)
        masked = jnp.where(cell < frames[0], cot[f, r, :].astype(f32), 0.0)
        grad = masked + norm_back(acc[rows, :], nm_t[rows, :], rs_t[rows, :], 1.0 + mod[4])
        dmid[rows, :] = grad
        normin[rows, :] = (grad * mod[2]).astype(bf16)
        return carry
    lax.fori_loop(0, 4, mid_grad, 0)
    dout[...] = out_back(normin, o_s)
    attend_back(0, 2)
    project_back(q_s, 0, TOK)

    def last_grad(i, carry):
        rows = pl.ds(pl.multiple_of(i * 64, 64), 64)
        f, r = i // 2, pl.ds(pl.multiple_of((i % 2) * 64, 64), 64)
        dnorm = acc[rows, :].astype(bf16).astype(f32)
        grad = norm_back(dnorm, nm_s[rows, :], rs_s[rows, :], 1.0 + mod[1])
        result[f, r, :] = (dmid[rows, :] + grad).astype(bf16)
        return carry
    lax.fori_loop(0, 4, last_grad, 0)

    for b in range(2):
        wait_scatter(rsend.at[b], asend_sem, 3 + b)


def per_device(inputs, mid_inputs, cotangent, modulation, frames, qkv_s, out_s, qkv_t, out_t):
    vmem, hbm = pl.BlockSpec(memory_space=pltpu.VMEM), pl.BlockSpec(memory_space=pltpu.HBM)
    dma = pltpu.SemaphoreType.DMA
    out = pl.pallas_call(
        kernel,
        out_shape=jax.ShapeDtypeStruct((2, 128, D), bf16),
        in_specs=[hbm] * 4 + [pl.BlockSpec(memory_space=pltpu.SMEM)] + [hbm] * 4,
        out_specs=vmem,
        scratch_shapes=[
            pltpu.VMEM((2, 128, D), bf16),
            pltpu.VMEM((2, 128, D), bf16),
            pltpu.VMEM((2, 128, D), bf16),
            pltpu.VMEM((6, 1, D), f32),
            pltpu.VMEM((27, 144), bf16),
            pltpu.VMEM((18, 72), bf16),
            pltpu.VMEM((27, 144), bf16),
            pltpu.VMEM((18, 72), bf16),
            dma((8,)),
            pltpu.VMEM((NZ, 64, 128), bf16),
            pltpu.VMEM((NZ, 64, 128), bf16),
            pltpu.VMEM((NZ, 128, QW), bf16),
            pltpu.VMEM((NZ, 128, OW), bf16),
            pltpu.VMEM((NY, 2, NX, 144, QW), bf16),
            pltpu.VMEM((NY, 2, NX, HP, OW), bf16),
            pltpu.VMEM((NY, 2, NX, 144, QW), bf16),
            pltpu.VMEM((NY, 2, NX, HP, OW), bf16),
            pltpu.VMEM((NSEQ, 4, D), bf16),
            pltpu.VMEM((NSEQ, 4, D), bf16),
            pltpu.VMEM((2, NSEQ, 2, HEADS * HP), bf16),
            pltpu.VMEM((2, NSEQ, 2, HEADS * HP), bf16),
            pltpu.VMEM((2, NSEQ, 2, D), bf16),
            pltpu.VMEM((2, NSEQ, 2, D), bf16),
            pltpu.VMEM((TOK, TOK), bf16),
            pltpu.VMEM((TOK, TOK), bf16),
            pltpu.VMEM((TOK, TOK), bf16),
            pltpu.VMEM((TOK, D), bf16),
            pltpu.VMEM((TOK, NY * QW), bf16),
            pltpu.VMEM((TOK, NY * QW), bf16),
            pltpu.VMEM((TOK, HEADS * HP), bf16),
            pltpu.VMEM((2 * HEADS, 128, 128), f32),
            pltpu.VMEM((TOK, D), f32),
            pltpu.VMEM((TOK, D), f32),
            pltpu.VMEM((TOK, 1), f32),
            pltpu.VMEM((TOK, D), f32),
            pltpu.VMEM((TOK, 1), f32),
            pltpu.VMEM((TOK, D), f32),
            dma((2, 2, 8)), dma((2, 2, 8)), dma((8, 12)), dma((8, 12)), dma((5,)), dma((5,)),
        ],
        compiler_params=pltpu.CompilerParams(
            collective_id=0, has_side_effects=True, vmem_limit_bytes=56 * 1024 * 1024
        ),
        name="blocks_grad",
    )(
        inputs[0], mid_inputs[0], cotangent[0], modulation.reshape(6, 1, D), frames,
        qkv_s.T, out_s.T, qkv_t.T, out_t.T,
    )
    return out[None]


def solution(mesh):
    big = P("dp", "seq", None, None)
    weight = P("dp", "seq")
    return jax.shard_map(
        per_device,
        mesh=mesh,
        in_specs=(big, big, big, P("dp", None, None), P("dp")) + (weight,) * 4,
        out_specs=big,
        check_vma=False,
    )
```
